512 devices in a mesh: dp: 64 (over y, z), tensor: 8 (over x, core).
Axes of the slice: x: 4, y: 8, z: 8, core: 2. Of those that a mesh axis runs over, the one named last changes fastest.
Arguments:
- features: bfloat16 [8192, 4096], P('dp', 'tensor'), may hold values from -6 to 6
- gate_pre: bfloat16 [8192, 7168], P('dp', 'tensor'), may hold values from -6 to 6
- up_pre: bfloat16 [8192, 7168], P('dp', 'tensor'), may hold values from -6 to 6
- hidden_grad: bfloat16 [8192, 7168], P('dp', 'tensor'), may hold values from -8 to 8
- lengths: int32 [64], replicated, may hold values from 1 to 128, as said below
- momentum: float32 [4096, 7168], P('dp', 'tensor'), may hold values from -6 to 6
Outputs:
- update: bfloat16 [8, 896, 4096], P('tensor', 'dp')
- new_momentum: float32 [4096, 7168], P('dp', 'tensor')
The draws below stay inside these ranges and needn't reach their ends.
Inputs may be any that keep to these rules, and one draw needn't show every extreme that they name: `lengths`: a whole number of trained tokens at the start of each sequence; some sequence has all 128 trained.
All inputs are finite; a program needn't handle non-finite values.
Results may differ from the reference program's by a relative error of at most 0.0058.
Values may be sent and summed in bfloat16 or wider, within the bound.
No kernel may reach another device: no remote copies, remote signals or barrier semaphores. Data moves between devices by JAX's collectives and lax.ppermute only.
A program may use at most 64 MiB of HBM per device.

```python
import math
import jax
import jax.numpy as jnp
from jax import lax

D = 4096
HID = 7168
SEQ_LEN = 128
BLK = 64
ITERS = 5
TOK_DEV = 128
TOKENS = 8192
SEQS = 64
TGROUPS = 8
HSHARD = 896
N_DP = 64


def draw_hidden_grad(key, part):
    key = jax.random.fold_in(key, 11)
    key_cols, key_rows, key_base = jax.random.split(key, 3)
    column_scale = jnp.exp(jax.random.uniform(key_cols, (1, HID), jnp.float32, math.log(0.25), math.log(4.0)))
    row_scale = jnp.exp(jax.random.uniform(key_rows, (TOKENS, 1), jnp.float32, math.log(0.5), math.log(2.0)))
    rising = 1.0 + 2.0 * jnp.arange(TOKENS, dtype=jnp.float32)[:, None] / TOKENS
    overall = 1.5 / math.sqrt(TOKENS)
    base_value = jnp.clip(jax.random.normal(key_base, (TOKENS, HID), jnp.float32), -4.0, 4.0)
    drawn = base_value * row_scale * rising * column_scale * overall
    return drawn.astype(jnp.bfloat16)


def draw_lengths(key, part):
    key = jax.random.fold_in(key, 5)
    key_draw, key_full = jax.random.split(key, 2)
    drawn = jax.random.randint(key_draw, (SEQS,), 1, SEQ_LEN + 1, dtype=jnp.int32)
    chosen = jax.random.randint(key_full, (), 0, SEQS, dtype=jnp.int32)
    return jnp.where(jnp.arange(SEQS, dtype=jnp.int32) == chosen, SEQ_LEN, drawn).astype(jnp.int32)


def block_scale(stream_key, extent, cuts, least, top_value):
    gain = 1.0
    for axis_at, shards_of in cuts:
        draws = jax.random.uniform(jax.random.fold_in(jax.random.fold_in(stream_key, 6), axis_at), (shards_of,), jnp.float32, least / len(cuts), top_value / len(cuts))
        gain = gain * jnp.repeat(jnp.exp(draws), extent[axis_at] // shards_of).reshape((-1,) + (1,) * (len(extent) - 1 - axis_at))
    return gain


def noise(key, dims, scale, reach, cuts=(), kind=jnp.bfloat16):
    level = block_scale(key, dims, cuts, -0.22, 0.18) if cuts else 1.0
    result = jax.random.normal(key, dims, jnp.float32) * scale * level
    return jnp.minimum(jnp.maximum(result, -reach), reach).astype(kind)


def setup_inputs(seed: int = 0) -> dict:
    arg_keys = jax.random.split(jax.random.key(seed), 7)
    features = noise(arg_keys[0], (TOKENS, D), 1.0, 6.0, ((0, 64), (1, 8)))
    gate_pre = noise(arg_keys[1], (TOKENS, HID), 1.0, 6.0, ((0, 64), (1, 8)))
    up_pre = noise(arg_keys[2], (TOKENS, HID), 1.0, 6.0, ((0, 64), (1, 8)))
    hidden_grad = draw_hidden_grad(jax.random.fold_in(arg_keys[6], 71), 0)
    lengths = draw_lengths(jax.random.fold_in(arg_keys[6], 71), 0)
    momentum = noise(arg_keys[5], (D, HID), 1.0, 6.0, ((0, 64), (1, 8)), jnp.float32)
    return {"features": features, "gate_pre": gate_pre, "up_pre": up_pre, "hidden_grad": hidden_grad, "lengths": lengths, "momentum": momentum}


momentum_decay = 0.95
linear_coeff = 3.4445
cubic_coeff = -4.775
quintic_coeff = 2.0315
norm_epsilon = 1e-07
update_gain = 0.2

def reference(features, gate_pre, up_pre, hidden_grad, lengths, momentum):
    position = jnp.arange(TOKENS, dtype=jnp.int32)
    token_limit = lengths[position // SEQ_LEN]
    trained = position % SEQ_LEN < token_limit
    gate_value = gate_pre.astype(jnp.float32)
    up_value = up_pre.astype(jnp.float32)
    cotangent = hidden_grad.astype(jnp.float32)
    sigmoid_gate = jax.nn.sigmoid(gate_value)
    gate_grad = cotangent * up_value * sigmoid_gate * (1.0 + gate_value * (1.0 - sigmoid_gate))
    gate_grad = jnp.where(trained[:, None], gate_grad, 0.0).astype(jnp.bfloat16)
    highest = lax.Precision.HIGHEST

    def add_group(total, group):
        first_row = (group * TOK_DEV).astype(jnp.int32)
        grad_rows = lax.dynamic_slice_in_dim(gate_grad, first_row, TOK_DEV, 0).astype(jnp.float32)
        input_rows = lax.dynamic_slice_in_dim(features, first_row, TOK_DEV, 0).astype(jnp.float32)
        partial_value = jnp.dot(input_rows.T, grad_rows, precision=highest, preferred_element_type=jnp.float32)
        partial_value = lax.optimization_barrier(partial_value.astype(jnp.bfloat16)).astype(jnp.float32)
        return (total + partial_value, None)
    grad, _ = lax.scan(add_group, jnp.zeros((D, HID), jnp.float32), jnp.arange(N_DP, dtype=jnp.int32))
    new_moment = momentum_decay * momentum + grad
    nesterov = grad + momentum_decay * new_moment
    stacked = nesterov.reshape(D // BLK, BLK, HID)
    block_norm = jnp.sqrt(lax.optimization_barrier(jnp.sum(stacked * stacked, axis=(1, 2))))
    orthogonal = stacked / (block_norm + norm_epsilon)[:, None, None]
    for iteration in range(ITERS):
        gram_matrix = jnp.einsum('kbr,kcr->kbc', orthogonal, orthogonal, precision=highest)
        square = jnp.einsum('kbc,kcd->kbd', gram_matrix, gram_matrix, precision=highest)
        polynomial = cubic_coeff * gram_matrix + quintic_coeff * square
        orthogonal = linear_coeff * orthogonal + jnp.einsum('kbc,kcr->kbr', polynomial, orthogonal, precision=highest)
    scaled = (update_gain * math.sqrt(HID) * orthogonal).reshape(D, HID).astype(jnp.bfloat16)
    update = scaled.T.reshape(TGROUPS, HSHARD, D)
    return (update, new_moment)
```

```python
import functools
import math

import jax
import jax.numpy as jnp
from jax import lax
from jax.experimental import pallas as pl
from jax.experimental.pallas import tpu as pltpu
from jax.sharding import Mesh
from jax.sharding import PartitionSpec as P

HID = 7168
SEQ_LEN = 128
BLK = 64
ITERS = 5
NY = 8
NZ = 8
NT = 8

momentum_decay = 0.95
linear_coeff = 3.4445
cubic_coeff = -4.775
quintic_coeff = 2.0315
norm_epsilon = 1e-07
update_gain = 0.2

HIGHEST = lax.Precision.HIGHEST


def gate_cotangent(gate_pre, up_pre, hidden_grad, trained_tokens):
    position = lax.broadcasted_iota(jnp.int32, gate_pre.shape, 0)
    gate_value = gate_pre.astype(jnp.float32)
    up_value = up_pre.astype(jnp.float32)
    cotangent = hidden_grad.astype(jnp.float32)
    sigmoid_gate = jax.nn.sigmoid(gate_value)
    gate_grad = cotangent * up_value * sigmoid_gate * (1.0 + gate_value * (1.0 - sigmoid_gate))
    return jnp.where(position < trained_tokens, gate_grad, 0.0).astype(jnp.bfloat16)


def partial_kernel(own_ref, *refs):
    feature_refs, grad_ref, out_ref, joined = refs[:NT], refs[NT], refs[NT + 1], refs[NT + 2]
    own = own_ref[0]
    tokens = feature_refs[0].shape[0]
    for shift in range(NT):
        group = lax.rem(own + NT - shift, NT)
        joined[pl.ds(pl.multiple_of(group * tokens, tokens), tokens), :] = feature_refs[shift][...]
    rows = out_ref.shape[0]
    step = 128
    for start in range(0, rows, step):
        product = lax.dot_general(
            joined[:, start : start + step],
            grad_ref[...],
            (((0,), (0,)), ((), ())),
            preferred_element_type=jnp.float32,
        )
        out_ref[start : start + step, :] = product.astype(out_ref.dtype)


def partial_product(own, feature_blocks, grads):
    tokens, rows = feature_blocks[0].shape
    columns = grads.shape[1]
    vmem = pl.BlockSpec(memory_space=pltpu.VMEM)
    return pl.pallas_call(
        partial_kernel,
        out_shape=jax.ShapeDtypeStruct((rows, columns), jnp.bfloat16),
        in_specs=[pl.BlockSpec(memory_space=pltpu.SMEM)] + [vmem] * (NT + 1),
        out_specs=vmem,
        scratch_shapes=[pltpu.VMEM((NT * tokens, rows), jnp.bfloat16)],
        compiler_params=pltpu.CompilerParams(vmem_limit_bytes=32 * 1024 * 1024),
        cost_estimate=pl.CostEstimate(
            flops=2 * NT * tokens * rows * columns, bytes_accessed=6_000_000, transcendentals=0
        ),
        name="partial_product",
    )(jnp.reshape(own, (1,)), *feature_blocks, grads)


def polar_map(gram_total):
    mul = functools.partial(jnp.dot, precision=HIGHEST, preferred_element_type=jnp.float32)
    size = gram_total.shape[0]
    eye = jnp.eye(size, dtype=jnp.float32)
    squares = jnp.sum(gram_total * eye)
    inverse = 1.0 / (jnp.sqrt(squares) + norm_epsilon)
    gram = gram_total * inverse * inverse
    mapping = eye
    for iteration in range(ITERS):
        square = mul(gram, gram)
        poly = linear_coeff * eye + cubic_coeff * gram + quintic_coeff * square
        mapping = poly if iteration == 0 else mul(poly, mapping)
        if iteration < ITERS - 1:
            gram = mul(mul(poly, gram), poly)
    return mapping * (inverse * (update_gain * math.sqrt(HID)))


def per_device(features, gate_pre, up_pre, hidden_grad, lengths, momentum):
    y, z, t = (lax.axis_index(name) for name in ("y", "z", "t"))
    swap = [(a * NT + b, b * NT + a) for a in range(NY) for b in range(NT)]
    own_features = lax.ppermute(features, ("y", "t"), swap)
    feature_blocks = [own_features] + [
        lax.ppermute(own_features, "t", [(i, (i + s) % NT) for i in range(NT)]) for s in range(1, NT)
    ]
    trained_tokens = lax.dynamic_index_in_dim(lengths, y * NZ + z, 0, keepdims=False)
    gate_grad = gate_cotangent(gate_pre, up_pre, hidden_grad, trained_tokens)
    grads = lax.all_gather(gate_grad, "y", axis=0, tiled=True)
    partial_value = partial_product(t, feature_blocks, grads)
    pieces = partial_value.reshape(NZ, BLK, partial_value.shape[1])
    received = lax.all_to_all(pieces, "z", split_axis=0, concat_axis=0, tiled=True)
    grad_block = jnp.sum(received.astype(jnp.float32), axis=0)
    new_moment = momentum_decay * momentum + grad_block
    nesterov = grad_block + momentum_decay * new_moment
    gram_own = lax.dot_general(
        nesterov, nesterov, (((1,), (1,)), ((), ())), precision=HIGHEST, preferred_element_type=jnp.float32
    )
    gram_total = gram_own
    for s in range(1, NT):
        gram_total = gram_total + lax.ppermute(gram_own, "t", [(i, (i + s) % NT) for i in range(NT)])
    mapping = polar_map(gram_total)
    update = lax.dot_general(
        nesterov, mapping, (((0,), (1,)), ((), ())), precision=HIGHEST, preferred_element_type=jnp.float32
    ).astype(jnp.bfloat16)
    unit_count = update.shape[0] // (NY * NZ)
    by_y = update.reshape(NY, NZ * unit_count, BLK)
    by_y = lax.all_to_all(by_y, "y", split_axis=0, concat_axis=0, tiled=True)
    by_z = by_y.reshape(NY, NZ, unit_count, BLK)
    by_z = lax.all_to_all(by_z, "z", split_axis=1, concat_axis=1, tiled=True)
    result = by_z.transpose(2, 0, 1, 3).reshape(1, unit_count, NY * NZ * BLK)
    return result, new_moment


def solution(mesh):
    fine = Mesh(mesh.devices.reshape(NY, NZ, NT), ("y", "z", "t"))
    split = P(("y", "z"), "t")
    return jax.shard_map(
        per_device,
        mesh=fine,
        in_specs=(split, split, split, split, P(), split),
        out_specs=(P("t", ("y", "z"), None), split),
        check_vma=False,
    )
```

```python
import functools
import math

import jax
import jax.numpy as jnp
from jax import lax
from jax.experimental import pallas as pl
from jax.experimental.pallas import tpu as pltpu
from jax.sharding import Mesh
from jax.sharding import PartitionSpec as P

HID = 7168
SEQ_LEN = 128
BLK = 64
ITERS = 5
NY = 8
NZ = 8
NT = 8

momentum_decay = 0.95
linear_coeff = 3.4445
cubic_coeff = -4.775
quintic_coeff = 2.0315
norm_epsilon = 1e-07
update_gain = 0.2

HIGHEST = lax.Precision.HIGHEST


def gate_kernel(place_ref, lengths_ref, gate_ref, up_ref, cotangent_ref, out_ref):
    rows = gate_ref.shape[0]
    position = lax.broadcasted_iota(jnp.int32, gate_ref.shape, 0) + pl.program_id(0) * rows
    gate_value = gate_ref[...].astype(jnp.float32)
    up_value = up_ref[...].astype(jnp.float32)
    cotangent = cotangent_ref[...].astype(jnp.float32)
    sigmoid_gate = jax.nn.sigmoid(gate_value)
    gate_grad = cotangent * up_value * sigmoid_gate * (1.0 + gate_value * (1.0 - sigmoid_gate))
    trained = position < lengths_ref[place_ref[0]]
    out_ref[...] = jnp.where(trained, gate_grad, 0.0).astype(out_ref.dtype)


def gate_cotangent(place, lengths, gate_pre, up_pre, hidden_grad):
    tokens, columns = gate_pre.shape
    rows = tokens // 2
    block = pl.BlockSpec((rows, columns), lambda i: (i, 0))
    smem = pl.BlockSpec(memory_space=pltpu.SMEM)
    return pl.pallas_call(
        gate_kernel,
        grid=(tokens // rows,),
        out_shape=jax.ShapeDtypeStruct((tokens, columns), jnp.bfloat16),
        in_specs=[smem, smem, block, block, block],
        out_specs=block,
        compiler_params=pltpu.CompilerParams(vmem_limit_bytes=16 * 1024 * 1024),
        cost_estimate=pl.CostEstimate(
            flops=12 * tokens * columns, bytes_accessed=8 * tokens * columns, transcendentals=tokens * columns
        ),
        name="gate_cotangent",
    )(jnp.reshape(place, (1,)), lengths, gate_pre, up_pre, hidden_grad)


def partial_kernel(feature_offsets, grad_offsets, y_ref, t_ref, *refs):
    feature_refs, grad_refs = refs[:2], refs[2 : 2 + NY]
    out_ref, features, grads = refs[2 + NY :]
    tokens = grad_refs[0].shape[0]
    y, t = y_ref[0], t_ref[0]

    def place(group):
        return pl.ds(pl.multiple_of(group * tokens, tokens), tokens)

    blocks = [
        (ref, start) for ref in feature_refs for start in range(0, ref.shape[0], tokens)
    ]
    for offset, (ref, start) in zip(feature_offsets, blocks):
        features[place(lax.bitwise_xor(t, offset)), :] = ref[start : start + tokens, :]
    for offset, ref in zip(grad_offsets, grad_refs):
        grads[place(lax.rem(y + (NY + offset), NY)), :] = ref[...]
    rows = out_ref.shape[0]
    step = 128
    for start in range(0, rows, step):
        product = lax.dot_general(
            features[:, start : start + step],
            grads[...],
            (((0,), (0,)), ((), ())),
            preferred_element_type=jnp.float32,
        )
        out_ref[start : start + step, :] = product.astype(out_ref.dtype)


def partial_product(y, t, feature_offsets, grad_offsets, feature_halves, grad_blocks):
    tokens, columns = grad_blocks[0].shape
    rows = feature_halves[0].shape[1]
    vmem = pl.BlockSpec(memory_space=pltpu.VMEM)
    smem = pl.BlockSpec(memory_space=pltpu.SMEM)
    return pl.pallas_call(
        functools.partial(partial_kernel, tuple(feature_offsets), tuple(grad_offsets)),
        out_shape=jax.ShapeDtypeStruct((rows, columns), jnp.bfloat16),
        in_specs=[smem, smem] + [vmem] * (2 + NY),
        out_specs=vmem,
        scratch_shapes=[
            pltpu.VMEM((NY * tokens, rows), jnp.bfloat16),
            pltpu.VMEM((NY * tokens, columns), jnp.bfloat16),
        ],
        compiler_params=pltpu.CompilerParams(vmem_limit_bytes=32 * 1024 * 1024),
        cost_estimate=pl.CostEstimate(
            flops=2 * NY * tokens * rows * columns, bytes_accessed=6_000_000, transcendentals=0
        ),
        name="partial_product",
    )(jnp.reshape(y, (1,)), jnp.reshape(t, (1,)), *feature_halves, *grad_blocks)


def momentum_kernel(parts_ref, momentum_ref, moment_ref, nesterov_ref, grams_ref):
    grad = parts_ref[0].astype(jnp.float32)
    for part in range(1, parts_ref.shape[0]):
        grad = grad + parts_ref[part].astype(jnp.float32)
    new_moment = momentum_decay * momentum_ref[...] + grad
    moment_ref[...] = new_moment
    nesterov = grad + momentum_decay * new_moment
    nesterov_ref[...] = nesterov
    gram = lax.dot_general(
        nesterov, nesterov, (((1,), (1,)), ((), ())), precision=HIGHEST, preferred_element_type=jnp.float32
    )
    half = gram.shape[0] // 2
    packed = jnp.concatenate([gram[:half], gram[half:]], axis=1)
    for part in range(grams_ref.shape[0]):
        grams_ref[part] = packed


def momentum_step(parts, momentum):
    size, columns = momentum.shape
    vmem = pl.BlockSpec(memory_space=pltpu.VMEM)
    return pl.pallas_call(
        momentum_kernel,
        out_shape=(
            jax.ShapeDtypeStruct((size, columns), jnp.float32),
            jax.ShapeDtypeStruct((size, columns), jnp.float32),
            jax.ShapeDtypeStruct((NT, size // 2, 2 * size), jnp.float32),
        ),
        in_specs=[vmem, vmem],
        out_specs=(vmem, vmem, vmem),
        compiler_params=pltpu.CompilerParams(vmem_limit_bytes=16 * 1024 * 1024),
        cost_estimate=pl.CostEstimate(flops=60_000_000, bytes_accessed=1_700_000, transcendentals=0),
        name="momentum_step",
    )(parts, momentum)


def polar_kernel(grams_ref, block_ref, out_ref):
    mul = functools.partial(jnp.dot, precision=HIGHEST, preferred_element_type=jnp.float32)
    packed = grams_ref[0]
    for part in range(1, grams_ref.shape[0]):
        packed = packed + grams_ref[part]
    size = packed.shape[1] // 2
    total = jnp.concatenate([packed[:, :size], packed[:, size:]], axis=0)
    shape = (size, size)
    diagonal = lax.broadcasted_iota(jnp.int32, shape, 0) == lax.broadcasted_iota(jnp.int32, shape, 1)
    eye = jnp.where(diagonal, 1.0, 0.0).astype(jnp.float32)
    squares = jnp.sum(jnp.sum(total * eye, axis=1, keepdims=True), axis=0, keepdims=True)
    inverse = 1.0 / (jnp.sqrt(squares) + norm_epsilon)
    gram = total * inverse * inverse
    mapping = None
    for iteration in range(ITERS):
        square = mul(gram, gram)
        poly = linear_coeff * eye + cubic_coeff * gram + quintic_coeff * square
        mapping = poly if iteration == 0 else mul(poly, mapping)
        if iteration < ITERS - 1:
            gram = mul(mul(poly, gram), poly)
    mapping = mapping * (inverse * (update_gain * math.sqrt(HID)))
    units = out_ref.shape[2]
    rows = mul(mapping, block_ref[...]).astype(out_ref.dtype)
    for part in range(out_ref.shape[0]):
        out_ref[part] = rows[:, part * units : (part + 1) * units]


def polar_update(grams, block):
    size, columns = block.shape
    vmem = pl.BlockSpec(memory_space=pltpu.VMEM)
    return pl.pallas_call(
        polar_kernel,
        out_shape=jax.ShapeDtypeStruct((NY, size, columns // NY), jnp.bfloat16),
        in_specs=[vmem, vmem],
        out_specs=vmem,
        compiler_params=pltpu.CompilerParams(vmem_limit_bytes=16 * 1024 * 1024),
        cost_estimate=pl.CostEstimate(flops=100_000_000, bytes_accessed=600_000, transcendentals=0),
        name="polar_update",
    )(grams, block)


def per_device(features, gate_pre, up_pre, hidden_grad, lengths, momentum):
    y, z, t = (lax.axis_index(name) for name in ("y", "z", "t"))
    swap = [(a * NT + b, b * NT + a) for a in range(NY) for b in range(NT)]
    held = lax.ppermute(features, ("y", "t"), swap)
    gate_grad = gate_cotangent(y * NZ + z, lengths, gate_pre, up_pre, hidden_grad)

    offsets = [0]
    halves = None
    for mask in [m for m in (1, 2, 6) if m < NT]:
        arrived = lax.ppermute(held, "t", [(i, i ^ mask) for i in range(NT)])
        halves = (held, arrived)
        offsets = offsets + [o ^ mask for o in offsets]
        held = jnp.concatenate(halves, axis=0)

    grad_blocks, grad_offsets = [gate_grad], [0]
    up, down = gate_grad, gate_grad
    for step in range(1, NY // 2 + 1):
        up = lax.ppermute(up, "y", [(i, (i + 1) % NY) for i in range(NY)])
        grad_blocks.append(up)
        grad_offsets.append(-step)
        if 2 * step < NY:
            down = lax.ppermute(down, "y", [(i, (i + NY - 1) % NY) for i in range(NY)])
            grad_blocks.append(down)
            grad_offsets.append(step)

    partial_value = partial_product(y, t, offsets, grad_offsets, halves, grad_blocks)
    pieces = partial_value.reshape(NZ, BLK, partial_value.shape[1])
    received = lax.all_to_all(pieces, "z", split_axis=0, concat_axis=0, tiled=True)
    new_moment, nesterov, grams = momentum_step(received, momentum)
    grams = lax.all_to_all(grams, "t", split_axis=0, concat_axis=0, tiled=True)
    by_y = polar_update(grams, nesterov)
    by_y = lax.all_to_all(by_y, "y", split_axis=0, concat_axis=0, tiled=True)
    unit_count = by_y.shape[2] // NZ
    by_z = by_y.reshape(NY, BLK, NZ, unit_count).transpose(2, 3, 0, 1)
    by_z = lax.all_to_all(by_z, "z", split_axis=0, concat_axis=0, tiled=True)
    result = by_z.transpose(1, 2, 0, 3).reshape(1, unit_count, NY * NZ * BLK)
    return result, new_moment


def solution(mesh):
    fine = Mesh(mesh.devices.reshape(NY, NZ, NT), ("y", "z", "t"))
    split = P(("y", "z"), "t")
    return jax.shard_map(
        per_device,
        mesh=fine,
        in_specs=(split, split, split, split, P(), split),
        out_specs=(P("t", ("y", "z"), None), split),
        check_vma=False,
    )
```

```python
import functools
import math

import jax
import jax.numpy as jnp
from jax import lax
from jax.experimental import pallas as pl
from jax.experimental.pallas import tpu as pltpu
from jax.sharding import Mesh
from jax.sharding import PartitionSpec as P

HID = 7168
SEQ_LEN = 128
BLK = 64
ITERS = 5
NY = 8
NZ = 8
NT = 8

momentum_decay = 0.95
linear_coeff = 3.4445
cubic_coeff = -4.775
quintic_coeff = 2.0315
norm_epsilon = 1e-07
update_gain = 0.2

HIGHEST = lax.Precision.HIGHEST
AXES = ("y", "z", "t")


def prepare_kernel(place_ref, lengths_ref, features_in, gate_in, up_in, cotangent_in, turned_ref, grad_ref, *scratch):
    buffers, arrived = scratch[:4], scratch[4]
    sources = (features_in, gate_in, up_in, cotangent_in)
    copies = [
        pltpu.make_async_copy(source, buffer, arrived.at[i])
        for i, (source, buffer) in enumerate(zip(sources, buffers))
    ]
    for copy in copies:
        copy.start()
    copies[0].wait()
    turned_ref[...] = buffers[0][...].T
    for copy in copies[1:]:
        copy.wait()
    gate_value, up_value, cotangent = (buffer[...].astype(jnp.float32) for buffer in buffers[1:])
    sigmoid_gate = jax.nn.sigmoid(gate_value)
    gate_grad = cotangent * up_value * sigmoid_gate * (1.0 + gate_value * (1.0 - sigmoid_gate))
    position = lax.broadcasted_iota(jnp.int32, gate_value.shape, 0)
    trained = position < lengths_ref[place_ref[0]]
    grad_ref[...] = jnp.where(trained, gate_grad, 0.0).astype(grad_ref.dtype)


def prepare(place, lengths, features, gate_pre, up_pre, hidden_grad):
    tokens, columns = gate_pre.shape
    rows = features.shape[1]
    hbm = pl.BlockSpec(memory_space=pltpu.HBM)
    vmem = pl.BlockSpec(memory_space=pltpu.VMEM)
    smem = pl.BlockSpec(memory_space=pltpu.SMEM)
    arrays = (features, gate_pre, up_pre, hidden_grad)
    return pl.pallas_call(
        prepare_kernel,
        out_shape=(
            jax.ShapeDtypeStruct((rows, tokens), jnp.bfloat16),
            jax.ShapeDtypeStruct((tokens, columns), jnp.bfloat16),
        ),
        in_specs=[smem, smem] + [hbm] * 4,
        out_specs=(vmem, vmem),
        scratch_shapes=[pltpu.VMEM(array.shape, array.dtype) for array in arrays]
        + [pltpu.SemaphoreType.DMA((4,))],
        compiler_params=pltpu.CompilerParams(vmem_limit_bytes=60 * 1024 * 1024),
        cost_estimate=pl.CostEstimate(
            flops=12 * tokens * columns, bytes_accessed=8 * tokens * columns, transcendentals=tokens * columns
        ),
        name="prepare",
    )(jnp.reshape(place, (1,)), lengths, *arrays)


def device_number(y, z, t):
    return (y * NZ + z) * NT + t


def ring_pairs(step):
    pairs = []
    for y in range(NY):
        for z in range(NZ):
            for t in range(NT):
                target = (y, (z + step) % NZ, t) if t % 2 else ((y + step) % NY, z, t)
                pairs.append((device_number(y, z, t), device_number(*target)))
    return pairs


def tensor_pairs(masks):
    return [
        (device_number(y, z, t), device_number(y, z, t ^ masks[t % 2]))
        for y in range(NY)
        for z in range(NZ)
        for t in range(NT)
    ]


def cross_groups():
    along_z = [[device_number(y, z, t) for z in range(NZ)] for y in range(NY) for t in range(0, NT, 2)]
    along_y = [[device_number(y, z, t) for y in range(NY)] for z in range(NZ) for t in range(1, NT, 2)]
    return along_z + along_y


def partial_kernel(orders, grad_offsets, y_ref, z_ref, t_ref, *refs):
    feature_refs, grad_refs = refs[:2], refs[2 : 2 + NY]
    out_ref, features, grads = refs[2 + NY :]
    tokens = grad_refs[0].shape[0]
    rows = out_ref.shape[0]
    t = t_ref[0]
    odd = lax.rem(t, 2)
    blocks = [(ref, start) for ref in feature_refs for start in range(0, ref.shape[0], rows)]

    @pl.when(odd == 0)
    def _():
        for offset, (ref, start) in zip(orders[0], blocks):
            group = lax.bitwise_xor(t, offset)
            features[:, pl.ds(pl.multiple_of(group * tokens, tokens), tokens)] = ref[start : start + rows, :]

    @pl.when(odd == 1)
    def _():
        for offset, (ref, start) in zip(orders[1], blocks):
            group = lax.bitwise_xor(t, offset)
            for z in range(NZ):
                features[pl.ds(pl.multiple_of(group * BLK, BLK), BLK), z * tokens : (z + 1) * tokens] = ref[
                    start + z * BLK : start + (z + 1) * BLK, :
                ]

    own = jnp.where(odd == 0, y_ref[0], z_ref[0])
    for offset, ref in zip(grad_offsets, grad_refs):
        group = lax.rem(own + (NY + offset), NY)
        grads[pl.ds(pl.multiple_of(group * tokens, tokens), tokens), :] = ref[...]
    step = 128
    for start in range(0, rows, step):
        product = jnp.dot(
            features[start : start + step, :], grads[...], preferred_element_type=jnp.float32
        )
        out_ref[start : start + step, :] = product.astype(out_ref.dtype)


def partial_product(y, z, t, orders, grad_offsets, feature_halves, grad_blocks):
    tokens, columns = grad_blocks[0].shape
    rows = NZ * BLK
    vmem = pl.BlockSpec(memory_space=pltpu.VMEM)
    smem = pl.BlockSpec(memory_space=pltpu.SMEM)
    return pl.pallas_call(
        functools.partial(partial_kernel, orders, tuple(grad_offsets)),
        out_shape=jax.ShapeDtypeStruct((rows, columns), jnp.bfloat16),
        in_specs=[smem] * 3 + [vmem] * (2 + NY),
        out_specs=vmem,
        scratch_shapes=[
            pltpu.VMEM((rows, NY * tokens), jnp.bfloat16),
            pltpu.VMEM((NY * tokens, columns), jnp.bfloat16),
        ],
        compiler_params=pltpu.CompilerParams(vmem_limit_bytes=32 * 1024 * 1024),
        cost_estimate=pl.CostEstimate(
            flops=2 * NY * tokens * rows * columns, bytes_accessed=6_000_000, transcendentals=0
        ),
        name="partial_product",
    )(*(jnp.reshape(i, (1,)) for i in (y, z, t)), *feature_halves, *grad_blocks)


def momentum_kernel(parts_ref, momentum_ref, moment_ref, nesterov_ref, grams_ref):
    grad = parts_ref[0].astype(jnp.float32)
    for part in range(1, parts_ref.shape[0]):
        grad = grad + parts_ref[part].astype(jnp.float32)
    new_moment = momentum_decay * momentum_ref[...] + grad
    moment_ref[...] = new_moment
    nesterov = grad + momentum_decay * new_moment
    nesterov_ref[...] = nesterov
    gram = lax.dot_general(
        nesterov, nesterov, (((1,), (1,)), ((), ())), precision=HIGHEST, preferred_element_type=jnp.float32
    )
    half = gram.shape[0] // 2
    packed = jnp.concatenate([gram[:half], gram[half:]], axis=1)
    for part in range(grams_ref.shape[0]):
        grams_ref[part] = packed


def momentum_step(parts, momentum):
    size, columns = momentum.shape
    vmem = pl.BlockSpec(memory_space=pltpu.VMEM)
    return pl.pallas_call(
        momentum_kernel,
        out_shape=(
            jax.ShapeDtypeStruct((size, columns), jnp.float32),
            jax.ShapeDtypeStruct((size, columns), jnp.float32),
            jax.ShapeDtypeStruct((NT, size // 2, 2 * size), jnp.float32),
        ),
        in_specs=[vmem, vmem],
        out_specs=(vmem, vmem, vmem),
        compiler_params=pltpu.CompilerParams(vmem_limit_bytes=16 * 1024 * 1024),
        cost_estimate=pl.CostEstimate(flops=60_000_000, bytes_accessed=1_700_000, transcendentals=0),
        name="momentum_step",
    )(parts, momentum)


def polar_kernel(grams_ref, block_ref, out_ref):
    mul = functools.partial(jnp.dot, precision=HIGHEST, preferred_element_type=jnp.float32)
    packed = grams_ref[0]
    for part in range(1, grams_ref.shape[0]):
        packed = packed + grams_ref[part]
    size = packed.shape[1] // 2
    total = jnp.concatenate([packed[:, :size], packed[:, size:]], axis=0)
    shape = (size, size)
    diagonal = lax.broadcasted_iota(jnp.int32, shape, 0) == lax.broadcasted_iota(jnp.int32, shape, 1)
    eye = jnp.where(diagonal, 1.0, 0.0).astype(jnp.float32)
    squares = jnp.sum(jnp.sum(total * eye, axis=1, keepdims=True), axis=0, keepdims=True)
    inverse = 1.0 / (jnp.sqrt(squares) + norm_epsilon)
    gram = total * inverse * inverse
    mapping = None
    for iteration in range(ITERS):
        square = mul(gram, gram)
        poly = linear_coeff * eye + cubic_coeff * gram + quintic_coeff * square
        mapping = poly if iteration == 0 else mul(poly, mapping)
        if iteration < ITERS - 1:
            gram = mul(mul(poly, gram), poly)
    mapping = mapping * (inverse * (update_gain * math.sqrt(HID)))
    units = out_ref.shape[2]
    rows = mul(mapping, block_ref[...]).astype(out_ref.dtype)
    for part in range(out_ref.shape[0]):
        out_ref[part] = rows[:, part * units : (part + 1) * units]


def polar_update(grams, block):
    size, columns = block.shape
    vmem = pl.BlockSpec(memory_space=pltpu.VMEM)
    return pl.pallas_call(
        polar_kernel,
        out_shape=jax.ShapeDtypeStruct((NY, size, columns // NY), jnp.bfloat16),
        in_specs=[vmem, vmem],
        out_specs=vmem,
        compiler_params=pltpu.CompilerParams(vmem_limit_bytes=16 * 1024 * 1024),
        cost_estimate=pl.CostEstimate(flops=100_000_000, bytes_accessed=600_000, transcendentals=0),
        name="polar_update",
    )(grams, block)


def per_device(features, gate_pre, up_pre, hidden_grad, lengths, momentum):
    y, z, t = (lax.axis_index(name) for name in AXES)
    turned, gate_grad = prepare(y * NZ + z, lengths, features, gate_pre, up_pre, hidden_grad)

    swap = [(a * NT + b, b * NT + a) for a in range(NY) for b in range(NT)]
    by_tokens = lax.ppermute(turned, ("y", "t"), swap)
    up, down = (lax.ppermute(gate_grad, AXES, ring_pairs(step)) for step in (1, -1))
    by_blocks = lax.all_to_all(
        turned.reshape(NZ, BLK, turned.shape[1]), "z", split_axis=0, concat_axis=0, tiled=True
    ).reshape(turned.shape)
    even = lax.rem(t, 2) == 0
    kept = jnp.where(even, by_tokens, by_blocks)
    given = jnp.where(even, by_blocks, by_tokens)
    orders, halves = ([0], [0]), None
    for masks in [m for m in ((1, 1), (2, 6), (6, 2)) if max(m) < NT]:
        arrived = lax.ppermute(given if halves is None else kept, AXES, tensor_pairs(masks))
        orders = tuple(order + [o ^ mask for o in order] for order, mask in zip(orders, masks))
        halves = (kept, arrived)
        kept = jnp.concatenate(halves, axis=0)

    grad_blocks, grad_offsets = [gate_grad], [0]
    for step in range(1, NY // 2 + 1):
        if step > 1:
            up = lax.ppermute(up, AXES, ring_pairs(1))
        grad_blocks.append(up)
        grad_offsets.append(-step)
        if 2 * step < NY:
            if step > 1:
                down = lax.ppermute(down, AXES, ring_pairs(-1))
            grad_blocks.append(down)
            grad_offsets.append(step)

    partial_value = partial_product(y, z, t, orders, grad_offsets, halves, grad_blocks)
    pieces = partial_value.reshape(NZ, BLK, partial_value.shape[1])
    received = lax.all_to_all(
        pieces, AXES, split_axis=0, concat_axis=0, axis_index_groups=cross_groups(), tiled=True
    )
    new_moment, nesterov, grams = momentum_step(received, momentum)
    grams = lax.all_to_all(grams, "t", split_axis=0, concat_axis=0, tiled=True)
    by_y = polar_update(grams, nesterov)
    by_y = lax.all_to_all(by_y, "y", split_axis=0, concat_axis=0, tiled=True)
    unit_count = by_y.shape[2] // NZ
    by_z = by_y.reshape(NY, BLK, NZ, unit_count).transpose(2, 3, 0, 1)
    by_z = lax.all_to_all(by_z, "z", split_axis=0, concat_axis=0, tiled=True)
    result = by_z.transpose(1, 2, 0, 3).reshape(1, unit_count, NY * NZ * BLK)
    return result, new_moment


def solution(mesh):
    fine = Mesh(mesh.devices.reshape(NY, NZ, NT), AXES)
    split = P(("y", "z"), "t")
    return jax.shard_map(
        per_device,
        mesh=fine,
        in_specs=(split, split, split, split, P(), split),
        out_specs=(P("t", ("y", "z"), None), split),
        check_vma=False,
    )
```

```python
import functools
import math

import jax
import jax.numpy as jnp
from jax import lax
from jax.experimental import pallas as pl
from jax.experimental.pallas import tpu as pltpu
from jax.sharding import Mesh
from jax.sharding import PartitionSpec as P

HID = 7168
SEQ_LEN = 128
BLK = 64
ITERS = 5
NY = 8
NZ = 8
NT = 8

momentum_decay = 0.95
linear_coeff = 3.4445
cubic_coeff = -4.775
quintic_coeff = 2.0315
norm_epsilon = 1e-07
update_gain = 0.2

HIGHEST = lax.Precision.HIGHEST


def gate_kernel(place_ref, lengths_ref, gate_in, up_in, cotangent_in, grad_ref, *scratch):
    buffers, arrived = scratch[:3], scratch[3]
    sources = (gate_in, up_in, cotangent_in)
    copies = [
        pltpu.make_async_copy(source, buffer, arrived.at[i])
        for i, (source, buffer) in enumerate(zip(sources, buffers))
    ]
    for copy in copies:
        copy.start()
    for copy in copies:
        copy.wait()
    gate_value, up_value, cotangent = (buffer[...].astype(jnp.float32) for buffer in buffers)
    sigmoid_gate = jax.nn.sigmoid(gate_value)
    gate_grad = cotangent * up_value * sigmoid_gate * (1.0 + gate_value * (1.0 - sigmoid_gate))
    position = lax.broadcasted_iota(jnp.int32, gate_value.shape, 0)
    trained = position < lengths_ref[place_ref[0]]
    grad_ref[...] = jnp.where(trained, gate_grad, 0.0).astype(grad_ref.dtype)


def gate_cotangent(place, lengths, gate_pre, up_pre, hidden_grad):
    tokens, columns = gate_pre.shape
    hbm = pl.BlockSpec(memory_space=pltpu.HBM)
    vmem = pl.BlockSpec(memory_space=pltpu.VMEM)
    smem = pl.BlockSpec(memory_space=pltpu.SMEM)
    arrays = (gate_pre, up_pre, hidden_grad)
    return pl.pallas_call(
        gate_kernel,
        out_shape=jax.ShapeDtypeStruct((tokens, columns), jnp.bfloat16),
        in_specs=[smem, smem] + [hbm] * 3,
        out_specs=vmem,
        scratch_shapes=[pltpu.VMEM(array.shape, array.dtype) for array in arrays]
        + [pltpu.SemaphoreType.DMA((3,))],
        compiler_params=pltpu.CompilerParams(vmem_limit_bytes=60 * 1024 * 1024),
        cost_estimate=pl.CostEstimate(
            flops=12 * tokens * columns, bytes_accessed=8 * tokens * columns, transcendentals=tokens * columns
        ),
        name="gate_cotangent",
    )(jnp.reshape(place, (1,)), lengths, *arrays)


def partial_kernel(feature_offsets, grad_offsets, y_ref, t_ref, *refs):
    feature_refs, grad_refs = refs[:2], refs[2 : 2 + NY]
    out_ref, features, grads = refs[2 + NY :]
    tokens = grad_refs[0].shape[0]
    y, t = y_ref[0], t_ref[0]

    def place(group):
        return pl.ds(pl.multiple_of(group * tokens, tokens), tokens)

    blocks = [
        (ref, start) for ref in feature_refs for start in range(0, ref.shape[0], tokens)
    ]
    for offset, (ref, start) in zip(feature_offsets, blocks):
        features[place(lax.bitwise_xor(t, offset)), :] = ref[start : start + tokens, :]
    for offset, ref in zip(grad_offsets, grad_refs):
        grads[place(lax.rem(y + (NY + offset), NY)), :] = ref[...]
    rows = out_ref.shape[0]
    step = 128
    for start in range(0, rows, step):
        product = lax.dot_general(
            features[:, start : start + step],
            grads[...],
            (((0,), (0,)), ((), ())),
            preferred_element_type=jnp.float32,
        )
        out_ref[start : start + step, :] = product.astype(out_ref.dtype)


def partial_product(y, t, feature_offsets, grad_offsets, feature_halves, grad_blocks):
    tokens, columns = grad_blocks[0].shape
    rows = feature_halves[0].shape[1]
    vmem = pl.BlockSpec(memory_space=pltpu.VMEM)
    smem = pl.BlockSpec(memory_space=pltpu.SMEM)
    return pl.pallas_call(
        functools.partial(partial_kernel, tuple(feature_offsets), tuple(grad_offsets)),
        out_shape=jax.ShapeDtypeStruct((rows, columns), jnp.bfloat16),
        in_specs=[smem, smem] + [vmem] * (2 + NY),
        out_specs=vmem,
        scratch_shapes=[
            pltpu.VMEM((NY * tokens, rows), jnp.bfloat16),
            pltpu.VMEM((NY * tokens, columns), jnp.bfloat16),
        ],
        compiler_params=pltpu.CompilerParams(vmem_limit_bytes=32 * 1024 * 1024),
        cost_estimate=pl.CostEstimate(
            flops=2 * NY * tokens * rows * columns, bytes_accessed=6_000_000, transcendentals=0
        ),
        name="partial_product",
    )(jnp.reshape(y, (1,)), jnp.reshape(t, (1,)), *feature_halves, *grad_blocks)


def momentum_kernel(parts_ref, momentum_ref, moment_ref, nesterov_ref, grams_ref):
    grad = parts_ref[0].astype(jnp.float32)
    for part in range(1, parts_ref.shape[0]):
        grad = grad + parts_ref[part].astype(jnp.float32)
    new_moment = momentum_decay * momentum_ref[...] + grad
    moment_ref[...] = new_moment
    nesterov = grad + momentum_decay * new_moment
    nesterov_ref[...] = nesterov
    gram = lax.dot_general(
        nesterov, nesterov, (((1,), (1,)), ((), ())), precision=HIGHEST, preferred_element_type=jnp.float32
    )
    half = gram.shape[0] // 2
    packed = jnp.concatenate([gram[:half], gram[half:]], axis=1)
    for part in range(grams_ref.shape[0]):
        grams_ref[part] = packed


def momentum_step(parts, momentum):
    size, columns = momentum.shape
    vmem = pl.BlockSpec(memory_space=pltpu.VMEM)
    return pl.pallas_call(
        momentum_kernel,
        out_shape=(
            jax.ShapeDtypeStruct((size, columns), jnp.float32),
            jax.ShapeDtypeStruct((size, columns), jnp.float32),
            jax.ShapeDtypeStruct((NT, size // 2, 2 * size), jnp.float32),
        ),
        in_specs=[vmem, vmem],
        out_specs=(vmem, vmem, vmem),
        compiler_params=pltpu.CompilerParams(vmem_limit_bytes=16 * 1024 * 1024),
        cost_estimate=pl.CostEstimate(flops=60_000_000, bytes_accessed=1_700_000, transcendentals=0),
        name="momentum_step",
    )(parts, momentum)


def polar_kernel(grams_ref, block_ref, out_ref):
    mul = functools.partial(jnp.dot, precision=HIGHEST, preferred_element_type=jnp.float32)
    packed = grams_ref[0]
    for part in range(1, grams_ref.shape[0]):
        packed = packed + grams_ref[part]
    size = packed.shape[1] // 2
    total = jnp.concatenate([packed[:, :size], packed[:, size:]], axis=0)
    shape = (size, size)
    diagonal = lax.broadcasted_iota(jnp.int32, shape, 0) == lax.broadcasted_iota(jnp.int32, shape, 1)
    eye = jnp.where(diagonal, 1.0, 0.0).astype(jnp.float32)
    squares = jnp.sum(jnp.sum(total * eye, axis=1, keepdims=True), axis=0, keepdims=True)
    inverse = 1.0 / (jnp.sqrt(squares) + norm_epsilon)
    gram = total * inverse * inverse
    mapping = None
    for iteration in range(ITERS):
        square = mul(gram, gram)
        poly = linear_coeff * eye + cubic_coeff * gram + quintic_coeff * square
        mapping = poly if iteration == 0 else mul(poly, mapping)
        if iteration < ITERS - 1:
            gram = mul(mul(poly, gram), poly)
    mapping = mapping * (inverse * (update_gain * math.sqrt(HID)))
    units = out_ref.shape[2]
    rows = mul(mapping, block_ref[...]).astype(out_ref.dtype)
    for part in range(out_ref.shape[0]):
        out_ref[part] = rows[:, part * units : (part + 1) * units]


def polar_update(grams, block):
    size, columns = block.shape
    vmem = pl.BlockSpec(memory_space=pltpu.VMEM)
    return pl.pallas_call(
        polar_kernel,
        out_shape=jax.ShapeDtypeStruct((NY, size, columns // NY), jnp.bfloat16),
        in_specs=[vmem, vmem],
        out_specs=vmem,
        compiler_params=pltpu.CompilerParams(vmem_limit_bytes=16 * 1024 * 1024),
        cost_estimate=pl.CostEstimate(flops=100_000_000, bytes_accessed=600_000, transcendentals=0),
        name="polar_update",
    )(grams, block)


def per_device(features, gate_pre, up_pre, hidden_grad, lengths, momentum):
    y, z, t = (lax.axis_index(name) for name in ("y", "z", "t"))
    swap = [(a * NT + b, b * NT + a) for a in range(NY) for b in range(NT)]
    held = lax.ppermute(features, ("y", "t"), swap)
    gate_grad = gate_cotangent(y * NZ + z, lengths, gate_pre, up_pre, hidden_grad)
    held, _ = lax.optimization_barrier((held, gate_grad))

    offsets = [0]
    halves = None
    for mask in [m for m in (2, 6, 1) if m < NT]:
        arrived = lax.ppermute(held, "t", [(i, i ^ mask) for i in range(NT)])
        halves = (held, arrived)
        offsets = offsets + [o ^ mask for o in offsets]
        held = jnp.concatenate(halves, axis=0)

    grad_blocks, grad_offsets = [gate_grad], [0]
    up, down = gate_grad, gate_grad
    for step in range(1, NY // 2 + 1):
        up = lax.ppermute(up, "y", [(i, (i + 1) % NY) for i in range(NY)])
        grad_blocks.append(up)
        grad_offsets.append(-step)
        if 2 * step < NY:
            down = lax.ppermute(down, "y", [(i, (i + NY - 1) % NY) for i in range(NY)])
            grad_blocks.append(down)
            grad_offsets.append(step)

    partial_value = partial_product(y, t, offsets, grad_offsets, halves, grad_blocks)
    pieces = partial_value.reshape(NZ, BLK, partial_value.shape[1])
    received = lax.all_to_all(pieces, "z", split_axis=0, concat_axis=0, tiled=True)
    new_moment, nesterov, grams = momentum_step(received, momentum)
    grams = lax.all_to_all(grams, "t", split_axis=0, concat_axis=0, tiled=True)
    by_y = polar_update(grams, nesterov)
    by_y = lax.all_to_all(by_y, "y", split_axis=0, concat_axis=0, tiled=True)
    unit_count = by_y.shape[2] // NZ
    by_z = by_y.reshape(NY, BLK, NZ, unit_count).transpose(2, 3, 0, 1)
    by_z = lax.all_to_all(by_z, "z", split_axis=0, concat_axis=0, tiled=True)
    result = by_z.transpose(1, 2, 0, 3).reshape(1, unit_count, NY * NZ * BLK)
    return result, new_moment


def solution(mesh):
    fine = Mesh(mesh.devices.reshape(NY, NZ, NT), ("y", "z", "t"))
    split = P(("y", "z"), "t")
    return jax.shard_map(
        per_device,
        mesh=fine,
        in_specs=(split, split, split, split, P(), split),
        out_specs=(P("t", ("y", "z"), None), split),
        check_vma=False,
    )
```

```python
import functools
import math

import jax
import jax.numpy as jnp
from jax import lax
from jax.experimental import pallas as pl
from jax.experimental.pallas import tpu as pltpu
from jax.sharding import Mesh
from jax.sharding import PartitionSpec as P

HID = 7168
SEQ_LEN = 128
BLK = 64
ITERS = 5
NY = 8
NZ = 8
NT = 8

momentum_decay = 0.95
linear_coeff = 3.4445
cubic_coeff = -4.775
quintic_coeff = 2.0315
norm_epsilon = 1e-07
update_gain = 0.2

HIGHEST = lax.Precision.HIGHEST


def gate_kernel(place_ref, lengths_ref, gate_in, up_in, cotangent_in, grad_ref, *scratch):
    buffers, arrived = scratch[:3], scratch[3]
    sources = (gate_in, up_in, cotangent_in)
    copies = [
        pltpu.make_async_copy(source, buffer, arrived.at[i])
        for i, (source, buffer) in enumerate(zip(sources, buffers))
    ]
    for copy in copies:
        copy.start()
    for copy in copies:
        copy.wait()
    gate_value, up_value, cotangent = (buffer[...].astype(jnp.float32) for buffer in buffers)
    sigmoid_gate = jax.nn.sigmoid(gate_value)
    gate_grad = cotangent * up_value * sigmoid_gate * (1.0 + gate_value * (1.0 - sigmoid_gate))
    position = lax.broadcasted_iota(jnp.int32, gate_value.shape, 0)
    trained = position < lengths_ref[place_ref[0]]
    grad_ref[...] = jnp.where(trained, gate_grad, 0.0).astype(grad_ref.dtype)


def gate_cotangent(place, lengths, gate_pre, up_pre, hidden_grad):
    tokens, columns = gate_pre.shape
    hbm = pl.BlockSpec(memory_space=pltpu.HBM)
    vmem = pl.BlockSpec(memory_space=pltpu.VMEM)
    smem = pl.BlockSpec(memory_space=pltpu.SMEM)
    arrays = (gate_pre, up_pre, hidden_grad)
    return pl.pallas_call(
        gate_kernel,
        out_shape=jax.ShapeDtypeStruct((tokens, columns), jnp.bfloat16),
        in_specs=[smem, smem] + [hbm] * 3,
        out_specs=vmem,
        scratch_shapes=[pltpu.VMEM(array.shape, array.dtype) for array in arrays]
        + [pltpu.SemaphoreType.DMA((3,))],
        compiler_params=pltpu.CompilerParams(vmem_limit_bytes=60 * 1024 * 1024),
        cost_estimate=pl.CostEstimate(
            flops=12 * tokens * columns, bytes_accessed=8 * tokens * columns, transcendentals=tokens * columns
        ),
        name="gate_cotangent",
    )(jnp.reshape(place, (1,)), lengths, *arrays)


def turn_kernel(value_in, turned_ref, buffer, arrived):
    copy = pltpu.make_async_copy(value_in, buffer, arrived)
    copy.start()
    copy.wait()
    turned_ref[...] = buffer[...].T


def turn(value):
    rows, columns = value.shape
    return pl.pallas_call(
        turn_kernel,
        out_shape=jax.ShapeDtypeStruct((columns, rows), value.dtype),
        in_specs=[pl.BlockSpec(memory_space=pltpu.HBM)],
        out_specs=pl.BlockSpec(memory_space=pltpu.VMEM),
        scratch_shapes=[pltpu.VMEM(value.shape, value.dtype), pltpu.SemaphoreType.DMA],
        compiler_params=pltpu.CompilerParams(vmem_limit_bytes=60 * 1024 * 1024),
        cost_estimate=pl.CostEstimate(flops=rows * columns, bytes_accessed=4 * rows * columns, transcendentals=0),
        name="turn",
    )(value)


def partial_kernel(feature_offsets, grad_offsets, z_ref, t_ref, *refs):
    feature_refs, grad_refs = refs[:2], refs[2 : 2 + NZ]
    out_ref, features, grads = refs[2 + NZ :]
    tokens = grad_refs[0].shape[0]
    rows = out_ref.shape[0]
    z, t = z_ref[0], t_ref[0]
    blocks = [(ref, start) for ref in feature_refs for start in range(0, ref.shape[0], rows)]
    for offset, (ref, start) in zip(feature_offsets, blocks):
        block_rows = pl.ds(pl.multiple_of(lax.bitwise_xor(t, offset) * BLK, BLK), BLK)
        for group in range(NZ):
            features[block_rows, group * tokens : (group + 1) * tokens] = ref[
                start + group * BLK : start + (group + 1) * BLK, :
            ]
    for offset, ref in zip(grad_offsets, grad_refs):
        group = lax.rem(z + (NZ + offset), NZ)
        grads[pl.ds(pl.multiple_of(group * tokens, tokens), tokens), :] = ref[...]
    step = 128
    for start in range(0, rows, step):
        product = jnp.dot(
            features[start : start + step, :], grads[...], preferred_element_type=jnp.float32
        )
        out_ref[start : start + step, :] = product.astype(out_ref.dtype)


def partial_product(z, t, feature_offsets, grad_offsets, feature_halves, grad_blocks):
    tokens, columns = grad_blocks[0].shape
    rows = NY * BLK
    vmem = pl.BlockSpec(memory_space=pltpu.VMEM)
    smem = pl.BlockSpec(memory_space=pltpu.SMEM)
    return pl.pallas_call(
        functools.partial(partial_kernel, tuple(feature_offsets), tuple(grad_offsets)),
        out_shape=jax.ShapeDtypeStruct((rows, columns), jnp.bfloat16),
        in_specs=[smem] * 2 + [vmem] * (2 + NZ),
        out_specs=vmem,
        scratch_shapes=[
            pltpu.VMEM((rows, NZ * tokens), jnp.bfloat16),
            pltpu.VMEM((NZ * tokens, columns), jnp.bfloat16),
        ],
        compiler_params=pltpu.CompilerParams(vmem_limit_bytes=32 * 1024 * 1024),
        cost_estimate=pl.CostEstimate(
            flops=2 * NZ * tokens * rows * columns, bytes_accessed=6_000_000, transcendentals=0
        ),
        name="partial_product",
    )(*(jnp.reshape(i, (1,)) for i in (z, t)), *feature_halves, *grad_blocks)


def momentum_kernel(parts_ref, momentum_ref, moment_ref, nesterov_ref, grams_ref):
    grad = parts_ref[0].astype(jnp.float32)
    for part in range(1, parts_ref.shape[0]):
        grad = grad + parts_ref[part].astype(jnp.float32)
    new_moment = momentum_decay * momentum_ref[...] + grad
    moment_ref[...] = new_moment
    nesterov = grad + momentum_decay * new_moment
    nesterov_ref[...] = nesterov
    gram = lax.dot_general(
        nesterov, nesterov, (((1,), (1,)), ((), ())), precision=HIGHEST, preferred_element_type=jnp.float32
    )
    half = gram.shape[0] // 2
    packed = jnp.concatenate([gram[:half], gram[half:]], axis=1)
    for part in range(grams_ref.shape[0]):
        grams_ref[part] = packed


def momentum_step(parts, momentum):
    size, columns = momentum.shape
    vmem = pl.BlockSpec(memory_space=pltpu.VMEM)
    return pl.pallas_call(
        momentum_kernel,
        out_shape=(
            jax.ShapeDtypeStruct((size, columns), jnp.float32),
            jax.ShapeDtypeStruct((size, columns), jnp.float32),
            jax.ShapeDtypeStruct((NT, size // 2, 2 * size), jnp.float32),
        ),
        in_specs=[vmem, vmem],
        out_specs=(vmem, vmem, vmem),
        compiler_params=pltpu.CompilerParams(vmem_limit_bytes=16 * 1024 * 1024),
        cost_estimate=pl.CostEstimate(flops=60_000_000, bytes_accessed=1_700_000, transcendentals=0),
        name="momentum_step",
    )(parts, momentum)


def polar_kernel(grams_ref, block_ref, out_ref):
    mul = functools.partial(jnp.dot, precision=HIGHEST, preferred_element_type=jnp.float32)
    packed = grams_ref[0]
    for part in range(1, grams_ref.shape[0]):
        packed = packed + grams_ref[part]
    size = packed.shape[1] // 2
    total = jnp.concatenate([packed[:, :size], packed[:, size:]], axis=0)
    shape = (size, size)
    diagonal = lax.broadcasted_iota(jnp.int32, shape, 0) == lax.broadcasted_iota(jnp.int32, shape, 1)
    eye = jnp.where(diagonal, 1.0, 0.0).astype(jnp.float32)
    squares = jnp.sum(jnp.sum(total * eye, axis=1, keepdims=True), axis=0, keepdims=True)
    inverse = 1.0 / (jnp.sqrt(squares) + norm_epsilon)
    gram = total * inverse * inverse
    mapping = None
    for iteration in range(ITERS):
        square = mul(gram, gram)
        poly = linear_coeff * eye + cubic_coeff * gram + quintic_coeff * square
        mapping = poly if iteration == 0 else mul(poly, mapping)
        if iteration < ITERS - 1:
            gram = mul(mul(poly, gram), poly)
    mapping = mapping * (inverse * (update_gain * math.sqrt(HID)))
    units = out_ref.shape[2]
    rows = mul(mapping, block_ref[...]).astype(out_ref.dtype)
    for part in range(out_ref.shape[0]):
        out_ref[part] = rows[:, part * units : (part + 1) * units]


def polar_update(grams, block):
    size, columns = block.shape
    vmem = pl.BlockSpec(memory_space=pltpu.VMEM)
    return pl.pallas_call(
        polar_kernel,
        out_shape=jax.ShapeDtypeStruct((NY, size, columns // NY), jnp.bfloat16),
        in_specs=[vmem, vmem],
        out_specs=vmem,
        compiler_params=pltpu.CompilerParams(vmem_limit_bytes=16 * 1024 * 1024),
        cost_estimate=pl.CostEstimate(flops=100_000_000, bytes_accessed=600_000, transcendentals=0),
        name="polar_update",
    )(grams, block)


def per_device(features, gate_pre, up_pre, hidden_grad, lengths, momentum):
    y, z, t = (lax.axis_index(name) for name in ("y", "z", "t"))

    turned = turn(features)
    held = lax.all_to_all(
        turned.reshape(NZ, BLK, turned.shape[1]), "z", split_axis=0, concat_axis=0, tiled=True
    ).reshape(turned.shape)
    gate_grad = gate_cotangent(y * NZ + z, lengths, gate_pre, up_pre, hidden_grad)
    held, _ = lax.optimization_barrier((held, gate_grad))
    feature_offsets, halves = [0], None
    for mask in [m for m in (2, 6, 1) if m < NT]:
        arrived = lax.ppermute(held, "t", [(i, i ^ mask) for i in range(NT)])
        halves = (held, arrived)
        feature_offsets = feature_offsets + [o ^ mask for o in feature_offsets]
        held = jnp.concatenate(halves, axis=0)

    grad_blocks, grad_offsets = [gate_grad], [0]
    up, down = gate_grad, gate_grad
    for step in range(1, NZ // 2 + 1):
        up = lax.ppermute(up, "z", [(i, (i + 1) % NZ) for i in range(NZ)])
        grad_blocks.append(up)
        grad_offsets.append(-step)
        if 2 * step < NZ:
            down = lax.ppermute(down, "z", [(i, (i + NZ - 1) % NZ) for i in range(NZ)])
            grad_blocks.append(down)
            grad_offsets.append(step)

    partial_value = partial_product(z, t, feature_offsets, grad_offsets, halves, grad_blocks)
    pieces = partial_value.reshape(NY, BLK, partial_value.shape[1])
    received = lax.all_to_all(pieces, "y", split_axis=0, concat_axis=0, tiled=True)
    new_moment, nesterov, grams = momentum_step(received, momentum)
    grams = lax.all_to_all(grams, "t", split_axis=0, concat_axis=0, tiled=True)
    by_y = polar_update(grams, nesterov)
    by_y = lax.all_to_all(by_y, "y", split_axis=0, concat_axis=0, tiled=True)
    unit_count = by_y.shape[2] // NZ
    by_z = by_y.reshape(NY, BLK, NZ, unit_count).transpose(2, 3, 0, 1)
    by_z = lax.all_to_all(by_z, "z", split_axis=0, concat_axis=0, tiled=True)
    result = by_z.transpose(1, 2, 0, 3).reshape(1, unit_count, NY * NZ * BLK)
    return result, new_moment


def solution(mesh):
    fine = Mesh(mesh.devices.reshape(NY, NZ, NT), ("y", "z", "t"))
    split = P(("y", "z"), "t")
    return jax.shard_map(
        per_device,
        mesh=fine,
        in_specs=(split, split, split, split, P(), split),
        out_specs=(P("t", ("y", "z"), None), split),
        check_vma=False,
    )
```

```python
import functools
import math

import jax
import jax.numpy as jnp
from jax import lax
from jax.experimental import pallas as pl
from jax.experimental.pallas import tpu as pltpu
from jax.sharding import Mesh
from jax.sharding import PartitionSpec as P

HID = 7168
SEQ_LEN = 128
BLK = 64
ITERS = 5
NY = 8
NZ = 8
NT = 8

momentum_decay = 0.95
linear_coeff = 3.4445
cubic_coeff = -4.775
quintic_coeff = 2.0315
norm_epsilon = 1e-07
update_gain = 0.2

HIGHEST = lax.Precision.HIGHEST


def gate_kernel(place_ref, lengths_ref, gate_in, up_in, cotangent_in, grad_ref, *scratch):
    buffers, arrived = scratch[:3], scratch[3]
    sources = (gate_in, up_in, cotangent_in)
    copies = [
        pltpu.make_async_copy(source, buffer, arrived.at[i])
        for i, (source, buffer) in enumerate(zip(sources, buffers))
    ]
    for copy in copies:
        copy.start()
    for copy in copies:
        copy.wait()
    gate_value, up_value, cotangent = (buffer[...].astype(jnp.float32) for buffer in buffers)
    sigmoid_gate = jax.nn.sigmoid(gate_value)
    gate_grad = cotangent * up_value * sigmoid_gate * (1.0 + gate_value * (1.0 - sigmoid_gate))
    position = lax.broadcasted_iota(jnp.int32, gate_value.shape, 0)
    trained = position < lengths_ref[place_ref[0]]
    grad_ref[...] = jnp.where(trained, gate_grad, 0.0).astype(grad_ref.dtype)


def gate_cotangent(place, lengths, gate_pre, up_pre, hidden_grad):
    tokens, columns = gate_pre.shape
    hbm = pl.BlockSpec(memory_space=pltpu.HBM)
    vmem = pl.BlockSpec(memory_space=pltpu.VMEM)
    smem = pl.BlockSpec(memory_space=pltpu.SMEM)
    arrays = (gate_pre, up_pre, hidden_grad)
    return pl.pallas_call(
        gate_kernel,
        out_shape=jax.ShapeDtypeStruct((tokens, columns), jnp.bfloat16),
        in_specs=[smem, smem] + [hbm] * 3,
        out_specs=vmem,
        scratch_shapes=[pltpu.VMEM(array.shape, array.dtype) for array in arrays]
        + [pltpu.SemaphoreType.DMA((3,))],
        compiler_params=pltpu.CompilerParams(vmem_limit_bytes=60 * 1024 * 1024),
        cost_estimate=pl.CostEstimate(
            flops=12 * tokens * columns, bytes_accessed=8 * tokens * columns, transcendentals=tokens * columns
        ),
        name="gate_cotangent",
    )(jnp.reshape(place, (1,)), lengths, *arrays)


def partial_kernel(feature_offsets, grad_offsets, y_ref, t_ref, *refs):
    feature_refs, grad_refs = refs[:2], refs[2 : 2 + NY]
    out_ref, features, grads = refs[2 + NY :]
    tokens = grad_refs[0].shape[0]
    y, t = y_ref[0], t_ref[0]

    def place(group):
        return pl.ds(pl.multiple_of(group * tokens, tokens), tokens)

    blocks = [
        (ref, start) for ref in feature_refs for start in range(0, ref.shape[0], tokens)
    ]
    for offset, (ref, start) in zip(feature_offsets, blocks):
        features[place(lax.bitwise_xor(lax.bitwise_xor(t, y), offset)), :] = ref[start : start + tokens, :]
    for offset, ref in zip(grad_offsets, grad_refs):
        grads[place(lax.rem(y + (NY + offset), NY)), :] = ref[...]
    rows = out_ref.shape[0]
    step = 128
    for start in range(0, rows, step):
        product = lax.dot_general(
            features[:, start : start + step],
            grads[...],
            (((0,), (0,)), ((), ())),
            preferred_element_type=jnp.float32,
        )
        out_ref[start : start + step, :] = product.astype(out_ref.dtype)


def partial_product(y, t, feature_offsets, grad_offsets, feature_halves, grad_blocks):
    tokens, columns = grad_blocks[0].shape
    rows = feature_halves[0].shape[1]
    vmem = pl.BlockSpec(memory_space=pltpu.VMEM)
    smem = pl.BlockSpec(memory_space=pltpu.SMEM)
    return pl.pallas_call(
        functools.partial(partial_kernel, tuple(feature_offsets), tuple(grad_offsets)),
        out_shape=jax.ShapeDtypeStruct((rows, columns), jnp.bfloat16),
        in_specs=[smem, smem] + [vmem] * (2 + NY),
        out_specs=vmem,
        scratch_shapes=[
            pltpu.VMEM((NY * tokens, rows), jnp.bfloat16),
            pltpu.VMEM((NY * tokens, columns), jnp.bfloat16),
        ],
        compiler_params=pltpu.CompilerParams(vmem_limit_bytes=32 * 1024 * 1024),
        cost_estimate=pl.CostEstimate(
            flops=2 * NY * tokens * rows * columns, bytes_accessed=6_000_000, transcendentals=0
        ),
        name="partial_product",
    )(jnp.reshape(y, (1,)), jnp.reshape(t, (1,)), *feature_halves, *grad_blocks)


def momentum_kernel(parts_ref, momentum_ref, moment_ref, nesterov_ref, grams_ref):
    grad = parts_ref[0].astype(jnp.float32)
    for part in range(1, parts_ref.shape[0]):
        grad = grad + parts_ref[part].astype(jnp.float32)
    new_moment = momentum_decay * momentum_ref[...] + grad
    moment_ref[...] = new_moment
    nesterov = grad + momentum_decay * new_moment
    nesterov_ref[...] = nesterov
    gram = lax.dot_general(
        nesterov, nesterov, (((1,), (1,)), ((), ())), precision=HIGHEST, preferred_element_type=jnp.float32
    )
    half = gram.shape[0] // 2
    packed = jnp.concatenate([gram[:half], gram[half:]], axis=1)
    for part in range(grams_ref.shape[0]):
        grams_ref[part] = packed


def momentum_step(parts, momentum):
    size, columns = momentum.shape
    vmem = pl.BlockSpec(memory_space=pltpu.VMEM)
    return pl.pallas_call(
        momentum_kernel,
        out_shape=(
            jax.ShapeDtypeStruct((size, columns), jnp.float32),
            jax.ShapeDtypeStruct((size, columns), jnp.float32),
            jax.ShapeDtypeStruct((NT, size // 2, 2 * size), jnp.float32),
        ),
        in_specs=[vmem, vmem],
        out_specs=(vmem, vmem, vmem),
        compiler_params=pltpu.CompilerParams(vmem_limit_bytes=16 * 1024 * 1024),
        cost_estimate=pl.CostEstimate(flops=60_000_000, bytes_accessed=1_700_000, transcendentals=0),
        name="momentum_step",
    )(parts, momentum)


def polar_kernel(grams_ref, block_ref, out_ref):
    mul = functools.partial(jnp.dot, precision=HIGHEST, preferred_element_type=jnp.float32)
    packed = grams_ref[0]
    for part in range(1, grams_ref.shape[0]):
        packed = packed + grams_ref[part]
    size = packed.shape[1] // 2
    total = jnp.concatenate([packed[:, :size], packed[:, size:]], axis=0)
    shape = (size, size)
    diagonal = lax.broadcasted_iota(jnp.int32, shape, 0) == lax.broadcasted_iota(jnp.int32, shape, 1)
    eye = jnp.where(diagonal, 1.0, 0.0).astype(jnp.float32)
    squares = jnp.sum(jnp.sum(total * eye, axis=1, keepdims=True), axis=0, keepdims=True)
    inverse = 1.0 / (jnp.sqrt(squares) + norm_epsilon)
    gram = total * inverse * inverse
    mapping = None
    for iteration in range(ITERS):
        square = mul(gram, gram)
        poly = linear_coeff * eye + cubic_coeff * gram + quintic_coeff * square
        mapping = poly if iteration == 0 else mul(poly, mapping)
        if iteration < ITERS - 1:
            gram = mul(mul(poly, gram), poly)
    mapping = mapping * (inverse * (update_gain * math.sqrt(HID)))
    units = out_ref.shape[2]
    rows = mul(mapping, block_ref[...]).astype(out_ref.dtype)
    for part in range(out_ref.shape[0]):
        out_ref[part] = rows[:, part * units : (part + 1) * units]


def polar_update(grams, block):
    size, columns = block.shape
    vmem = pl.BlockSpec(memory_space=pltpu.VMEM)
    return pl.pallas_call(
        polar_kernel,
        out_shape=jax.ShapeDtypeStruct((NY, size, columns // NY), jnp.bfloat16),
        in_specs=[vmem, vmem],
        out_specs=vmem,
        compiler_params=pltpu.CompilerParams(vmem_limit_bytes=16 * 1024 * 1024),
        cost_estimate=pl.CostEstimate(flops=100_000_000, bytes_accessed=600_000, transcendentals=0),
        name="polar_update",
    )(grams, block)


def per_device(features, gate_pre, up_pre, hidden_grad, lengths, momentum):
    y, z, t = (lax.axis_index(name) for name in ("y", "z", "t"))
    swap = [(a * NT + b, b * NT + (a ^ b)) for a in range(NY) for b in range(NT)]
    held = lax.ppermute(features, ("y", "t"), swap)
    gate_grad = gate_cotangent(y * NZ + z, lengths, gate_pre, up_pre, hidden_grad)
    held, _ = lax.optimization_barrier((held, gate_grad))

    offsets = [0]
    halves = None
    for mask in [m for m in (2, 6, 1) if m < NT]:
        arrived = lax.ppermute(held, "t", [(i, i ^ mask) for i in range(NT)])
        halves = (held, arrived)
        offsets = offsets + [o ^ mask for o in offsets]
        held = jnp.concatenate(halves, axis=0)

    grad_blocks, grad_offsets = [gate_grad], [0]
    up, down = gate_grad, gate_grad
    for step in range(1, NY // 2 + 1):
        up = lax.ppermute(up, "y", [(i, (i + 1) % NY) for i in range(NY)])
        grad_blocks.append(up)
        grad_offsets.append(-step)
        if 2 * step < NY:
            down = lax.ppermute(down, "y", [(i, (i + NY - 1) % NY) for i in range(NY)])
            grad_blocks.append(down)
            grad_offsets.append(step)

    partial_value = partial_product(y, t, offsets, grad_offsets, halves, grad_blocks)
    pieces = partial_value.reshape(NZ, BLK, partial_value.shape[1])
    received = lax.all_to_all(pieces, "z", split_axis=0, concat_axis=0, tiled=True)
    new_moment, nesterov, grams = momentum_step(received, momentum)
    grams = lax.all_to_all(grams, "t", split_axis=0, concat_axis=0, tiled=True)
    by_y = polar_update(grams, nesterov)
    by_y = lax.all_to_all(by_y, "y", split_axis=0, concat_axis=0, tiled=True)
    unit_count = by_y.shape[2] // NZ
    by_z = by_y.reshape(NY, BLK, NZ, unit_count).transpose(2, 3, 0, 1)
    by_z = lax.all_to_all(by_z, "z", split_axis=0, concat_axis=0, tiled=True)
    result = by_z.transpose(1, 2, 0, 3).reshape(1, unit_count, NY * NZ * BLK)
    return result, new_moment


def solution(mesh):
    fine = Mesh(mesh.devices.reshape(NY, NZ, NT), ("y", "z", "t"))
    split = P(("y", "z"), "t")
    return jax.shard_map(
        per_device,
        mesh=fine,
        in_specs=(split, split, split, split, P(), split),
        out_specs=(P("t", ("y", "z"), None), split),
        check_vma=False,
    )
```

```python
import functools
import math

import jax
import jax.numpy as jnp
from jax import lax
from jax.experimental import pallas as pl
from jax.experimental.pallas import tpu as pltpu
from jax.sharding import Mesh
from jax.sharding import PartitionSpec as P

HID = 7168
SEQ_LEN = 128
BLK = 64
ITERS = 5
NY = 8
NZ = 8
NT = 8

momentum_decay = 0.95
linear_coeff = 3.4445
cubic_coeff = -4.775
quintic_coeff = 2.0315
norm_epsilon = 1e-07
update_gain = 0.2

HIGHEST = lax.Precision.HIGHEST
AXES = ("y", "z", "t")


def prepare_kernel(place_ref, lengths_ref, features_in, gate_in, up_in, cotangent_in, turned_ref, grad_ref, *scratch):
    buffers, arrived = scratch[:4], scratch[4]
    sources = (features_in, gate_in, up_in, cotangent_in)
    copies = [
        pltpu.make_async_copy(source, buffer, arrived.at[i])
        for i, (source, buffer) in enumerate(zip(sources, buffers))
    ]
    for copy in copies:
        copy.start()
    copies[0].wait()
    turned_ref[...] = buffers[0][...].T
    for copy in copies[1:]:
        copy.wait()
    gate_value, up_value, cotangent = (buffer[...].astype(jnp.float32) for buffer in buffers[1:])
    sigmoid_gate = jax.nn.sigmoid(gate_value)
    gate_grad = cotangent * up_value * sigmoid_gate * (1.0 + gate_value * (1.0 - sigmoid_gate))
    position = lax.broadcasted_iota(jnp.int32, gate_value.shape, 0)
    trained = position < lengths_ref[place_ref[0]]
    grad_ref[...] = jnp.where(trained, gate_grad, 0.0).astype(grad_ref.dtype)


def prepare(place, lengths, features, gate_pre, up_pre, hidden_grad):
    tokens, columns = gate_pre.shape
    rows = features.shape[1]
    hbm = pl.BlockSpec(memory_space=pltpu.HBM)
    vmem = pl.BlockSpec(memory_space=pltpu.VMEM)
    smem = pl.BlockSpec(memory_space=pltpu.SMEM)
    arrays = (features, gate_pre, up_pre, hidden_grad)
    return pl.pallas_call(
        prepare_kernel,
        out_shape=(
            jax.ShapeDtypeStruct((rows, tokens), jnp.bfloat16),
            jax.ShapeDtypeStruct((tokens, columns), jnp.bfloat16),
        ),
        in_specs=[smem, smem] + [hbm] * 4,
        out_specs=(vmem, vmem),
        scratch_shapes=[pltpu.VMEM(array.shape, array.dtype) for array in arrays]
        + [pltpu.SemaphoreType.DMA((4,))],
        compiler_params=pltpu.CompilerParams(vmem_limit_bytes=60 * 1024 * 1024),
        cost_estimate=pl.CostEstimate(
            flops=12 * tokens * columns, bytes_accessed=8 * tokens * columns, transcendentals=tokens * columns
        ),
        name="prepare",
    )(jnp.reshape(place, (1,)), lengths, *arrays)


def device_number(y, z, t):
    return (y * NZ + z) * NT + t


def line_groups(even_axis):
    groups = []
    for t in range(NT):
        along_y = (t % 2 == 0) == (even_axis == "y")
        for fixed in range(NZ if along_y else NY):
            line = [(i, fixed) if along_y else (fixed, i) for i in range(NY if along_y else NZ)]
            groups.append([device_number(y, z, t) for y, z in line])
    return groups


def tensor_pairs(masks):
    return [
        (device_number(y, z, t), device_number(y, z, t ^ masks[t % 2]))
        for y in range(NY)
        for z in range(NZ)
        for t in range(NT)
    ]


def partial_kernel(orders, t_ref, first_ref, second_ref, grads_ref, out_ref, features):
    rows = out_ref.shape[0]
    tokens = first_ref.shape[1]
    t = t_ref[0]
    blocks = [(ref, start) for ref in (first_ref, second_ref) for start in range(0, ref.shape[0], rows)]

    @pl.when(lax.rem(t, 2) == 0)
    def _():
        for offset, (ref, start) in zip(orders[0], blocks):
            group = lax.bitwise_xor(t, offset)
            features[:, pl.ds(pl.multiple_of(group * tokens, tokens), tokens)] = ref[start : start + rows, :]

    @pl.when(lax.rem(t, 2) == 1)
    def _():
        for offset, (ref, start) in zip(orders[1], blocks):
            block_rows = pl.ds(pl.multiple_of(lax.bitwise_xor(t, offset) * BLK, BLK), BLK)
            for z in range(NZ):
                features[block_rows, z * tokens : (z + 1) * tokens] = ref[
                    start + z * BLK : start + (z + 1) * BLK, :
                ]

    step = 128
    for start in range(0, rows, step):
        product = jnp.dot(
            features[start : start + step, :], grads_ref[...], preferred_element_type=jnp.float32
        )
        out_ref[start : start + step, :] = product.astype(out_ref.dtype)


def partial_product(t, orders, feature_halves, grads):
    tokens, columns = grads.shape
    rows = NZ * BLK
    vmem = pl.BlockSpec(memory_space=pltpu.VMEM)
    return pl.pallas_call(
        functools.partial(partial_kernel, orders),
        out_shape=jax.ShapeDtypeStruct((rows, columns), jnp.bfloat16),
        in_specs=[pl.BlockSpec(memory_space=pltpu.SMEM), vmem, vmem, vmem],
        out_specs=vmem,
        scratch_shapes=[pltpu.VMEM((rows, tokens), jnp.bfloat16)],
        compiler_params=pltpu.CompilerParams(vmem_limit_bytes=32 * 1024 * 1024),
        cost_estimate=pl.CostEstimate(
            flops=2 * tokens * rows * columns, bytes_accessed=6_000_000, transcendentals=0
        ),
        name="partial_product",
    )(jnp.reshape(t, (1,)), *feature_halves, grads)


def momentum_kernel(parts_ref, momentum_ref, moment_ref, nesterov_ref, grams_ref):
    grad = parts_ref[0].astype(jnp.float32)
    for part in range(1, parts_ref.shape[0]):
        grad = grad + parts_ref[part].astype(jnp.float32)
    new_moment = momentum_decay * momentum_ref[...] + grad
    moment_ref[...] = new_moment
    nesterov = grad + momentum_decay * new_moment
    nesterov_ref[...] = nesterov
    gram = lax.dot_general(
        nesterov, nesterov, (((1,), (1,)), ((), ())), precision=HIGHEST, preferred_element_type=jnp.float32
    )
    half = gram.shape[0] // 2
    packed = jnp.concatenate([gram[:half], gram[half:]], axis=1)
    for part in range(grams_ref.shape[0]):
        grams_ref[part] = packed


def momentum_step(parts, momentum):
    size, columns = momentum.shape
    vmem = pl.BlockSpec(memory_space=pltpu.VMEM)
    return pl.pallas_call(
        momentum_kernel,
        out_shape=(
            jax.ShapeDtypeStruct((size, columns), jnp.float32),
            jax.ShapeDtypeStruct((size, columns), jnp.float32),
            jax.ShapeDtypeStruct((NT, size // 2, 2 * size), jnp.float32),
        ),
        in_specs=[vmem, vmem],
        out_specs=(vmem, vmem, vmem),
        compiler_params=pltpu.CompilerParams(vmem_limit_bytes=16 * 1024 * 1024),
        cost_estimate=pl.CostEstimate(flops=60_000_000, bytes_accessed=1_700_000, transcendentals=0),
        name="momentum_step",
    )(parts, momentum)


def polar_kernel(grams_ref, block_ref, out_ref):
    mul = functools.partial(jnp.dot, precision=HIGHEST, preferred_element_type=jnp.float32)
    packed = grams_ref[0]
    for part in range(1, grams_ref.shape[0]):
        packed = packed + grams_ref[part]
    size = packed.shape[1] // 2
    total = jnp.concatenate([packed[:, :size], packed[:, size:]], axis=0)
    shape = (size, size)
    diagonal = lax.broadcasted_iota(jnp.int32, shape, 0) == lax.broadcasted_iota(jnp.int32, shape, 1)
    eye = jnp.where(diagonal, 1.0, 0.0).astype(jnp.float32)
    squares = jnp.sum(jnp.sum(total * eye, axis=1, keepdims=True), axis=0, keepdims=True)
    inverse = 1.0 / (jnp.sqrt(squares) + norm_epsilon)
    gram = total * inverse * inverse
    mapping = None
    for iteration in range(ITERS):
        square = mul(gram, gram)
        poly = linear_coeff * eye + cubic_coeff * gram + quintic_coeff * square
        mapping = poly if iteration == 0 else mul(poly, mapping)
        if iteration < ITERS - 1:
            gram = mul(mul(poly, gram), poly)
    mapping = mapping * (inverse * (update_gain * math.sqrt(HID)))
    units = out_ref.shape[2]
    rows = mul(mapping, block_ref[...]).astype(out_ref.dtype)
    for part in range(out_ref.shape[0]):
        out_ref[part] = rows[:, part * units : (part + 1) * units]


def polar_update(grams, block):
    size, columns = block.shape
    vmem = pl.BlockSpec(memory_space=pltpu.VMEM)
    return pl.pallas_call(
        polar_kernel,
        out_shape=jax.ShapeDtypeStruct((NY, size, columns // NY), jnp.bfloat16),
        in_specs=[vmem, vmem],
        out_specs=vmem,
        compiler_params=pltpu.CompilerParams(vmem_limit_bytes=16 * 1024 * 1024),
        cost_estimate=pl.CostEstimate(flops=100_000_000, bytes_accessed=600_000, transcendentals=0),
        name="polar_update",
    )(grams, block)


def per_device(features, gate_pre, up_pre, hidden_grad, lengths, momentum):
    y, z, t = (lax.axis_index(name) for name in AXES)
    turned, gate_grad = prepare(y * NZ + z, lengths, features, gate_pre, up_pre, hidden_grad)

    swap = [(a * NT + b, b * NT + a) for a in range(NY) for b in range(NT)]
    by_tokens = lax.ppermute(features, ("y", "t"), swap).T
    grads = lax.all_gather(gate_grad, AXES, axis_index_groups=line_groups("y"), axis=0, tiled=True)
    by_blocks = lax.all_to_all(
        turned.reshape(NZ, BLK, turned.shape[1]), "z", split_axis=0, concat_axis=0, tiled=True
    ).reshape(turned.shape)
    even = lax.rem(t, 2) == 0
    kept = jnp.where(even, by_tokens, by_blocks)
    given = jnp.where(even, by_blocks, by_tokens)
    orders, halves = ([0], [0]), None
    for masks in [m for m in ((1, 1), (2, 6), (6, 2)) if max(m) < NT]:
        arrived = lax.ppermute(given if halves is None else kept, AXES, tensor_pairs(masks))
        orders = tuple(order + [o ^ mask for o in order] for order, mask in zip(orders, masks))
        halves = (kept, arrived)
        kept = jnp.concatenate(halves, axis=0)

    partial_value = partial_product(t, orders, halves, grads)
    pieces = partial_value.reshape(NZ, BLK, partial_value.shape[1])
    received = lax.all_to_all(
        pieces, AXES, split_axis=0, concat_axis=0, axis_index_groups=line_groups("z"), tiled=True
    )
    new_moment, nesterov, grams = momentum_step(received, momentum)
    grams = lax.all_to_all(grams, "t", split_axis=0, concat_axis=0, tiled=True)
    by_y = polar_update(grams, nesterov)
    by_y = lax.all_to_all(by_y, "y", split_axis=0, concat_axis=0, tiled=True)
    unit_count = by_y.shape[2] // NZ
    by_z = by_y.reshape(NY, BLK, NZ, unit_count).transpose(2, 3, 0, 1)
    by_z = lax.all_to_all(by_z, "z", split_axis=0, concat_axis=0, tiled=True)
    result = by_z.transpose(1, 2, 0, 3).reshape(1, unit_count, NY * NZ * BLK)
    return result, new_moment


def solution(mesh):
    fine = Mesh(mesh.devices.reshape(NY, NZ, NT), AXES)
    split = P(("y", "z"), "t")
    return jax.shard_map(
        per_device,
        mesh=fine,
        in_specs=(split, split, split, split, P(), split),
        out_specs=(P("t", ("y", "z"), None), split),
        check_vma=False,
    )
```

```python
import functools
import math

import jax
import jax.numpy as jnp
from jax import lax
from jax.experimental import pallas as pl
from jax.experimental.pallas import tpu as pltpu
from jax.sharding import Mesh
from jax.sharding import PartitionSpec as P

HID = 7168
SEQ_LEN = 128
BLK = 64
ITERS = 5
NY = 8
NZ = 8
NT = 8

momentum_decay = 0.95
linear_coeff = 3.4445
cubic_coeff = -4.775
quintic_coeff = 2.0315
norm_epsilon = 1e-07
update_gain = 0.2

HIGHEST = lax.Precision.HIGHEST
AXES = ("y", "z", "t")


def prepare_kernel(place_ref, lengths_ref, features_in, gate_in, up_in, cotangent_in, turned_ref, copies_ref, *scratch):
    buffers, arrived = scratch[:4], scratch[4]
    sources = (features_in, gate_in, up_in, cotangent_in)
    copies = [
        pltpu.make_async_copy(source, buffer, arrived.at[i])
        for i, (source, buffer) in enumerate(zip(sources, buffers))
    ]
    for copy in copies:
        copy.start()
    copies[0].wait()
    turned_ref[...] = buffers[0][...].T
    for copy in copies[1:]:
        copy.wait()
    gate_value, up_value, cotangent = (buffer[...].astype(jnp.float32) for buffer in buffers[1:])
    sigmoid_gate = jax.nn.sigmoid(gate_value)
    gate_grad = cotangent * up_value * sigmoid_gate * (1.0 + gate_value * (1.0 - sigmoid_gate))
    position = lax.broadcasted_iota(jnp.int32, gate_value.shape, 0)
    trained = position < lengths_ref[place_ref[0]]
    gate_grad = jnp.where(trained, gate_grad, 0.0).astype(copies_ref.dtype)
    for part in range(copies_ref.shape[0]):
        copies_ref[part] = gate_grad


def prepare(place, lengths, features, gate_pre, up_pre, hidden_grad):
    tokens, columns = gate_pre.shape
    rows = features.shape[1]
    hbm = pl.BlockSpec(memory_space=pltpu.HBM)
    vmem = pl.BlockSpec(memory_space=pltpu.VMEM)
    smem = pl.BlockSpec(memory_space=pltpu.SMEM)
    arrays = (features, gate_pre, up_pre, hidden_grad)
    return pl.pallas_call(
        prepare_kernel,
        out_shape=(
            jax.ShapeDtypeStruct((rows, tokens), jnp.bfloat16),
            jax.ShapeDtypeStruct((NZ, tokens, columns), jnp.bfloat16),
        ),
        in_specs=[smem, smem] + [hbm] * 4,
        out_specs=(vmem, vmem),
        scratch_shapes=[pltpu.VMEM(array.shape, array.dtype) for array in arrays]
        + [pltpu.SemaphoreType.DMA((4,))],
        compiler_params=pltpu.CompilerParams(vmem_limit_bytes=60 * 1024 * 1024),
        cost_estimate=pl.CostEstimate(
            flops=12 * tokens * columns, bytes_accessed=8 * tokens * columns, transcendentals=tokens * columns
        ),
        name="prepare",
    )(jnp.reshape(place, (1,)), lengths, *arrays)


def turn_kernel(value_ref, turned_ref):
    turned_ref[...] = value_ref[...].T


def turn(value):
    rows, columns = value.shape
    vmem = pl.BlockSpec(memory_space=pltpu.VMEM)
    return pl.pallas_call(
        turn_kernel,
        out_shape=jax.ShapeDtypeStruct((columns, rows), value.dtype),
        in_specs=[vmem],
        out_specs=vmem,
        compiler_params=pltpu.CompilerParams(vmem_limit_bytes=8 * 1024 * 1024),
        cost_estimate=pl.CostEstimate(flops=rows * columns, bytes_accessed=4 * rows * columns, transcendentals=0),
        name="turn",
    )(value)


def device_number(y, z, t):
    return (y * NZ + z) * NT + t


def line_groups(even_axis):
    groups = []
    for t in range(NT):
        along_y = (t % 2 == 0) == (even_axis == "y")
        for fixed in range(NZ if along_y else NY):
            line = [(i, fixed) if along_y else (fixed, i) for i in range(NY if along_y else NZ)]
            groups.append([device_number(y, z, t) for y, z in line])
    return groups


def tensor_pairs(masks):
    return [
        (device_number(y, z, t), device_number(y, z, t ^ masks[t % 2]))
        for y in range(NY)
        for z in range(NZ)
        for t in range(NT)
    ]


def partial_kernel(orders, t_ref, first_ref, second_ref, grads_ref, out_ref, features):
    rows = out_ref.shape[0]
    tokens = first_ref.shape[1]
    t = t_ref[0]
    blocks = [(ref, start) for ref in (first_ref, second_ref) for start in range(0, ref.shape[0], rows)]

    @pl.when(lax.rem(t, 2) == 0)
    def _():
        for offset, (ref, start) in zip(orders[0], blocks):
            group = lax.bitwise_xor(t, offset)
            features[:, pl.ds(pl.multiple_of(group * tokens, tokens), tokens)] = ref[start : start + rows, :]

    @pl.when(lax.rem(t, 2) == 1)
    def _():
        for offset, (ref, start) in zip(orders[1], blocks):
            block_rows = pl.ds(pl.multiple_of(lax.bitwise_xor(t, offset) * BLK, BLK), BLK)
            for z in range(NZ):
                features[block_rows, z * tokens : (z + 1) * tokens] = ref[
                    start + z * BLK : start + (z + 1) * BLK, :
                ]

    step = 128
    for start in range(0, rows, step):
        product = jnp.dot(
            features[start : start + step, :], grads_ref[...], preferred_element_type=jnp.float32
        )
        out_ref[start : start + step, :] = product.astype(out_ref.dtype)


def partial_product(t, orders, feature_halves, grads):
    tokens, columns = grads.shape
    rows = NZ * BLK
    vmem = pl.BlockSpec(memory_space=pltpu.VMEM)
    return pl.pallas_call(
        functools.partial(partial_kernel, orders),
        out_shape=jax.ShapeDtypeStruct((rows, columns), jnp.bfloat16),
        in_specs=[pl.BlockSpec(memory_space=pltpu.SMEM), vmem, vmem, vmem],
        out_specs=vmem,
        scratch_shapes=[pltpu.VMEM((rows, tokens), jnp.bfloat16)],
        compiler_params=pltpu.CompilerParams(vmem_limit_bytes=32 * 1024 * 1024),
        cost_estimate=pl.CostEstimate(
            flops=2 * tokens * rows * columns, bytes_accessed=6_000_000, transcendentals=0
        ),
        name="partial_product",
    )(jnp.reshape(t, (1,)), *feature_halves, grads)


def momentum_kernel(parts_ref, momentum_ref, moment_ref, nesterov_ref, grams_ref):
    grad = parts_ref[0].astype(jnp.float32)
    for part in range(1, parts_ref.shape[0]):
        grad = grad + parts_ref[part].astype(jnp.float32)
    new_moment = momentum_decay * momentum_ref[...] + grad
    moment_ref[...] = new_moment
    nesterov = grad + momentum_decay * new_moment
    nesterov_ref[...] = nesterov
    gram = lax.dot_general(
        nesterov, nesterov, (((1,), (1,)), ((), ())), precision=HIGHEST, preferred_element_type=jnp.float32
    )
    half = gram.shape[0] // 2
    packed = jnp.concatenate([gram[:half], gram[half:]], axis=1)
    for part in range(grams_ref.shape[0]):
        grams_ref[part] = packed


def momentum_step(parts, momentum):
    size, columns = momentum.shape
    vmem = pl.BlockSpec(memory_space=pltpu.VMEM)
    return pl.pallas_call(
        momentum_kernel,
        out_shape=(
            jax.ShapeDtypeStruct((size, columns), jnp.float32),
            jax.ShapeDtypeStruct((size, columns), jnp.float32),
            jax.ShapeDtypeStruct((NT, size // 2, 2 * size), jnp.float32),
        ),
        in_specs=[vmem, vmem],
        out_specs=(vmem, vmem, vmem),
        compiler_params=pltpu.CompilerParams(vmem_limit_bytes=16 * 1024 * 1024),
        cost_estimate=pl.CostEstimate(flops=60_000_000, bytes_accessed=1_700_000, transcendentals=0),
        name="momentum_step",
    )(parts, momentum)


def polar_kernel(grams_ref, block_ref, out_ref):
    mul = functools.partial(jnp.dot, precision=HIGHEST, preferred_element_type=jnp.float32)
    packed = grams_ref[0]
    for part in range(1, grams_ref.shape[0]):
        packed = packed + grams_ref[part]
    size = packed.shape[1] // 2
    total = jnp.concatenate([packed[:, :size], packed[:, size:]], axis=0)
    shape = (size, size)
    diagonal = lax.broadcasted_iota(jnp.int32, shape, 0) == lax.broadcasted_iota(jnp.int32, shape, 1)
    eye = jnp.where(diagonal, 1.0, 0.0).astype(jnp.float32)
    squares = jnp.sum(jnp.sum(total * eye, axis=1, keepdims=True), axis=0, keepdims=True)
    inverse = 1.0 / (jnp.sqrt(squares) + norm_epsilon)
    gram = total * inverse * inverse
    mapping = None
    for iteration in range(ITERS):
        square = mul(gram, gram)
        poly = linear_coeff * eye + cubic_coeff * gram + quintic_coeff * square
        mapping = poly if iteration == 0 else mul(poly, mapping)
        if iteration < ITERS - 1:
            gram = mul(mul(poly, gram), poly)
    mapping = mapping * (inverse * (update_gain * math.sqrt(HID)))
    units = out_ref.shape[2]
    rows = mul(mapping, block_ref[...]).astype(out_ref.dtype)
    for part in range(out_ref.shape[0]):
        out_ref[part] = rows[:, part * units : (part + 1) * units]


def polar_update(grams, block):
    size, columns = block.shape
    vmem = pl.BlockSpec(memory_space=pltpu.VMEM)
    return pl.pallas_call(
        polar_kernel,
        out_shape=jax.ShapeDtypeStruct((NY, size, columns // NY), jnp.bfloat16),
        in_specs=[vmem, vmem],
        out_specs=vmem,
        compiler_params=pltpu.CompilerParams(vmem_limit_bytes=16 * 1024 * 1024),
        cost_estimate=pl.CostEstimate(flops=100_000_000, bytes_accessed=600_000, transcendentals=0),
        name="polar_update",
    )(grams, block)


def per_device(features, gate_pre, up_pre, hidden_grad, lengths, momentum):
    y, z, t = (lax.axis_index(name) for name in AXES)
    swap = [(a * NT + b, b * NT + a) for a in range(NY) for b in range(NT)]
    swapped = lax.ppermute(features, ("y", "t"), swap)
    turned, copies = prepare(y * NZ + z, lengths, features, gate_pre, up_pre, hidden_grad)

    by_blocks = lax.all_to_all(
        turned.reshape(NZ, BLK, turned.shape[1]), "z", split_axis=0, concat_axis=0, tiled=True
    ).reshape(turned.shape)
    copies, swapped, by_blocks = lax.optimization_barrier((copies, swapped, by_blocks))
    grads = lax.all_to_all(
        copies, AXES, split_axis=0, concat_axis=0, axis_index_groups=line_groups("y"), tiled=True
    ).reshape(-1, copies.shape[2])
    by_tokens = turn(swapped)
    even = lax.rem(t, 2) == 0
    kept = jnp.where(even, by_tokens, by_blocks)
    given = jnp.where(even, by_blocks, by_tokens)
    orders, halves = ([0], [0]), None
    for masks in [m for m in ((1, 1), (2, 6), (6, 2)) if max(m) < NT]:
        arrived = lax.ppermute(given if halves is None else kept, AXES, tensor_pairs(masks))
        orders = tuple(order + [o ^ mask for o in order] for order, mask in zip(orders, masks))
        halves = (kept, arrived)
        kept = jnp.concatenate(halves, axis=0)

    partial_value = partial_product(t, orders, halves, grads)
    pieces = partial_value.reshape(NZ, BLK, partial_value.shape[1])
    received = lax.all_to_all(
        pieces, AXES, split_axis=0, concat_axis=0, axis_index_groups=line_groups("z"), tiled=True
    )
    new_moment, nesterov, grams = momentum_step(received, momentum)
    grams = lax.all_to_all(grams, "t", split_axis=0, concat_axis=0, tiled=True)
    by_y = polar_update(grams, nesterov)
    by_y = lax.all_to_all(by_y, "y", split_axis=0, concat_axis=0, tiled=True)
    unit_count = by_y.shape[2] // NZ
    by_z = by_y.reshape(NY, BLK, NZ, unit_count).transpose(2, 3, 0, 1)
    by_z = lax.all_to_all(by_z, "z", split_axis=0, concat_axis=0, tiled=True)
    result = by_z.transpose(1, 2, 0, 3).reshape(1, unit_count, NY * NZ * BLK)
    return result, new_moment


def solution(mesh):
    fine = Mesh(mesh.devices.reshape(NY, NZ, NT), AXES)
    split = P(("y", "z"), "t")
    return jax.shard_map(
        per_device,
        mesh=fine,
        in_specs=(split, split, split, split, P(), split),
        out_specs=(P("t", ("y", "z"), None), split),
        check_vma=False,
    )
```

```python
import functools
import math

import jax
import jax.numpy as jnp
from jax import lax
from jax.experimental import pallas as pl
from jax.experimental.pallas import tpu as pltpu
from jax.sharding import Mesh
from jax.sharding import PartitionSpec as P

HID = 7168
SEQ_LEN = 128
BLK = 64
ITERS = 5
NY = 8
NZ = 8
NT = 8

momentum_decay = 0.95
linear_coeff = 3.4445
cubic_coeff = -4.775
quintic_coeff = 2.0315
norm_epsilon = 1e-07
update_gain = 0.2

HIGHEST = lax.Precision.HIGHEST
AXES = ("y", "z", "t")


def gate_kernel(place_ref, lengths_ref, gate_in, up_in, cotangent_in, copies_ref, *scratch):
    buffers, arrived = scratch[:3], scratch[3]
    sources = (gate_in, up_in, cotangent_in)
    copies = [
        pltpu.make_async_copy(source, buffer, arrived.at[i])
        for i, (source, buffer) in enumerate(zip(sources, buffers))
    ]
    for copy in copies:
        copy.start()
    for copy in copies:
        copy.wait()
    gate_value, up_value, cotangent = (buffer[...].astype(jnp.float32) for buffer in buffers)
    sigmoid_gate = jax.nn.sigmoid(gate_value)
    gate_grad = cotangent * up_value * sigmoid_gate * (1.0 + gate_value * (1.0 - sigmoid_gate))
    position = lax.broadcasted_iota(jnp.int32, gate_value.shape, 0)
    trained = position < lengths_ref[place_ref[0]]
    gate_grad = jnp.where(trained, gate_grad, 0.0).astype(copies_ref.dtype)
    for part in range(copies_ref.shape[0]):
        copies_ref[part] = gate_grad


def gate_cotangent(place, lengths, gate_pre, up_pre, hidden_grad):
    tokens, columns = gate_pre.shape
    hbm = pl.BlockSpec(memory_space=pltpu.HBM)
    vmem = pl.BlockSpec(memory_space=pltpu.VMEM)
    smem = pl.BlockSpec(memory_space=pltpu.SMEM)
    arrays = (gate_pre, up_pre, hidden_grad)
    return pl.pallas_call(
        gate_kernel,
        out_shape=jax.ShapeDtypeStruct((NZ, tokens, columns), jnp.bfloat16),
        in_specs=[smem, smem] + [hbm] * 3,
        out_specs=vmem,
        scratch_shapes=[pltpu.VMEM(array.shape, array.dtype) for array in arrays]
        + [pltpu.SemaphoreType.DMA((3,))],
        compiler_params=pltpu.CompilerParams(vmem_limit_bytes=60 * 1024 * 1024),
        cost_estimate=pl.CostEstimate(
            flops=64 * tokens * columns, bytes_accessed=400 * tokens * columns, transcendentals=tokens * columns
        ),
        name="gate_cotangent",
    )(jnp.reshape(place, (1,)), lengths, *arrays)


def turn_first_kernel(value_in, turned_ref, buffer, arrived):
    copy = pltpu.make_async_copy(value_in, buffer, arrived)
    copy.start()
    copy.wait()
    turned_ref[...] = buffer[...].T


def turn_first(value):
    rows, columns = value.shape
    return pl.pallas_call(
        turn_first_kernel,
        out_shape=jax.ShapeDtypeStruct((columns, rows), value.dtype),
        in_specs=[pl.BlockSpec(memory_space=pltpu.HBM)],
        out_specs=pl.BlockSpec(memory_space=pltpu.VMEM),
        scratch_shapes=[pltpu.VMEM(value.shape, value.dtype), pltpu.SemaphoreType.DMA],
        compiler_params=pltpu.CompilerParams(vmem_limit_bytes=60 * 1024 * 1024),
        cost_estimate=pl.CostEstimate(flops=rows * columns, bytes_accessed=4 * rows * columns, transcendentals=0),
        name="turn_first",
    )(value)


def turn_kernel(value_ref, turned_ref):
    turned_ref[...] = value_ref[...].T


def turn(value):
    rows, columns = value.shape
    vmem = pl.BlockSpec(memory_space=pltpu.VMEM)
    return pl.pallas_call(
        turn_kernel,
        out_shape=jax.ShapeDtypeStruct((columns, rows), value.dtype),
        in_specs=[vmem],
        out_specs=vmem,
        compiler_params=pltpu.CompilerParams(vmem_limit_bytes=8 * 1024 * 1024),
        cost_estimate=pl.CostEstimate(flops=rows * columns, bytes_accessed=4 * rows * columns, transcendentals=0),
        name="turn",
    )(value)


def device_number(y, z, t):
    return (y * NZ + z) * NT + t


def line_groups(even_axis):
    groups = []
    for t in range(NT):
        along_y = (t % 2 == 0) == (even_axis == "y")
        for fixed in range(NZ if along_y else NY):
            line = [(i, fixed) if along_y else (fixed, i) for i in range(NY if along_y else NZ)]
            groups.append([device_number(y, z, t) for y, z in line])
    return groups


def tensor_pairs(masks):
    return [
        (device_number(y, z, t), device_number(y, z, t ^ masks[t % 2]))
        for y in range(NY)
        for z in range(NZ)
        for t in range(NT)
    ]


def partial_kernel(orders, t_ref, first_ref, second_ref, grads_ref, out_ref, features):
    rows = out_ref.shape[0]
    tokens = first_ref.shape[1]
    t = t_ref[0]
    blocks = [(ref, start) for ref in (first_ref, second_ref) for start in range(0, ref.shape[0], rows)]

    @pl.when(lax.rem(t, 2) == 0)
    def _():
        for offset, (ref, start) in zip(orders[0], blocks):
            group = lax.bitwise_xor(t, offset)
            features[:, pl.ds(pl.multiple_of(group * tokens, tokens), tokens)] = ref[start : start + rows, :]

    @pl.when(lax.rem(t, 2) == 1)
    def _():
        for offset, (ref, start) in zip(orders[1], blocks):
            block_rows = pl.ds(pl.multiple_of(lax.bitwise_xor(t, offset) * BLK, BLK), BLK)
            for z in range(NZ):
                features[block_rows, z * tokens : (z + 1) * tokens] = ref[
                    start + z * BLK : start + (z + 1) * BLK, :
                ]

    step = 128
    for start in range(0, rows, step):
        product = jnp.dot(
            features[start : start + step, :], grads_ref[...], preferred_element_type=jnp.float32
        )
        out_ref[start : start + step, :] = product.astype(out_ref.dtype)


def partial_product(t, orders, feature_halves, grads):
    tokens, columns = grads.shape
    rows = NZ * BLK
    vmem = pl.BlockSpec(memory_space=pltpu.VMEM)
    return pl.pallas_call(
        functools.partial(partial_kernel, orders),
        out_shape=jax.ShapeDtypeStruct((rows, columns), jnp.bfloat16),
        in_specs=[pl.BlockSpec(memory_space=pltpu.SMEM), vmem, vmem, vmem],
        out_specs=vmem,
        scratch_shapes=[pltpu.VMEM((rows, tokens), jnp.bfloat16)],
        compiler_params=pltpu.CompilerParams(vmem_limit_bytes=32 * 1024 * 1024),
        cost_estimate=pl.CostEstimate(
            flops=2 * tokens * rows * columns, bytes_accessed=6_000_000, transcendentals=0
        ),
        name="partial_product",
    )(jnp.reshape(t, (1,)), *feature_halves, grads)


def momentum_kernel(parts_ref, momentum_ref, moment_ref, nesterov_ref, grams_ref):
    grad = parts_ref[0].astype(jnp.float32)
    for part in range(1, parts_ref.shape[0]):
        grad = grad + parts_ref[part].astype(jnp.float32)
    new_moment = momentum_decay * momentum_ref[...] + grad
    moment_ref[...] = new_moment
    nesterov = grad + momentum_decay * new_moment
    nesterov_ref[...] = nesterov
    gram = lax.dot_general(
        nesterov, nesterov, (((1,), (1,)), ((), ())), precision=HIGHEST, preferred_element_type=jnp.float32
    )
    half = gram.shape[0] // 2
    packed = jnp.concatenate([gram[:half], gram[half:]], axis=1)
    for part in range(grams_ref.shape[0]):
        grams_ref[part] = packed


def momentum_step(parts, momentum):
    size, columns = momentum.shape
    vmem = pl.BlockSpec(memory_space=pltpu.VMEM)
    return pl.pallas_call(
        momentum_kernel,
        out_shape=(
            jax.ShapeDtypeStruct((size, columns), jnp.float32),
            jax.ShapeDtypeStruct((size, columns), jnp.float32),
            jax.ShapeDtypeStruct((NT, size // 2, 2 * size), jnp.float32),
        ),
        in_specs=[vmem, vmem],
        out_specs=(vmem, vmem, vmem),
        compiler_params=pltpu.CompilerParams(vmem_limit_bytes=16 * 1024 * 1024),
        cost_estimate=pl.CostEstimate(flops=60_000_000, bytes_accessed=1_700_000, transcendentals=0),
        name="momentum_step",
    )(parts, momentum)


def polar_kernel(grams_ref, block_ref, out_ref):
    mul = functools.partial(jnp.dot, precision=HIGHEST, preferred_element_type=jnp.float32)
    packed = grams_ref[0]
    for part in range(1, grams_ref.shape[0]):
        packed = packed + grams_ref[part]
    size = packed.shape[1] // 2
    total = jnp.concatenate([packed[:, :size], packed[:, size:]], axis=0)
    shape = (size, size)
    diagonal = lax.broadcasted_iota(jnp.int32, shape, 0) == lax.broadcasted_iota(jnp.int32, shape, 1)
    eye = jnp.where(diagonal, 1.0, 0.0).astype(jnp.float32)
    squares = jnp.sum(jnp.sum(total * eye, axis=1, keepdims=True), axis=0, keepdims=True)
    inverse = 1.0 / (jnp.sqrt(squares) + norm_epsilon)
    gram = total * inverse * inverse
    mapping = None
    for iteration in range(ITERS):
        square = mul(gram, gram)
        poly = linear_coeff * eye + cubic_coeff * gram + quintic_coeff * square
        mapping = poly if iteration == 0 else mul(poly, mapping)
        if iteration < ITERS - 1:
            gram = mul(mul(poly, gram), poly)
    mapping = mapping * (inverse * (update_gain * math.sqrt(HID)))
    units = out_ref.shape[2]
    rows = mul(mapping, block_ref[...]).astype(out_ref.dtype)
    for part in range(out_ref.shape[0]):
        out_ref[part] = rows[:, part * units : (part + 1) * units]


def polar_update(grams, block):
    size, columns = block.shape
    vmem = pl.BlockSpec(memory_space=pltpu.VMEM)
    return pl.pallas_call(
        polar_kernel,
        out_shape=jax.ShapeDtypeStruct((NY, size, columns // NY), jnp.bfloat16),
        in_specs=[vmem, vmem],
        out_specs=vmem,
        compiler_params=pltpu.CompilerParams(vmem_limit_bytes=16 * 1024 * 1024),
        cost_estimate=pl.CostEstimate(flops=100_000_000, bytes_accessed=600_000, transcendentals=0),
        name="polar_update",
    )(grams, block)


def per_device(features, gate_pre, up_pre, hidden_grad, lengths, momentum):
    y, z, t = (lax.axis_index(name) for name in AXES)
    swap = [(a * NT + b, b * NT + a) for a in range(NY) for b in range(NT)]
    swapped = lax.ppermute(features, ("y", "t"), swap)
    turned = turn_first(features)
    copies = gate_cotangent(y * NZ + z, lengths, gate_pre, up_pre, hidden_grad)

    by_blocks = lax.all_to_all(
        turned.reshape(NZ, BLK, turned.shape[1]), "z", split_axis=0, concat_axis=0, tiled=True
    ).reshape(turned.shape)
    copies, swapped, by_blocks = lax.optimization_barrier((copies, swapped, by_blocks))
    grads = lax.all_to_all(
        copies, AXES, split_axis=0, concat_axis=0, axis_index_groups=line_groups("y"), tiled=True
    ).reshape(-1, copies.shape[2])
    by_tokens = turn(swapped)
    even = lax.rem(t, 2) == 0
    kept = jnp.where(even, by_tokens, by_blocks)
    given = jnp.where(even, by_blocks, by_tokens)
    orders, halves = ([0], [0]), None
    for masks in [m for m in ((1, 1), (2, 6), (6, 2)) if max(m) < NT]:
        arrived = lax.ppermute(given if halves is None else kept, AXES, tensor_pairs(masks))
        orders = tuple(order + [o ^ mask for o in order] for order, mask in zip(orders, masks))
        halves = (kept, arrived)
        kept = jnp.concatenate(halves, axis=0)

    partial_value = partial_product(t, orders, halves, grads)
    pieces = partial_value.reshape(NZ, BLK, partial_value.shape[1])
    received = lax.all_to_all(
        pieces, AXES, split_axis=0, concat_axis=0, axis_index_groups=line_groups("z"), tiled=True
    )
    new_moment, nesterov, grams = momentum_step(received, momentum)
    grams = lax.all_to_all(grams, "t", split_axis=0, concat_axis=0, tiled=True)
    by_y = polar_update(grams, nesterov)
    by_y = lax.all_to_all(by_y, "y", split_axis=0, concat_axis=0, tiled=True)
    unit_count = by_y.shape[2] // NZ
    by_z = by_y.reshape(NY, BLK, NZ, unit_count).transpose(2, 3, 0, 1)
    by_z = lax.all_to_all(by_z, "z", split_axis=0, concat_axis=0, tiled=True)
    result = by_z.transpose(1, 2, 0, 3).reshape(1, unit_count, NY * NZ * BLK)
    return result, new_moment


def solution(mesh):
    fine = Mesh(mesh.devices.reshape(NY, NZ, NT), AXES)
    split = P(("y", "z"), "t")
    return jax.shard_map(
        per_device,
        mesh=fine,
        in_specs=(split, split, split, split, P(), split),
        out_specs=(P("t", ("y", "z"), None), split),
        check_vma=False,
    )
```

```python
import functools
import math

import jax
import jax.numpy as jnp
from jax import lax
from jax.experimental import pallas as pl
from jax.experimental.pallas import tpu as pltpu
from jax.sharding import Mesh
from jax.sharding import PartitionSpec as P

HID = 7168
SEQ_LEN = 128
BLK = 64
ITERS = 5
NY = 8
NZ = 8
NT = 8

momentum_decay = 0.95
linear_coeff = 3.4445
cubic_coeff = -4.775
quintic_coeff = 2.0315
norm_epsilon = 1e-07
update_gain = 0.2

HIGHEST = lax.Precision.HIGHEST
AXES = ("y", "z", "t")


def gate_kernel(place_ref, lengths_ref, gate_in, up_in, cotangent_in, copies_ref, *scratch):
    buffers, arrived = scratch[:3], scratch[3]
    sources = (gate_in, up_in, cotangent_in)
    copies = [
        pltpu.make_async_copy(source, buffer, arrived.at[i])
        for i, (source, buffer) in enumerate(zip(sources, buffers))
    ]
    for copy in copies:
        copy.start()
    for copy in copies:
        copy.wait()
    gate_value, up_value, cotangent = (buffer[...].astype(jnp.float32) for buffer in buffers)
    sigmoid_gate = jax.nn.sigmoid(gate_value)
    gate_grad = cotangent * up_value * sigmoid_gate * (1.0 + gate_value * (1.0 - sigmoid_gate))
    position = lax.broadcasted_iota(jnp.int32, gate_value.shape, 0)
    trained = position < lengths_ref[place_ref[0]]
    gate_grad = jnp.where(trained, gate_grad, 0.0).astype(copies_ref.dtype)
    for part in range(copies_ref.shape[0]):
        copies_ref[part] = gate_grad


def gate_cotangent(place, lengths, gate_pre, up_pre, hidden_grad):
    tokens, columns = gate_pre.shape
    hbm = pl.BlockSpec(memory_space=pltpu.HBM)
    vmem = pl.BlockSpec(memory_space=pltpu.VMEM)
    smem = pl.BlockSpec(memory_space=pltpu.SMEM)
    arrays = (gate_pre, up_pre, hidden_grad)
    return pl.pallas_call(
        gate_kernel,
        out_shape=jax.ShapeDtypeStruct((NZ, tokens, columns), jnp.bfloat16),
        in_specs=[smem, smem] + [hbm] * 3,
        out_specs=vmem,
        scratch_shapes=[pltpu.VMEM(array.shape, array.dtype) for array in arrays]
        + [pltpu.SemaphoreType.DMA((3,))],
        compiler_params=pltpu.CompilerParams(vmem_limit_bytes=60 * 1024 * 1024),
        cost_estimate=pl.CostEstimate(
            flops=64 * tokens * columns, bytes_accessed=400 * tokens * columns, transcendentals=tokens * columns
        ),
        name="gate_cotangent",
    )(jnp.reshape(place, (1,)), lengths, *arrays)


def turn_first_kernel(value_in, turned_ref, buffer, arrived):
    copy = pltpu.make_async_copy(value_in, buffer, arrived)
    copy.start()
    copy.wait()
    turned_ref[...] = buffer[...].T


def turn_first(value):
    rows, columns = value.shape
    return pl.pallas_call(
        turn_first_kernel,
        out_shape=jax.ShapeDtypeStruct((columns, rows), value.dtype),
        in_specs=[pl.BlockSpec(memory_space=pltpu.HBM)],
        out_specs=pl.BlockSpec(memory_space=pltpu.VMEM),
        scratch_shapes=[pltpu.VMEM(value.shape, value.dtype), pltpu.SemaphoreType.DMA],
        compiler_params=pltpu.CompilerParams(vmem_limit_bytes=60 * 1024 * 1024),
        cost_estimate=pl.CostEstimate(flops=rows * columns, bytes_accessed=4 * rows * columns, transcendentals=0),
        name="turn_first",
    )(value)


def turn_kernel(value_ref, turned_ref):
    turned_ref[...] = value_ref[...].T


def turn(value):
    rows, columns = value.shape
    vmem = pl.BlockSpec(memory_space=pltpu.VMEM)
    return pl.pallas_call(
        turn_kernel,
        out_shape=jax.ShapeDtypeStruct((columns, rows), value.dtype),
        in_specs=[vmem],
        out_specs=vmem,
        compiler_params=pltpu.CompilerParams(vmem_limit_bytes=8 * 1024 * 1024),
        cost_estimate=pl.CostEstimate(flops=rows * columns, bytes_accessed=3000 * rows * columns, transcendentals=0),
        name="turn",
    )(value)


def device_number(y, z, t):
    return (y * NZ + z) * NT + t


def line_groups(even_axis):
    groups = []
    for t in range(NT):
        along_y = (t % 2 == 0) == (even_axis == "y")
        for fixed in range(NZ if along_y else NY):
            line = [(i, fixed) if along_y else (fixed, i) for i in range(NY if along_y else NZ)]
            groups.append([device_number(y, z, t) for y, z in line])
    return groups


def tensor_pairs(masks):
    return [
        (device_number(y, z, t), device_number(y, z, t ^ masks[t % 2]))
        for y in range(NY)
        for z in range(NZ)
        for t in range(NT)
    ]


def partial_kernel(orders, t_ref, first_ref, second_ref, grads_ref, out_ref, features):
    rows = out_ref.shape[0]
    tokens = first_ref.shape[1]
    t = t_ref[0]
    blocks = [(ref, start) for ref in (first_ref, second_ref) for start in range(0, ref.shape[0], rows)]

    @pl.when(lax.rem(t, 2) == 0)
    def _():
        for offset, (ref, start) in zip(orders[0], blocks):
            group = lax.bitwise_xor(t, offset)
            features[:, pl.ds(pl.multiple_of(group * tokens, tokens), tokens)] = ref[start : start + rows, :]

    @pl.when(lax.rem(t, 2) == 1)
    def _():
        for offset, (ref, start) in zip(orders[1], blocks):
            block_rows = pl.ds(pl.multiple_of(lax.bitwise_xor(t, offset) * BLK, BLK), BLK)
            for z in range(NZ):
                features[block_rows, z * tokens : (z + 1) * tokens] = ref[
                    start + z * BLK : start + (z + 1) * BLK, :
                ]

    step = 128
    for start in range(0, rows, step):
        product = jnp.dot(
            features[start : start + step, :], grads_ref[...], preferred_element_type=jnp.float32
        )
        out_ref[start : start + step, :] = product.astype(out_ref.dtype)


def partial_product(t, orders, feature_halves, grads):
    tokens, columns = grads.shape
    rows = NZ * BLK
    vmem = pl.BlockSpec(memory_space=pltpu.VMEM)
    return pl.pallas_call(
        functools.partial(partial_kernel, orders),
        out_shape=jax.ShapeDtypeStruct((rows, columns), jnp.bfloat16),
        in_specs=[pl.BlockSpec(memory_space=pltpu.SMEM), vmem, vmem, vmem],
        out_specs=vmem,
        scratch_shapes=[pltpu.VMEM((rows, tokens), jnp.bfloat16)],
        compiler_params=pltpu.CompilerParams(vmem_limit_bytes=32 * 1024 * 1024),
        cost_estimate=pl.CostEstimate(
            flops=2 * tokens * rows * columns, bytes_accessed=6_000_000, transcendentals=0
        ),
        name="partial_product",
    )(jnp.reshape(t, (1,)), *feature_halves, grads)


def momentum_kernel(parts_ref, momentum_ref, moment_ref, nesterov_ref, grams_ref):
    grad = parts_ref[0].astype(jnp.float32)
    for part in range(1, parts_ref.shape[0]):
        grad = grad + parts_ref[part].astype(jnp.float32)
    new_moment = momentum_decay * momentum_ref[...] + grad
    moment_ref[...] = new_moment
    nesterov = grad + momentum_decay * new_moment
    nesterov_ref[...] = nesterov
    gram = lax.dot_general(
        nesterov, nesterov, (((1,), (1,)), ((), ())), precision=HIGHEST, preferred_element_type=jnp.float32
    )
    half = gram.shape[0] // 2
    packed = jnp.concatenate([gram[:half], gram[half:]], axis=1)
    for part in range(grams_ref.shape[0]):
        grams_ref[part] = packed


def momentum_step(parts, momentum):
    size, columns = momentum.shape
    vmem = pl.BlockSpec(memory_space=pltpu.VMEM)
    return pl.pallas_call(
        momentum_kernel,
        out_shape=(
            jax.ShapeDtypeStruct((size, columns), jnp.float32),
            jax.ShapeDtypeStruct((size, columns), jnp.float32),
            jax.ShapeDtypeStruct((NT, size // 2, 2 * size), jnp.float32),
        ),
        in_specs=[vmem, vmem],
        out_specs=(vmem, vmem, vmem),
        compiler_params=pltpu.CompilerParams(vmem_limit_bytes=16 * 1024 * 1024),
        cost_estimate=pl.CostEstimate(flops=60_000_000, bytes_accessed=1_700_000, transcendentals=0),
        name="momentum_step",
    )(parts, momentum)


def polar_kernel(grams_ref, block_ref, out_ref):
    mul = functools.partial(jnp.dot, precision=HIGHEST, preferred_element_type=jnp.float32)
    packed = grams_ref[0]
    for part in range(1, grams_ref.shape[0]):
        packed = packed + grams_ref[part]
    size = packed.shape[1] // 2
    total = jnp.concatenate([packed[:, :size], packed[:, size:]], axis=0)
    shape = (size, size)
    diagonal = lax.broadcasted_iota(jnp.int32, shape, 0) == lax.broadcasted_iota(jnp.int32, shape, 1)
    eye = jnp.where(diagonal, 1.0, 0.0).astype(jnp.float32)
    squares = jnp.sum(jnp.sum(total * eye, axis=1, keepdims=True), axis=0, keepdims=True)
    inverse = 1.0 / (jnp.sqrt(squares) + norm_epsilon)
    gram = total * inverse * inverse
    mapping = None
    for iteration in range(ITERS):
        square = mul(gram, gram)
        poly = linear_coeff * eye + cubic_coeff * gram + quintic_coeff * square
        mapping = poly if iteration == 0 else mul(poly, mapping)
        if iteration < ITERS - 1:
            gram = mul(mul(poly, gram), poly)
    mapping = mapping * (inverse * (update_gain * math.sqrt(HID)))
    units = out_ref.shape[2]
    rows = mul(mapping, block_ref[...]).astype(out_ref.dtype)
    for part in range(out_ref.shape[0]):
        out_ref[part] = rows[:, part * units : (part + 1) * units]


def polar_update(grams, block):
    size, columns = block.shape
    vmem = pl.BlockSpec(memory_space=pltpu.VMEM)
    return pl.pallas_call(
        polar_kernel,
        out_shape=jax.ShapeDtypeStruct((NY, size, columns // NY), jnp.bfloat16),
        in_specs=[vmem, vmem],
        out_specs=vmem,
        compiler_params=pltpu.CompilerParams(vmem_limit_bytes=16 * 1024 * 1024),
        cost_estimate=pl.CostEstimate(flops=100_000_000, bytes_accessed=600_000, transcendentals=0),
        name="polar_update",
    )(grams, block)


def per_device(features, gate_pre, up_pre, hidden_grad, lengths, momentum):
    y, z, t = (lax.axis_index(name) for name in AXES)
    swap = [(a * NT + b, b * NT + a) for a in range(NY) for b in range(NT)]
    swapped = lax.ppermute(features, ("y", "t"), swap)
    turned = turn_first(features)
    copies = gate_cotangent(y * NZ + z, lengths, gate_pre, up_pre, hidden_grad)

    by_blocks = lax.all_to_all(
        turned.reshape(NZ, BLK, turned.shape[1]), "z", split_axis=0, concat_axis=0, tiled=True
    ).reshape(turned.shape)
    copies, by_blocks = lax.optimization_barrier((copies, by_blocks))
    grads = lax.all_to_all(
        copies, AXES, split_axis=0, concat_axis=0, axis_index_groups=line_groups("y"), tiled=True
    ).reshape(-1, copies.shape[2])
    by_tokens = turn(swapped)
    even = lax.rem(t, 2) == 0
    kept = jnp.where(even, by_tokens, by_blocks)
    given = jnp.where(even, by_blocks, by_tokens)
    orders, halves = ([0], [0]), None
    for masks in [m for m in ((1, 1), (2, 6), (6, 2)) if max(m) < NT]:
        arrived = lax.ppermute(given if halves is None else kept, AXES, tensor_pairs(masks))
        orders = tuple(order + [o ^ mask for o in order] for order, mask in zip(orders, masks))
        halves = (kept, arrived)
        kept = jnp.concatenate(halves, axis=0)

    partial_value = partial_product(t, orders, halves, grads)
    pieces = partial_value.reshape(NZ, BLK, partial_value.shape[1])
    received = lax.all_to_all(
        pieces, AXES, split_axis=0, concat_axis=0, axis_index_groups=line_groups("z"), tiled=True
    )
    new_moment, nesterov, grams = momentum_step(received, momentum)
    grams = lax.all_to_all(grams, "t", split_axis=0, concat_axis=0, tiled=True)
    by_y = polar_update(grams, nesterov)
    by_y = lax.all_to_all(by_y, "y", split_axis=0, concat_axis=0, tiled=True)
    unit_count = by_y.shape[2] // NZ
    by_z = by_y.reshape(NY, BLK, NZ, unit_count).transpose(2, 3, 0, 1)
    by_z = lax.all_to_all(by_z, "z", split_axis=0, concat_axis=0, tiled=True)
    result = by_z.transpose(1, 2, 0, 3).reshape(1, unit_count, NY * NZ * BLK)
    return result, new_moment


def solution(mesh):
    fine = Mesh(mesh.devices.reshape(NY, NZ, NT), AXES)
    split = P(("y", "z"), "t")
    return jax.shard_map(
        per_device,
        mesh=fine,
        in_specs=(split, split, split, split, P(), split),
        out_specs=(P("t", ("y", "z"), None), split),
        check_vma=False,
    )
```

```python
import functools
import math

import jax
import jax.numpy as jnp
from jax import lax
from jax.experimental import pallas as pl
from jax.experimental.pallas import tpu as pltpu
from jax.sharding import Mesh
from jax.sharding import PartitionSpec as P

HID = 7168
SEQ_LEN = 128
BLK = 64
ITERS = 5
NY = 8
NZ = 8
NT = 8

momentum_decay = 0.95
linear_coeff = 3.4445
cubic_coeff = -4.775
quintic_coeff = 2.0315
norm_epsilon = 1e-07
update_gain = 0.2

HIGHEST = lax.Precision.HIGHEST
AXES = ("y", "z", "t")


def gate_kernel(place_ref, lengths_ref, gate_in, up_in, cotangent_in, copies_ref, *scratch):
    buffers, arrived = scratch[:3], scratch[3]
    sources = (gate_in, up_in, cotangent_in)
    copies = [
        pltpu.make_async_copy(source, buffer, arrived.at[i])
        for i, (source, buffer) in enumerate(zip(sources, buffers))
    ]
    for copy in copies:
        copy.start()
    for copy in copies:
        copy.wait()
    gate_value, up_value, cotangent = (buffer[...].astype(jnp.float32) for buffer in buffers)
    sigmoid_gate = jax.nn.sigmoid(gate_value)
    gate_grad = cotangent * up_value * sigmoid_gate * (1.0 + gate_value * (1.0 - sigmoid_gate))
    position = lax.broadcasted_iota(jnp.int32, gate_value.shape, 0)
    trained = position < lengths_ref[place_ref[0]]
    gate_grad = jnp.where(trained, gate_grad, 0.0).astype(copies_ref.dtype)
    for part in range(copies_ref.shape[0]):
        copies_ref[part] = gate_grad


def gate_cotangent(place, lengths, gate_pre, up_pre, hidden_grad):
    tokens, columns = gate_pre.shape
    hbm = pl.BlockSpec(memory_space=pltpu.HBM)
    vmem = pl.BlockSpec(memory_space=pltpu.VMEM)
    smem = pl.BlockSpec(memory_space=pltpu.SMEM)
    arrays = (gate_pre, up_pre, hidden_grad)
    return pl.pallas_call(
        gate_kernel,
        out_shape=jax.ShapeDtypeStruct((NZ, tokens, columns), jnp.bfloat16),
        in_specs=[smem, smem] + [hbm] * 3,
        out_specs=vmem,
        scratch_shapes=[pltpu.VMEM(array.shape, array.dtype) for array in arrays]
        + [pltpu.SemaphoreType.DMA((3,))],
        compiler_params=pltpu.CompilerParams(vmem_limit_bytes=60 * 1024 * 1024),
        cost_estimate=pl.CostEstimate(
            flops=64 * tokens * columns, bytes_accessed=400 * tokens * columns, transcendentals=tokens * columns
        ),
        name="gate_cotangent",
    )(jnp.reshape(place, (1,)), lengths, *arrays)


def turn_first_kernel(value_in, turned_ref, buffer, arrived):
    copy = pltpu.make_async_copy(value_in, buffer, arrived)
    copy.start()
    copy.wait()
    turned_ref[...] = buffer[...].T


def turn_first(value):
    rows, columns = value.shape
    return pl.pallas_call(
        turn_first_kernel,
        out_shape=jax.ShapeDtypeStruct((columns, rows), value.dtype),
        in_specs=[pl.BlockSpec(memory_space=pltpu.HBM)],
        out_specs=pl.BlockSpec(memory_space=pltpu.VMEM),
        scratch_shapes=[pltpu.VMEM(value.shape, value.dtype), pltpu.SemaphoreType.DMA],
        compiler_params=pltpu.CompilerParams(vmem_limit_bytes=60 * 1024 * 1024),
        cost_estimate=pl.CostEstimate(flops=rows * columns, bytes_accessed=4 * rows * columns, transcendentals=0),
        name="turn_first",
    )(value)


def turn_kernel(value_ref, turned_ref):
    turned_ref[...] = value_ref[...].T


def turn(value):
    rows, columns = value.shape
    vmem = pl.BlockSpec(memory_space=pltpu.VMEM)
    return pl.pallas_call(
        turn_kernel,
        out_shape=jax.ShapeDtypeStruct((columns, rows), value.dtype),
        in_specs=[vmem],
        out_specs=vmem,
        compiler_params=pltpu.CompilerParams(vmem_limit_bytes=8 * 1024 * 1024),
        cost_estimate=pl.CostEstimate(flops=rows * columns, bytes_accessed=4 * rows * columns, transcendentals=0),
        name="turn",
    )(value)


def device_number(y, z, t):
    return (y * NZ + z) * NT + t


def line_groups(even_axis):
    groups = []
    for t in range(NT):
        along_y = (t % 2 == 0) == (even_axis == "y")
        for fixed in range(NZ if along_y else NY):
            line = [(i, fixed) if along_y else (fixed, i) for i in range(NY if along_y else NZ)]
            groups.append([device_number(y, z, t) for y, z in line])
    return groups


def tensor_pairs(masks):
    return [
        (device_number(y, z, t), device_number(y, z, t ^ masks[t % 2]))
        for y in range(NY)
        for z in range(NZ)
        for t in range(NT)
    ]


def partial_kernel(orders, t_ref, first_ref, second_ref, grads_ref, out_ref, features):
    rows = out_ref.shape[0]
    tokens = first_ref.shape[1]
    t = t_ref[0]
    blocks = [(ref, start) for ref in (first_ref, second_ref) for start in range(0, ref.shape[0], rows)]

    @pl.when(lax.rem(t, 2) == 0)
    def _():
        for offset, (ref, start) in zip(orders[0], blocks):
            group = lax.bitwise_xor(t, offset)
            features[:, pl.ds(pl.multiple_of(group * tokens, tokens), tokens)] = ref[start : start + rows, :]

    @pl.when(lax.rem(t, 2) == 1)
    def _():
        for offset, (ref, start) in zip(orders[1], blocks):
            block_rows = pl.ds(pl.multiple_of(lax.bitwise_xor(t, offset) * BLK, BLK), BLK)
            for z in range(NZ):
                features[block_rows, z * tokens : (z + 1) * tokens] = ref[
                    start + z * BLK : start + (z + 1) * BLK, :
                ]

    step = 128
    for start in range(0, rows, step):
        product = jnp.dot(
            features[start : start + step, :], grads_ref[...], preferred_element_type=jnp.float32
        )
        out_ref[start : start + step, :] = product.astype(out_ref.dtype)


def partial_product(t, orders, feature_halves, grads):
    tokens, columns = grads.shape
    rows = NZ * BLK
    vmem = pl.BlockSpec(memory_space=pltpu.VMEM)
    return pl.pallas_call(
        functools.partial(partial_kernel, orders),
        out_shape=jax.ShapeDtypeStruct((rows, columns), jnp.bfloat16),
        in_specs=[pl.BlockSpec(memory_space=pltpu.SMEM), vmem, vmem, vmem],
        out_specs=vmem,
        scratch_shapes=[pltpu.VMEM((rows, tokens), jnp.bfloat16)],
        compiler_params=pltpu.CompilerParams(vmem_limit_bytes=32 * 1024 * 1024),
        cost_estimate=pl.CostEstimate(
            flops=2 * tokens * rows * columns, bytes_accessed=6_000_000, transcendentals=0
        ),
        name="partial_product",
    )(jnp.reshape(t, (1,)), *feature_halves, grads)


def momentum_kernel(parts_ref, momentum_ref, moment_ref, nesterov_ref, grams_ref):
    grad = parts_ref[0].astype(jnp.float32)
    for part in range(1, parts_ref.shape[0]):
        grad = grad + parts_ref[part].astype(jnp.float32)
    new_moment = momentum_decay * momentum_ref[...] + grad
    moment_ref[...] = new_moment
    nesterov = grad + momentum_decay * new_moment
    nesterov_ref[...] = nesterov
    gram = lax.dot_general(
        nesterov, nesterov, (((1,), (1,)), ((), ())), precision=HIGHEST, preferred_element_type=jnp.float32
    )
    half = gram.shape[0] // 2
    packed = jnp.concatenate([gram[:half], gram[half:]], axis=1)
    for part in range(grams_ref.shape[0]):
        grams_ref[part] = packed


def momentum_step(parts, momentum):
    size, columns = momentum.shape
    vmem = pl.BlockSpec(memory_space=pltpu.VMEM)
    return pl.pallas_call(
        momentum_kernel,
        out_shape=(
            jax.ShapeDtypeStruct((size, columns), jnp.float32),
            jax.ShapeDtypeStruct((size, columns), jnp.float32),
            jax.ShapeDtypeStruct((NT, size // 2, 2 * size), jnp.float32),
        ),
        in_specs=[vmem, vmem],
        out_specs=(vmem, vmem, vmem),
        compiler_params=pltpu.CompilerParams(vmem_limit_bytes=16 * 1024 * 1024),
        cost_estimate=pl.CostEstimate(flops=60_000_000, bytes_accessed=1_700_000, transcendentals=0),
        name="momentum_step",
    )(parts, momentum)


def polar_kernel(grams_ref, block_ref, out_ref):
    mul = functools.partial(jnp.dot, precision=HIGHEST, preferred_element_type=jnp.float32)
    packed = grams_ref[0]
    for part in range(1, grams_ref.shape[0]):
        packed = packed + grams_ref[part]
    size = packed.shape[1] // 2
    total = jnp.concatenate([packed[:, :size], packed[:, size:]], axis=0)
    shape = (size, size)
    diagonal = lax.broadcasted_iota(jnp.int32, shape, 0) == lax.broadcasted_iota(jnp.int32, shape, 1)
    eye = jnp.where(diagonal, 1.0, 0.0).astype(jnp.float32)
    squares = jnp.sum(jnp.sum(total * eye, axis=1, keepdims=True), axis=0, keepdims=True)
    inverse = 1.0 / (jnp.sqrt(squares) + norm_epsilon)
    gram = total * inverse * inverse
    mapping = None
    for iteration in range(ITERS):
        square = mul(gram, gram)
        poly = linear_coeff * eye + cubic_coeff * gram + quintic_coeff * square
        mapping = poly if iteration == 0 else mul(poly, mapping)
        if iteration < ITERS - 1:
            gram = mul(mul(poly, gram), poly)
    mapping = mapping * (inverse * (update_gain * math.sqrt(HID)))
    units = out_ref.shape[2]
    rows = mul(mapping, block_ref[...]).astype(out_ref.dtype)
    for part in range(out_ref.shape[0]):
        out_ref[part] = rows[:, part * units : (part + 1) * units]


def polar_update(grams, block):
    size, columns = block.shape
    vmem = pl.BlockSpec(memory_space=pltpu.VMEM)
    return pl.pallas_call(
        polar_kernel,
        out_shape=jax.ShapeDtypeStruct((NY, size, columns // NY), jnp.bfloat16),
        in_specs=[vmem, vmem],
        out_specs=vmem,
        compiler_params=pltpu.CompilerParams(vmem_limit_bytes=16 * 1024 * 1024),
        cost_estimate=pl.CostEstimate(flops=100_000_000, bytes_accessed=600_000, transcendentals=0),
        name="polar_update",
    )(grams, block)


def per_device(features, gate_pre, up_pre, hidden_grad, lengths, momentum):
    y, z, t = (lax.axis_index(name) for name in AXES)
    swap = [(a * NT + b, b * NT + a) for a in range(NY) for b in range(NT)]
    swapped = lax.ppermute(features, ("y", "t"), swap)
    turned, swapped = lax.optimization_barrier((turn_first(features), swapped))
    copies = gate_cotangent(y * NZ + z, lengths, gate_pre, up_pre, hidden_grad)

    by_blocks = lax.all_to_all(
        turned.reshape(NZ, BLK, turned.shape[1]), "z", split_axis=0, concat_axis=0, tiled=True
    ).reshape(turned.shape)
    copies, by_blocks = lax.optimization_barrier((copies, by_blocks))
    grads = lax.all_to_all(
        copies, AXES, split_axis=0, concat_axis=0, axis_index_groups=line_groups("y"), tiled=True
    ).reshape(-1, copies.shape[2])
    by_tokens = turn(swapped)
    even = lax.rem(t, 2) == 0
    kept = jnp.where(even, by_tokens, by_blocks)
    given = jnp.where(even, by_blocks, by_tokens)
    orders, halves = ([0], [0]), None
    for masks in [m for m in ((1, 1), (2, 6), (6, 2)) if max(m) < NT]:
        arrived = lax.ppermute(given if halves is None else kept, AXES, tensor_pairs(masks))
        orders = tuple(order + [o ^ mask for o in order] for order, mask in zip(orders, masks))
        halves = (kept, arrived)
        kept = jnp.concatenate(halves, axis=0)

    partial_value = partial_product(t, orders, halves, grads)
    pieces = partial_value.reshape(NZ, BLK, partial_value.shape[1])
    received = lax.all_to_all(
        pieces, AXES, split_axis=0, concat_axis=0, axis_index_groups=line_groups("z"), tiled=True
    )
    new_moment, nesterov, grams = momentum_step(received, momentum)
    grams = lax.all_to_all(grams, "t", split_axis=0, concat_axis=0, tiled=True)
    by_y = polar_update(grams, nesterov)
    by_y = lax.all_to_all(by_y, "y", split_axis=0, concat_axis=0, tiled=True)
    unit_count = by_y.shape[2] // NZ
    by_z = by_y.reshape(NY, BLK, NZ, unit_count).transpose(2, 3, 0, 1)
    by_z = lax.all_to_all(by_z, "z", split_axis=0, concat_axis=0, tiled=True)
    result = by_z.transpose(1, 2, 0, 3).reshape(1, unit_count, NY * NZ * BLK)
    return result, new_moment


def solution(mesh):
    fine = Mesh(mesh.devices.reshape(NY, NZ, NT), AXES)
    split = P(("y", "z"), "t")
    return jax.shard_map(
        per_device,
        mesh=fine,
        in_specs=(split, split, split, split, P(), split),
        out_specs=(P("t", ("y", "z"), None), split),
        check_vma=False,
    )
```

```python
import functools
import math

import jax
import jax.numpy as jnp
from jax import lax
from jax.experimental import pallas as pl
from jax.experimental.pallas import tpu as pltpu
from jax.sharding import Mesh
from jax.sharding import PartitionSpec as P

HID = 7168
SEQ_LEN = 128
BLK = 64
ITERS = 5
NY = 8
NZ = 8
NT = 8

momentum_decay = 0.95
linear_coeff = 3.4445
cubic_coeff = -4.775
quintic_coeff = 2.0315
norm_epsilon = 1e-07
update_gain = 0.2

HIGHEST = lax.Precision.HIGHEST
AXES = ("y", "z", "t")


def gate_kernel(place_ref, lengths_ref, gate_in, up_in, cotangent_in, copies_ref, *scratch):
    buffers, arrived = scratch[:3], scratch[3]
    sources = (gate_in, up_in, cotangent_in)
    copies = [
        pltpu.make_async_copy(source, buffer, arrived.at[i])
        for i, (source, buffer) in enumerate(zip(sources, buffers))
    ]
    for copy in copies:
        copy.start()
    for copy in copies:
        copy.wait()
    gate_value, up_value, cotangent = (buffer[...].astype(jnp.float32) for buffer in buffers)
    sigmoid_gate = jax.nn.sigmoid(gate_value)
    gate_grad = cotangent * up_value * sigmoid_gate * (1.0 + gate_value * (1.0 - sigmoid_gate))
    position = lax.broadcasted_iota(jnp.int32, gate_value.shape, 0)
    trained = position < lengths_ref[place_ref[0]]
    gate_grad = jnp.where(trained, gate_grad, 0.0).astype(copies_ref.dtype)
    for part in range(copies_ref.shape[0]):
        copies_ref[part] = gate_grad


def gate_cotangent(place, lengths, gate_pre, up_pre, hidden_grad):
    tokens, columns = gate_pre.shape
    hbm = pl.BlockSpec(memory_space=pltpu.HBM)
    vmem = pl.BlockSpec(memory_space=pltpu.VMEM)
    smem = pl.BlockSpec(memory_space=pltpu.SMEM)
    arrays = (gate_pre, up_pre, hidden_grad)
    return pl.pallas_call(
        gate_kernel,
        out_shape=jax.ShapeDtypeStruct((NZ, tokens, columns), jnp.bfloat16),
        in_specs=[smem, smem] + [hbm] * 3,
        out_specs=vmem,
        scratch_shapes=[pltpu.VMEM(array.shape, array.dtype) for array in arrays]
        + [pltpu.SemaphoreType.DMA((3,))],
        compiler_params=pltpu.CompilerParams(vmem_limit_bytes=60 * 1024 * 1024),
        cost_estimate=pl.CostEstimate(
            flops=64 * tokens * columns, bytes_accessed=8000 * tokens * columns, transcendentals=tokens * columns
        ),
        name="gate_cotangent",
    )(jnp.reshape(place, (1,)), lengths, *arrays)


def turn_first_kernel(value_in, turned_ref, buffer, arrived):
    copy = pltpu.make_async_copy(value_in, buffer, arrived)
    copy.start()
    copy.wait()
    turned_ref[...] = buffer[...].T


def turn_first(value):
    rows, columns = value.shape
    return pl.pallas_call(
        turn_first_kernel,
        out_shape=jax.ShapeDtypeStruct((columns, rows), value.dtype),
        in_specs=[pl.BlockSpec(memory_space=pltpu.HBM)],
        out_specs=pl.BlockSpec(memory_space=pltpu.VMEM),
        scratch_shapes=[pltpu.VMEM(value.shape, value.dtype), pltpu.SemaphoreType.DMA],
        compiler_params=pltpu.CompilerParams(vmem_limit_bytes=60 * 1024 * 1024),
        cost_estimate=pl.CostEstimate(flops=rows * columns, bytes_accessed=4 * rows * columns, transcendentals=0),
        name="turn_first",
    )(value)


def turn_kernel(value_ref, turned_ref):
    turned_ref[...] = value_ref[...].T


def turn(value):
    rows, columns = value.shape
    vmem = pl.BlockSpec(memory_space=pltpu.VMEM)
    return pl.pallas_call(
        turn_kernel,
        out_shape=jax.ShapeDtypeStruct((columns, rows), value.dtype),
        in_specs=[vmem],
        out_specs=vmem,
        compiler_params=pltpu.CompilerParams(vmem_limit_bytes=8 * 1024 * 1024),
        cost_estimate=pl.CostEstimate(flops=rows * columns, bytes_accessed=4 * rows * columns, transcendentals=0),
        name="turn",
    )(value)


def device_number(y, z, t):
    return (y * NZ + z) * NT + t


def line_groups(even_axis):
    groups = []
    for t in range(NT):
        along_y = (t % 2 == 0) == (even_axis == "y")
        for fixed in range(NZ if along_y else NY):
            line = [(i, fixed) if along_y else (fixed, i) for i in range(NY if along_y else NZ)]
            groups.append([device_number(y, z, t) for y, z in line])
    return groups


def tensor_pairs(masks):
    return [
        (device_number(y, z, t), device_number(y, z, t ^ masks[t % 2]))
        for y in range(NY)
        for z in range(NZ)
        for t in range(NT)
    ]


def partial_kernel(orders, t_ref, first_ref, second_ref, grads_ref, out_ref, features):
    rows = out_ref.shape[0]
    tokens = first_ref.shape[1]
    t = t_ref[0]
    blocks = [(ref, start) for ref in (first_ref, second_ref) for start in range(0, ref.shape[0], rows)]

    @pl.when(lax.rem(t, 2) == 0)
    def _():
        for offset, (ref, start) in zip(orders[0], blocks):
            group = lax.bitwise_xor(t, offset)
            features[:, pl.ds(pl.multiple_of(group * tokens, tokens), tokens)] = ref[start : start + rows, :]

    @pl.when(lax.rem(t, 2) == 1)
    def _():
        for offset, (ref, start) in zip(orders[1], blocks):
            block_rows = pl.ds(pl.multiple_of(lax.bitwise_xor(t, offset) * BLK, BLK), BLK)
            for z in range(NZ):
                features[block_rows, z * tokens : (z + 1) * tokens] = ref[
                    start + z * BLK : start + (z + 1) * BLK, :
                ]

    step = 128
    for start in range(0, rows, step):
        product = jnp.dot(
            features[start : start + step, :], grads_ref[...], preferred_element_type=jnp.float32
        )
        out_ref[start : start + step, :] = product.astype(out_ref.dtype)


def partial_product(t, orders, feature_halves, grads):
    tokens, columns = grads.shape
    rows = NZ * BLK
    vmem = pl.BlockSpec(memory_space=pltpu.VMEM)
    return pl.pallas_call(
        functools.partial(partial_kernel, orders),
        out_shape=jax.ShapeDtypeStruct((rows, columns), jnp.bfloat16),
        in_specs=[pl.BlockSpec(memory_space=pltpu.SMEM), vmem, vmem, vmem],
        out_specs=vmem,
        scratch_shapes=[pltpu.VMEM((rows, tokens), jnp.bfloat16)],
        compiler_params=pltpu.CompilerParams(vmem_limit_bytes=32 * 1024 * 1024),
        cost_estimate=pl.CostEstimate(
            flops=2 * tokens * rows * columns, bytes_accessed=6_000_000, transcendentals=0
        ),
        name="partial_product",
    )(jnp.reshape(t, (1,)), *feature_halves, grads)


def momentum_kernel(parts_ref, momentum_ref, moment_ref, nesterov_ref, grams_ref):
    grad = parts_ref[0].astype(jnp.float32)
    for part in range(1, parts_ref.shape[0]):
        grad = grad + parts_ref[part].astype(jnp.float32)
    new_moment = momentum_decay * momentum_ref[...] + grad
    moment_ref[...] = new_moment
    nesterov = grad + momentum_decay * new_moment
    nesterov_ref[...] = nesterov
    gram = lax.dot_general(
        nesterov, nesterov, (((1,), (1,)), ((), ())), precision=HIGHEST, preferred_element_type=jnp.float32
    )
    half = gram.shape[0] // 2
    packed = jnp.concatenate([gram[:half], gram[half:]], axis=1)
    for part in range(grams_ref.shape[0]):
        grams_ref[part] = packed


def momentum_step(parts, momentum):
    size, columns = momentum.shape
    vmem = pl.BlockSpec(memory_space=pltpu.VMEM)
    return pl.pallas_call(
        momentum_kernel,
        out_shape=(
            jax.ShapeDtypeStruct((size, columns), jnp.float32),
            jax.ShapeDtypeStruct((size, columns), jnp.float32),
            jax.ShapeDtypeStruct((NT, size // 2, 2 * size), jnp.float32),
        ),
        in_specs=[vmem, vmem],
        out_specs=(vmem, vmem, vmem),
        compiler_params=pltpu.CompilerParams(vmem_limit_bytes=16 * 1024 * 1024),
        cost_estimate=pl.CostEstimate(flops=60_000_000, bytes_accessed=1_700_000, transcendentals=0),
        name="momentum_step",
    )(parts, momentum)


def polar_kernel(grams_ref, block_ref, out_ref):
    mul = functools.partial(jnp.dot, precision=HIGHEST, preferred_element_type=jnp.float32)
    packed = grams_ref[0]
    for part in range(1, grams_ref.shape[0]):
        packed = packed + grams_ref[part]
    size = packed.shape[1] // 2
    total = jnp.concatenate([packed[:, :size], packed[:, size:]], axis=0)
    shape = (size, size)
    diagonal = lax.broadcasted_iota(jnp.int32, shape, 0) == lax.broadcasted_iota(jnp.int32, shape, 1)
    eye = jnp.where(diagonal, 1.0, 0.0).astype(jnp.float32)
    squares = jnp.sum(jnp.sum(total * eye, axis=1, keepdims=True), axis=0, keepdims=True)
    inverse = 1.0 / (jnp.sqrt(squares) + norm_epsilon)
    gram = total * inverse * inverse
    mapping = None
    for iteration in range(ITERS):
        square = mul(gram, gram)
        poly = linear_coeff * eye + cubic_coeff * gram + quintic_coeff * square
        mapping = poly if iteration == 0 else mul(poly, mapping)
        if iteration < ITERS - 1:
            gram = mul(mul(poly, gram), poly)
    mapping = mapping * (inverse * (update_gain * math.sqrt(HID)))
    units = out_ref.shape[2]
    rows = mul(mapping, block_ref[...]).astype(out_ref.dtype)
    for part in range(out_ref.shape[0]):
        out_ref[part] = rows[:, part * units : (part + 1) * units]


def polar_update(grams, block):
    size, columns = block.shape
    vmem = pl.BlockSpec(memory_space=pltpu.VMEM)
    return pl.pallas_call(
        polar_kernel,
        out_shape=jax.ShapeDtypeStruct((NY, size, columns // NY), jnp.bfloat16),
        in_specs=[vmem, vmem],
        out_specs=vmem,
        compiler_params=pltpu.CompilerParams(vmem_limit_bytes=16 * 1024 * 1024),
        cost_estimate=pl.CostEstimate(flops=100_000_000, bytes_accessed=600_000, transcendentals=0),
        name="polar_update",
    )(grams, block)


def per_device(features, gate_pre, up_pre, hidden_grad, lengths, momentum):
    y, z, t = (lax.axis_index(name) for name in AXES)
    swap = [(a * NT + b, b * NT + a) for a in range(NY) for b in range(NT)]
    swapped = lax.ppermute(features, ("y", "t"), swap)
    turned = turn_first(features)
    copies = gate_cotangent(y * NZ + z, lengths, gate_pre, up_pre, hidden_grad)

    by_blocks = lax.all_to_all(
        turned.reshape(NZ, BLK, turned.shape[1]), "z", split_axis=0, concat_axis=0, tiled=True
    ).reshape(turned.shape)
    by_blocks, swapped, copies = lax.optimization_barrier((by_blocks, swapped, copies))
    grads = lax.all_to_all(
        copies, AXES, split_axis=0, concat_axis=0, axis_index_groups=line_groups("y"), tiled=True
    ).reshape(-1, copies.shape[2])
    by_tokens = turn(swapped)
    odd = lax.rem(t, 2) == 1
    kept = jnp.where(odd, by_blocks, by_tokens)
    given = jnp.where(odd, by_tokens, by_blocks)
    orders, halves = ([0], [0]), None
    for masks in [m for m in ((1, 1), (2, 6), (6, 2)) if max(m) < NT]:
        arrived = lax.ppermute(given if halves is None else kept, AXES, tensor_pairs(masks))
        orders = tuple(order + [o ^ mask for o in order] for order, mask in zip(orders, masks))
        halves = (kept, arrived)
        kept = jnp.concatenate(halves, axis=0)

    partial_value = partial_product(t, orders, halves, grads)
    pieces = partial_value.reshape(NZ, BLK, partial_value.shape[1])
    received = lax.all_to_all(
        pieces, AXES, split_axis=0, concat_axis=0, axis_index_groups=line_groups("z"), tiled=True
    )
    new_moment, nesterov, grams = momentum_step(received, momentum)
    grams = lax.all_to_all(grams, "t", split_axis=0, concat_axis=0, tiled=True)
    by_y = polar_update(grams, nesterov)
    by_y = lax.all_to_all(by_y, "y", split_axis=0, concat_axis=0, tiled=True)
    unit_count = by_y.shape[2] // NZ
    by_z = by_y.reshape(NY, BLK, NZ, unit_count).transpose(2, 3, 0, 1)
    by_z = lax.all_to_all(by_z, "z", split_axis=0, concat_axis=0, tiled=True)
    result = by_z.transpose(1, 2, 0, 3).reshape(1, unit_count, NY * NZ * BLK)
    return result, new_moment


def solution(mesh):
    fine = Mesh(mesh.devices.reshape(NY, NZ, NT), AXES)
    split = P(("y", "z"), "t")
    return jax.shard_map(
        per_device,
        mesh=fine,
        in_specs=(split, split, split, split, P(), split),
        out_specs=(P("t", ("y", "z"), None), split),
        check_vma=False,
    )
```

```python
import functools
import math

import jax
import jax.numpy as jnp
from jax import lax
from jax.experimental import pallas as pl
from jax.experimental.pallas import tpu as pltpu
from jax.sharding import Mesh
from jax.sharding import PartitionSpec as P

HID = 7168
SEQ_LEN = 128
BLK = 64
ITERS = 5
NY = 8
NZ = 8
NT = 8

momentum_decay = 0.95
linear_coeff = 3.4445
cubic_coeff = -4.775
quintic_coeff = 2.0315
norm_epsilon = 1e-07
update_gain = 0.2

HIGHEST = lax.Precision.HIGHEST
AXES = ("y", "z", "t")


def gate_kernel(place_ref, lengths_ref, gate_in, up_in, cotangent_in, copies_ref, *scratch):
    buffers, arrived = scratch[:3], scratch[3]
    sources = (gate_in, up_in, cotangent_in)
    copies = [
        pltpu.make_async_copy(source, buffer, arrived.at[i])
        for i, (source, buffer) in enumerate(zip(sources, buffers))
    ]
    for copy in copies:
        copy.start()
    for copy in copies:
        copy.wait()
    gate_value, up_value, cotangent = (buffer[...].astype(jnp.float32) for buffer in buffers)
    sigmoid_gate = jax.nn.sigmoid(gate_value)
    gate_grad = cotangent * up_value * sigmoid_gate * (1.0 + gate_value * (1.0 - sigmoid_gate))
    position = lax.broadcasted_iota(jnp.int32, gate_value.shape, 0)
    trained = position < lengths_ref[place_ref[0]]
    gate_grad = jnp.where(trained, gate_grad, 0.0).astype(copies_ref.dtype)
    for part in range(copies_ref.shape[0]):
        copies_ref[part] = gate_grad


def gate_cotangent(place, lengths, gate_pre, up_pre, hidden_grad):
    tokens, columns = gate_pre.shape
    hbm = pl.BlockSpec(memory_space=pltpu.HBM)
    vmem = pl.BlockSpec(memory_space=pltpu.VMEM)
    smem = pl.BlockSpec(memory_space=pltpu.SMEM)
    arrays = (gate_pre, up_pre, hidden_grad)
    return pl.pallas_call(
        gate_kernel,
        out_shape=jax.ShapeDtypeStruct((NZ, tokens, columns), jnp.bfloat16),
        in_specs=[smem, smem] + [hbm] * 3,
        out_specs=vmem,
        scratch_shapes=[pltpu.VMEM(array.shape, array.dtype) for array in arrays]
        + [pltpu.SemaphoreType.DMA((3,))],
        compiler_params=pltpu.CompilerParams(vmem_limit_bytes=60 * 1024 * 1024),
        cost_estimate=pl.CostEstimate(
            flops=64 * tokens * columns, bytes_accessed=400 * tokens * columns, transcendentals=tokens * columns
        ),
        name="gate_cotangent",
    )(jnp.reshape(place, (1,)), lengths, *arrays)


def arrange_kernel(orders, t_ref, first_ref, second_ref, out_ref):
    tokens = out_ref.shape[2]
    t = t_ref[0]
    blocks = [(ref, start) for ref in (first_ref, second_ref) for start in range(0, ref.shape[0], tokens)]

    @pl.when(lax.rem(t, 2) == 0)
    def _():
        for offset, (ref, start) in zip(orders[0], blocks):
            out_ref[lax.bitwise_xor(t, offset)] = ref[start : start + tokens, :].T

    @pl.when(lax.rem(t, 2) == 1)
    def _():
        for offset, (ref, start) in zip(orders[1], blocks):
            turned = ref[start : start + tokens, :].T
            rows = pl.ds(pl.multiple_of(lax.bitwise_xor(t, offset) * BLK, BLK), BLK)
            for z in range(NZ):
                out_ref[z, rows, :] = turned[z * BLK : (z + 1) * BLK, :]


def arrange(t, orders, halves, tokens):
    rows = halves[0].shape[1]
    vmem = pl.BlockSpec(memory_space=pltpu.VMEM)
    return pl.pallas_call(
        functools.partial(arrange_kernel, orders),
        out_shape=jax.ShapeDtypeStruct((NZ, rows, tokens), jnp.bfloat16),
        in_specs=[pl.BlockSpec(memory_space=pltpu.SMEM), vmem, vmem],
        out_specs=vmem,
        compiler_params=pltpu.CompilerParams(vmem_limit_bytes=16 * 1024 * 1024),
        cost_estimate=pl.CostEstimate(
            flops=NZ * rows * tokens, bytes_accessed=4 * NZ * rows * tokens, transcendentals=0
        ),
        name="arrange",
    )(jnp.reshape(t, (1,)), *halves)


def device_number(y, z, t):
    return (y * NZ + z) * NT + t


def line_groups(even_axis):
    groups = []
    for t in range(NT):
        along_y = (t % 2 == 0) == (even_axis == "y")
        for fixed in range(NZ if along_y else NY):
            line = [(i, fixed) if along_y else (fixed, i) for i in range(NY if along_y else NZ)]
            groups.append([device_number(y, z, t) for y, z in line])
    return groups


def tensor_pairs(masks):
    return [
        (device_number(y, z, t), device_number(y, z, t ^ masks[t % 2]))
        for y in range(NY)
        for z in range(NZ)
        for t in range(NT)
    ]


def partial_kernel(pieces_ref, grads_ref, out_ref, features):
    rows = out_ref.shape[0]
    tokens = pieces_ref.shape[2]
    for group in range(pieces_ref.shape[0]):
        features[:, group * tokens : (group + 1) * tokens] = pieces_ref[group]
    step = 128
    for start in range(0, rows, step):
        product = jnp.dot(
            features[start : start + step, :], grads_ref[...], preferred_element_type=jnp.float32
        )
        out_ref[start : start + step, :] = product.astype(out_ref.dtype)


def partial_product(pieces, grads):
    tokens, columns = grads.shape
    rows = pieces.shape[1]
    vmem = pl.BlockSpec(memory_space=pltpu.VMEM)
    return pl.pallas_call(
        partial_kernel,
        out_shape=jax.ShapeDtypeStruct((rows, columns), jnp.bfloat16),
        in_specs=[vmem, vmem],
        out_specs=vmem,
        scratch_shapes=[pltpu.VMEM((rows, tokens), jnp.bfloat16)],
        compiler_params=pltpu.CompilerParams(vmem_limit_bytes=32 * 1024 * 1024),
        cost_estimate=pl.CostEstimate(
            flops=2 * tokens * rows * columns, bytes_accessed=6_000_000, transcendentals=0
        ),
        name="partial_product",
    )(pieces, grads)


def momentum_kernel(parts_ref, momentum_ref, moment_ref, nesterov_ref, grams_ref):
    grad = parts_ref[0].astype(jnp.float32)
    for part in range(1, parts_ref.shape[0]):
        grad = grad + parts_ref[part].astype(jnp.float32)
    new_moment = momentum_decay * momentum_ref[...] + grad
    moment_ref[...] = new_moment
    nesterov = grad + momentum_decay * new_moment
    nesterov_ref[...] = nesterov
    gram = lax.dot_general(
        nesterov, nesterov, (((1,), (1,)), ((), ())), precision=HIGHEST, preferred_element_type=jnp.float32
    )
    half = gram.shape[0] // 2
    packed = jnp.concatenate([gram[:half], gram[half:]], axis=1)
    for part in range(grams_ref.shape[0]):
        grams_ref[part] = packed


def momentum_step(parts, momentum):
    size, columns = momentum.shape
    vmem = pl.BlockSpec(memory_space=pltpu.VMEM)
    return pl.pallas_call(
        momentum_kernel,
        out_shape=(
            jax.ShapeDtypeStruct((size, columns), jnp.float32),
            jax.ShapeDtypeStruct((size, columns), jnp.float32),
            jax.ShapeDtypeStruct((NT, size // 2, 2 * size), jnp.float32),
        ),
        in_specs=[vmem, vmem],
        out_specs=(vmem, vmem, vmem),
        compiler_params=pltpu.CompilerParams(vmem_limit_bytes=16 * 1024 * 1024),
        cost_estimate=pl.CostEstimate(flops=60_000_000, bytes_accessed=1_700_000, transcendentals=0),
        name="momentum_step",
    )(parts, momentum)


def polar_kernel(grams_ref, block_ref, out_ref):
    mul = functools.partial(jnp.dot, precision=HIGHEST, preferred_element_type=jnp.float32)
    packed = grams_ref[0]
    for part in range(1, grams_ref.shape[0]):
        packed = packed + grams_ref[part]
    size = packed.shape[1] // 2
    total = jnp.concatenate([packed[:, :size], packed[:, size:]], axis=0)
    shape = (size, size)
    diagonal = lax.broadcasted_iota(jnp.int32, shape, 0) == lax.broadcasted_iota(jnp.int32, shape, 1)
    eye = jnp.where(diagonal, 1.0, 0.0).astype(jnp.float32)
    squares = jnp.sum(jnp.sum(total * eye, axis=1, keepdims=True), axis=0, keepdims=True)
    inverse = 1.0 / (jnp.sqrt(squares) + norm_epsilon)
    gram = total * inverse * inverse
    mapping = None
    for iteration in range(ITERS):
        square = mul(gram, gram)
        poly = linear_coeff * eye + cubic_coeff * gram + quintic_coeff * square
        mapping = poly if iteration == 0 else mul(poly, mapping)
        if iteration < ITERS - 1:
            gram = mul(mul(poly, gram), poly)
    mapping = mapping * (inverse * (update_gain * math.sqrt(HID)))
    units = out_ref.shape[2]
    rows = mul(mapping, block_ref[...]).astype(out_ref.dtype)
    for part in range(out_ref.shape[0]):
        out_ref[part] = rows[:, part * units : (part + 1) * units]


def polar_update(grams, block):
    size, columns = block.shape
    vmem = pl.BlockSpec(memory_space=pltpu.VMEM)
    return pl.pallas_call(
        polar_kernel,
        out_shape=jax.ShapeDtypeStruct((NY, size, columns // NY), jnp.bfloat16),
        in_specs=[vmem, vmem],
        out_specs=vmem,
        compiler_params=pltpu.CompilerParams(vmem_limit_bytes=16 * 1024 * 1024),
        cost_estimate=pl.CostEstimate(flops=100_000_000, bytes_accessed=600_000, transcendentals=0),
        name="polar_update",
    )(grams, block)


def per_device(features, gate_pre, up_pre, hidden_grad, lengths, momentum):
    y, z, t = (lax.axis_index(name) for name in AXES)
    copies = gate_cotangent(y * NZ + z, lengths, gate_pre, up_pre, hidden_grad)

    held, halves, orders, first = features, None, ([0], [0]), None
    for masks in [m for m in ((2, 6), (6, 2), (1, 1)) if max(m) < NT]:
        arrived = lax.ppermute(held, AXES, tensor_pairs(masks))
        orders = tuple(orders[p] + [o ^ masks[p] for o in orders[p ^ (masks[p] & 1)]] for p in (0, 1))
        halves = (held, arrived)
        held = jnp.concatenate(halves, axis=0)
        first = arrived if first is None else first

    lines = functools.partial(
        lax.all_to_all, axis_name=AXES, split_axis=0, concat_axis=0, axis_index_groups=line_groups("y"), tiled=True
    )
    copies, _ = lax.optimization_barrier((copies, first))
    grads = lines(copies).reshape(-1, copies.shape[2])
    inputs = lines(arrange(t, orders, halves, features.shape[0]))
    partial_value = partial_product(inputs, grads)
    pieces = partial_value.reshape(NZ, BLK, partial_value.shape[1])
    received = lax.all_to_all(
        pieces, AXES, split_axis=0, concat_axis=0, axis_index_groups=line_groups("z"), tiled=True
    )
    new_moment, nesterov, grams = momentum_step(received, momentum)
    grams = lax.all_to_all(grams, "t", split_axis=0, concat_axis=0, tiled=True)
    by_y = polar_update(grams, nesterov)
    by_y = lax.all_to_all(by_y, "y", split_axis=0, concat_axis=0, tiled=True)
    unit_count = by_y.shape[2] // NZ
    by_z = by_y.reshape(NY, BLK, NZ, unit_count).transpose(2, 3, 0, 1)
    by_z = lax.all_to_all(by_z, "z", split_axis=0, concat_axis=0, tiled=True)
    result = by_z.transpose(1, 2, 0, 3).reshape(1, unit_count, NY * NZ * BLK)
    return result, new_moment


def solution(mesh):
    fine = Mesh(mesh.devices.reshape(NY, NZ, NT), AXES)
    split = P(("y", "z"), "t")
    return jax.shard_map(
        per_device,
        mesh=fine,
        in_specs=(split, split, split, split, P(), split),
        out_specs=(P("t", ("y", "z"), None), split),
        check_vma=False,
    )
```

```python
import functools
import math

import jax
import jax.numpy as jnp
from jax import lax
from jax.experimental import pallas as pl
from jax.experimental.pallas import tpu as pltpu
from jax.sharding import Mesh
from jax.sharding import PartitionSpec as P

HID = 7168
SEQ_LEN = 128
BLK = 64
ITERS = 5
NY = 8
NZ = 8
NT = 8

momentum_decay = 0.95
linear_coeff = 3.4445
cubic_coeff = -4.775
quintic_coeff = 2.0315
norm_epsilon = 1e-07
update_gain = 0.2

HIGHEST = lax.Precision.HIGHEST
AXES = ("y", "z", "t")


def gate_kernel(place_ref, lengths_ref, gate_in, up_in, cotangent_in, copies_ref, *scratch):
    buffers, arrived = scratch[:3], scratch[3]
    sources = (gate_in, up_in, cotangent_in)
    copies = [
        pltpu.make_async_copy(source, buffer, arrived.at[i])
        for i, (source, buffer) in enumerate(zip(sources, buffers))
    ]
    for copy in copies:
        copy.start()
    for copy in copies:
        copy.wait()
    gate_value, up_value, cotangent = (buffer[...].astype(jnp.float32) for buffer in buffers)
    sigmoid_gate = jax.nn.sigmoid(gate_value)
    gate_grad = cotangent * up_value * sigmoid_gate * (1.0 + gate_value * (1.0 - sigmoid_gate))
    position = lax.broadcasted_iota(jnp.int32, gate_value.shape, 0)
    trained = position < lengths_ref[place_ref[0]]
    gate_grad = jnp.where(trained, gate_grad, 0.0).astype(copies_ref.dtype)
    for part in range(copies_ref.shape[0]):
        copies_ref[part] = gate_grad


def gate_cotangent(place, lengths, gate_pre, up_pre, hidden_grad):
    tokens, columns = gate_pre.shape
    hbm = pl.BlockSpec(memory_space=pltpu.HBM)
    vmem = pl.BlockSpec(memory_space=pltpu.VMEM)
    smem = pl.BlockSpec(memory_space=pltpu.SMEM)
    arrays = (gate_pre, up_pre, hidden_grad)
    return pl.pallas_call(
        gate_kernel,
        out_shape=jax.ShapeDtypeStruct((NZ, tokens, columns), jnp.bfloat16),
        in_specs=[smem, smem] + [hbm] * 3,
        out_specs=vmem,
        scratch_shapes=[pltpu.VMEM(array.shape, array.dtype) for array in arrays]
        + [pltpu.SemaphoreType.DMA((3,))],
        compiler_params=pltpu.CompilerParams(vmem_limit_bytes=60 * 1024 * 1024),
        cost_estimate=pl.CostEstimate(
            flops=64 * tokens * columns, bytes_accessed=24 * tokens * columns, transcendentals=tokens * columns
        ),
        name="gate_cotangent",
    )(jnp.reshape(place, (1,)), lengths, *arrays)


def arrange_kernel(orders, t_ref, first_ref, second_ref, out_ref):
    tokens = out_ref.shape[2]
    t = t_ref[0]
    blocks = [(ref, start) for ref in (first_ref, second_ref) for start in range(0, ref.shape[0], tokens)]

    @pl.when(lax.rem(t, 2) == 0)
    def _():
        for offset, (ref, start) in zip(orders[0], blocks):
            out_ref[lax.bitwise_xor(t, offset)] = ref[start : start + tokens, :].T

    @pl.when(lax.rem(t, 2) == 1)
    def _():
        for offset, (ref, start) in zip(orders[1], blocks):
            turned = ref[start : start + tokens, :].T
            rows = pl.ds(pl.multiple_of(lax.bitwise_xor(t, offset) * BLK, BLK), BLK)
            for z in range(NZ):
                out_ref[z, rows, :] = turned[z * BLK : (z + 1) * BLK, :]


def arrange(t, orders, halves, tokens):
    rows = halves[0].shape[1]
    vmem = pl.BlockSpec(memory_space=pltpu.VMEM)
    return pl.pallas_call(
        functools.partial(arrange_kernel, orders),
        out_shape=jax.ShapeDtypeStruct((NZ, rows, tokens), jnp.bfloat16),
        in_specs=[pl.BlockSpec(memory_space=pltpu.SMEM), vmem, vmem],
        out_specs=vmem,
        compiler_params=pltpu.CompilerParams(vmem_limit_bytes=16 * 1024 * 1024),
        cost_estimate=pl.CostEstimate(
            flops=NZ * rows * tokens, bytes_accessed=4 * NZ * rows * tokens, transcendentals=0
        ),
        name="arrange",
    )(jnp.reshape(t, (1,)), *halves)


def device_number(y, z, t):
    return (y * NZ + z) * NT + t


def line_groups(even_axis):
    groups = []
    for t in range(NT):
        along_y = (t % 2 == 0) == (even_axis == "y")
        for fixed in range(NZ if along_y else NY):
            line = [(i, fixed) if along_y else (fixed, i) for i in range(NY if along_y else NZ)]
            groups.append([device_number(y, z, t) for y, z in line])
    return groups


def tensor_pairs(masks):
    return [
        (device_number(y, z, t), device_number(y, z, t ^ masks[t % 2]))
        for y in range(NY)
        for z in range(NZ)
        for t in range(NT)
    ]


def partial_kernel(pieces_ref, grads_ref, out_ref, features):
    rows = out_ref.shape[0]
    tokens = pieces_ref.shape[2]
    for group in range(pieces_ref.shape[0]):
        features[:, group * tokens : (group + 1) * tokens] = pieces_ref[group]
    step = 128
    for start in range(0, rows, step):
        product = jnp.dot(
            features[start : start + step, :], grads_ref[...], preferred_element_type=jnp.float32
        )
        out_ref[start : start + step, :] = product.astype(out_ref.dtype)


def partial_product(pieces, grads):
    tokens, columns = grads.shape
    rows = pieces.shape[1]
    vmem = pl.BlockSpec(memory_space=pltpu.VMEM)
    return pl.pallas_call(
        partial_kernel,
        out_shape=jax.ShapeDtypeStruct((rows, columns), jnp.bfloat16),
        in_specs=[vmem, vmem],
        out_specs=vmem,
        scratch_shapes=[pltpu.VMEM((rows, tokens), jnp.bfloat16)],
        compiler_params=pltpu.CompilerParams(vmem_limit_bytes=32 * 1024 * 1024),
        cost_estimate=pl.CostEstimate(
            flops=2 * tokens * rows * columns, bytes_accessed=6_000_000, transcendentals=0
        ),
        name="partial_product",
    )(pieces, grads)


def momentum_kernel(parts_ref, momentum_ref, moment_ref, nesterov_ref, grams_ref):
    grad = parts_ref[0].astype(jnp.float32)
    for part in range(1, parts_ref.shape[0]):
        grad = grad + parts_ref[part].astype(jnp.float32)
    new_moment = momentum_decay * momentum_ref[...] + grad
    moment_ref[...] = new_moment
    nesterov = grad + momentum_decay * new_moment
    nesterov_ref[...] = nesterov
    gram = lax.dot_general(
        nesterov, nesterov, (((1,), (1,)), ((), ())), precision=HIGHEST, preferred_element_type=jnp.float32
    )
    half = gram.shape[0] // 2
    packed = jnp.concatenate([gram[:half], gram[half:]], axis=1)
    for part in range(grams_ref.shape[0]):
        grams_ref[part] = packed


def momentum_step(parts, momentum):
    size, columns = momentum.shape
    vmem = pl.BlockSpec(memory_space=pltpu.VMEM)
    return pl.pallas_call(
        momentum_kernel,
        out_shape=(
            jax.ShapeDtypeStruct((size, columns), jnp.float32),
            jax.ShapeDtypeStruct((size, columns), jnp.float32),
            jax.ShapeDtypeStruct((NT, size // 2, 2 * size), jnp.float32),
        ),
        in_specs=[vmem, vmem],
        out_specs=(vmem, vmem, vmem),
        compiler_params=pltpu.CompilerParams(vmem_limit_bytes=16 * 1024 * 1024),
        cost_estimate=pl.CostEstimate(flops=60_000_000, bytes_accessed=1_700_000, transcendentals=0),
        name="momentum_step",
    )(parts, momentum)


def polar_kernel(grams_ref, block_ref, out_ref):
    mul = functools.partial(jnp.dot, precision=HIGHEST, preferred_element_type=jnp.float32)
    packed = grams_ref[0]
    for part in range(1, grams_ref.shape[0]):
        packed = packed + grams_ref[part]
    size = packed.shape[1] // 2
    total = jnp.concatenate([packed[:, :size], packed[:, size:]], axis=0)
    shape = (size, size)
    diagonal = lax.broadcasted_iota(jnp.int32, shape, 0) == lax.broadcasted_iota(jnp.int32, shape, 1)
    eye = jnp.where(diagonal, 1.0, 0.0).astype(jnp.float32)
    squares = jnp.sum(jnp.sum(total * eye, axis=1, keepdims=True), axis=0, keepdims=True)
    inverse = 1.0 / (jnp.sqrt(squares) + norm_epsilon)
    gram = total * inverse * inverse
    mapping = None
    for iteration in range(ITERS):
        square = mul(gram, gram)
        poly = linear_coeff * eye + cubic_coeff * gram + quintic_coeff * square
        mapping = poly if iteration == 0 else mul(poly, mapping)
        if iteration < ITERS - 1:
            gram = mul(mul(poly, gram), poly)
    mapping = mapping * (inverse * (update_gain * math.sqrt(HID)))
    units = out_ref.shape[2]
    rows = mul(mapping, block_ref[...]).astype(out_ref.dtype)
    for part in range(out_ref.shape[0]):
        out_ref[part] = rows[:, part * units : (part + 1) * units]


def polar_update(grams, block):
    size, columns = block.shape
    vmem = pl.BlockSpec(memory_space=pltpu.VMEM)
    return pl.pallas_call(
        polar_kernel,
        out_shape=jax.ShapeDtypeStruct((NY, size, columns // NY), jnp.bfloat16),
        in_specs=[vmem, vmem],
        out_specs=vmem,
        compiler_params=pltpu.CompilerParams(vmem_limit_bytes=16 * 1024 * 1024),
        cost_estimate=pl.CostEstimate(flops=100_000_000, bytes_accessed=600_000, transcendentals=0),
        name="polar_update",
    )(grams, block)


def per_device(features, gate_pre, up_pre, hidden_grad, lengths, momentum):
    y, z, t = (lax.axis_index(name) for name in AXES)
    copies = gate_cotangent(y * NZ + z, lengths, gate_pre, up_pre, hidden_grad)

    held, halves, orders = features, None, ([0], [0])
    for masks in [m for m in ((2, 6), (6, 2), (1, 1)) if max(m) < NT]:
        arrived = lax.ppermute(held, AXES, tensor_pairs(masks))
        if halves is None:
            arrived, copies = lax.optimization_barrier((arrived, copies))
        orders = tuple(orders[p] + [o ^ masks[p] for o in orders[p ^ (masks[p] & 1)]] for p in (0, 1))
        halves = (held, arrived)
        held = jnp.concatenate(halves, axis=0)

    lines = functools.partial(
        lax.all_to_all, axis_name=AXES, split_axis=0, concat_axis=0, axis_index_groups=line_groups("y"), tiled=True
    )
    grads = lines(copies).reshape(-1, copies.shape[2])
    inputs = lines(arrange(t, orders, halves, features.shape[0]))
    partial_value = partial_product(inputs, grads)
    pieces = partial_value.reshape(NZ, BLK, partial_value.shape[1])
    received = lax.all_to_all(
        pieces, AXES, split_axis=0, concat_axis=0, axis_index_groups=line_groups("z"), tiled=True
    )
    new_moment, nesterov, grams = momentum_step(received, momentum)
    grams = lax.all_to_all(grams, "t", split_axis=0, concat_axis=0, tiled=True)
    by_y = polar_update(grams, nesterov)
    by_y = lax.all_to_all(by_y, "y", split_axis=0, concat_axis=0, tiled=True)
    unit_count = by_y.shape[2] // NZ
    by_z = by_y.reshape(NY, BLK, NZ, unit_count).transpose(2, 3, 0, 1)
    by_z = lax.all_to_all(by_z, "z", split_axis=0, concat_axis=0, tiled=True)
    result = by_z.transpose(1, 2, 0, 3).reshape(1, unit_count, NY * NZ * BLK)
    return result, new_moment


def solution(mesh):
    fine = Mesh(mesh.devices.reshape(NY, NZ, NT), AXES)
    split = P(("y", "z"), "t")
    return jax.shard_map(
        per_device,
        mesh=fine,
        in_specs=(split, split, split, split, P(), split),
        out_specs=(P("t", ("y", "z"), None), split),
        check_vma=False,
    )
```

```python
import functools
import math

import jax
import jax.numpy as jnp
from jax import lax
from jax.experimental import pallas as pl
from jax.experimental.pallas import tpu as pltpu
from jax.sharding import Mesh
from jax.sharding import PartitionSpec as P

HID = 7168
SEQ_LEN = 128
BLK = 64
ITERS = 5
NY = 8
NZ = 8
NT = 8

momentum_decay = 0.95
linear_coeff = 3.4445
cubic_coeff = -4.775
quintic_coeff = 2.0315
norm_epsilon = 1e-07
update_gain = 0.2

HIGHEST = lax.Precision.HIGHEST
AXES = ("y", "z", "t")


def gate_kernel(place_ref, lengths_ref, gate_in, up_in, cotangent_in, copies_ref, *scratch):
    buffers, arrived = scratch[:3], scratch[3]
    sources = (gate_in, up_in, cotangent_in)
    copies = [
        pltpu.make_async_copy(source, buffer, arrived.at[i])
        for i, (source, buffer) in enumerate(zip(sources, buffers))
    ]
    for copy in copies:
        copy.start()
    for copy in copies:
        copy.wait()
    gate_value, up_value, cotangent = (buffer[...].astype(jnp.float32) for buffer in buffers)
    sigmoid_gate = jax.nn.sigmoid(gate_value)
    gate_grad = cotangent * up_value * sigmoid_gate * (1.0 + gate_value * (1.0 - sigmoid_gate))
    position = lax.broadcasted_iota(jnp.int32, gate_value.shape, 0)
    trained = position < lengths_ref[place_ref[0]]
    gate_grad = jnp.where(trained, gate_grad, 0.0).astype(copies_ref.dtype)
    for part in range(copies_ref.shape[0]):
        copies_ref[part] = gate_grad


def gate_cotangent(place, lengths, gate_pre, up_pre, hidden_grad):
    tokens, columns = gate_pre.shape
    hbm = pl.BlockSpec(memory_space=pltpu.HBM)
    vmem = pl.BlockSpec(memory_space=pltpu.VMEM)
    smem = pl.BlockSpec(memory_space=pltpu.SMEM)
    arrays = (gate_pre, up_pre, hidden_grad)
    return pl.pallas_call(
        gate_kernel,
        out_shape=jax.ShapeDtypeStruct((NZ, tokens, columns), jnp.bfloat16),
        in_specs=[smem, smem] + [hbm] * 3,
        out_specs=vmem,
        scratch_shapes=[pltpu.VMEM(array.shape, array.dtype) for array in arrays]
        + [pltpu.SemaphoreType.DMA((3,))],
        compiler_params=pltpu.CompilerParams(vmem_limit_bytes=60 * 1024 * 1024),
        cost_estimate=pl.CostEstimate(
            flops=64 * tokens * columns, bytes_accessed=400 * tokens * columns, transcendentals=tokens * columns
        ),
        name="gate_cotangent",
    )(jnp.reshape(place, (1,)), lengths, *arrays)


def turn_first_kernel(value_in, turned_ref, buffer, arrived):
    copy = pltpu.make_async_copy(value_in, buffer, arrived)
    copy.start()
    copy.wait()
    turned_ref[...] = buffer[...].T


def turn_first(value):
    rows, columns = value.shape
    return pl.pallas_call(
        turn_first_kernel,
        out_shape=jax.ShapeDtypeStruct((columns, rows), value.dtype),
        in_specs=[pl.BlockSpec(memory_space=pltpu.HBM)],
        out_specs=pl.BlockSpec(memory_space=pltpu.VMEM),
        scratch_shapes=[pltpu.VMEM(value.shape, value.dtype), pltpu.SemaphoreType.DMA],
        compiler_params=pltpu.CompilerParams(vmem_limit_bytes=60 * 1024 * 1024),
        cost_estimate=pl.CostEstimate(flops=rows * columns, bytes_accessed=4 * rows * columns, transcendentals=0),
        name="turn_first",
    )(value)


def turn_kernel(value_ref, turned_ref):
    turned_ref[...] = value_ref[...].T


def turn(value):
    rows, columns = value.shape
    vmem = pl.BlockSpec(memory_space=pltpu.VMEM)
    return pl.pallas_call(
        turn_kernel,
        out_shape=jax.ShapeDtypeStruct((columns, rows), value.dtype),
        in_specs=[vmem],
        out_specs=vmem,
        compiler_params=pltpu.CompilerParams(vmem_limit_bytes=8 * 1024 * 1024),
        cost_estimate=pl.CostEstimate(flops=rows * columns, bytes_accessed=4 * rows * columns, transcendentals=0),
        name="turn",
    )(value)


def device_number(y, z, t):
    return (y * NZ + z) * NT + t


def line_groups(even_axis):
    groups = []
    for t in range(NT):
        along_y = (t % 2 == 0) == (even_axis == "y")
        for fixed in range(NZ if along_y else NY):
            line = [(i, fixed) if along_y else (fixed, i) for i in range(NY if along_y else NZ)]
            groups.append([device_number(y, z, t) for y, z in line])
    return groups


def tensor_pairs(masks):
    return [
        (device_number(y, z, t), device_number(y, z, t ^ masks[t % 2]))
        for y in range(NY)
        for z in range(NZ)
        for t in range(NT)
    ]


def partial_kernel(orders, t_ref, first_ref, second_ref, grads_ref, out_ref, features):
    rows = out_ref.shape[0]
    tokens = first_ref.shape[1]
    t = t_ref[0]
    blocks = [(ref, start) for ref in (first_ref, second_ref) for start in range(0, ref.shape[0], rows)]

    @pl.when(lax.rem(t, 2) == 0)
    def _():
        for offset, (ref, start) in zip(orders[0], blocks):
            group = lax.bitwise_xor(t, offset)
            features[:, pl.ds(pl.multiple_of(group * tokens, tokens), tokens)] = ref[start : start + rows, :]

    @pl.when(lax.rem(t, 2) == 1)
    def _():
        for offset, (ref, start) in zip(orders[1], blocks):
            block_rows = pl.ds(pl.multiple_of(lax.bitwise_xor(t, offset) * BLK, BLK), BLK)
            for z in range(NZ):
                features[block_rows, z * tokens : (z + 1) * tokens] = ref[
                    start + z * BLK : start + (z + 1) * BLK, :
                ]

    step = 128
    for start in range(0, rows, step):
        product = jnp.dot(
            features[start : start + step, :], grads_ref[...], preferred_element_type=jnp.float32
        )
        out_ref[start : start + step, :] = product.astype(out_ref.dtype)


def partial_product(t, orders, feature_halves, grads):
    tokens, columns = grads.shape
    rows = NZ * BLK
    vmem = pl.BlockSpec(memory_space=pltpu.VMEM)
    return pl.pallas_call(
        functools.partial(partial_kernel, orders),
        out_shape=jax.ShapeDtypeStruct((rows, columns), jnp.bfloat16),
        in_specs=[pl.BlockSpec(memory_space=pltpu.SMEM), vmem, vmem, vmem],
        out_specs=vmem,
        scratch_shapes=[pltpu.VMEM((rows, tokens), jnp.bfloat16)],
        compiler_params=pltpu.CompilerParams(vmem_limit_bytes=32 * 1024 * 1024),
        cost_estimate=pl.CostEstimate(
            flops=2 * tokens * rows * columns, bytes_accessed=6_000_000, transcendentals=0
        ),
        name="partial_product",
    )(jnp.reshape(t, (1,)), *feature_halves, grads)


def momentum_kernel(parts_ref, momentum_ref, moment_ref, nesterov_ref, grams_ref):
    grad = parts_ref[0].astype(jnp.float32)
    for part in range(1, parts_ref.shape[0]):
        grad = grad + parts_ref[part].astype(jnp.float32)
    new_moment = momentum_decay * momentum_ref[...] + grad
    moment_ref[...] = new_moment
    nesterov = grad + momentum_decay * new_moment
    nesterov_ref[...] = nesterov
    gram = lax.dot_general(
        nesterov, nesterov, (((1,), (1,)), ((), ())), precision=HIGHEST, preferred_element_type=jnp.float32
    )
    half = gram.shape[0] // 2
    packed = jnp.concatenate([gram[:half], gram[half:]], axis=1)
    for part in range(grams_ref.shape[0]):
        grams_ref[part] = packed


def momentum_step(parts, momentum):
    size, columns = momentum.shape
    vmem = pl.BlockSpec(memory_space=pltpu.VMEM)
    return pl.pallas_call(
        momentum_kernel,
        out_shape=(
            jax.ShapeDtypeStruct((size, columns), jnp.float32),
            jax.ShapeDtypeStruct((size, columns), jnp.float32),
            jax.ShapeDtypeStruct((NT, size // 2, 2 * size), jnp.float32),
        ),
        in_specs=[vmem, vmem],
        out_specs=(vmem, vmem, vmem),
        compiler_params=pltpu.CompilerParams(vmem_limit_bytes=16 * 1024 * 1024),
        cost_estimate=pl.CostEstimate(flops=60_000_000, bytes_accessed=1_700_000, transcendentals=0),
        name="momentum_step",
    )(parts, momentum)


def polar_kernel(grams_ref, block_ref, out_ref):
    mul = functools.partial(jnp.dot, precision=HIGHEST, preferred_element_type=jnp.float32)
    packed = grams_ref[0]
    for part in range(1, grams_ref.shape[0]):
        packed = packed + grams_ref[part]
    size = packed.shape[1] // 2
    total = jnp.concatenate([packed[:, :size], packed[:, size:]], axis=0)
    shape = (size, size)
    diagonal = lax.broadcasted_iota(jnp.int32, shape, 0) == lax.broadcasted_iota(jnp.int32, shape, 1)
    eye = jnp.where(diagonal, 1.0, 0.0).astype(jnp.float32)
    squares = jnp.sum(jnp.sum(total * eye, axis=1, keepdims=True), axis=0, keepdims=True)
    inverse = 1.0 / (jnp.sqrt(squares) + norm_epsilon)
    gram = total * inverse * inverse
    mapping = None
    for iteration in range(ITERS):
        square = mul(gram, gram)
        poly = linear_coeff * eye + cubic_coeff * gram + quintic_coeff * square
        mapping = poly if iteration == 0 else mul(poly, mapping)
        if iteration < ITERS - 1:
            gram = mul(mul(poly, gram), poly)
    mapping = mapping * (inverse * (update_gain * math.sqrt(HID)))
    units = out_ref.shape[2]
    rows = mul(mapping, block_ref[...]).astype(out_ref.dtype)
    for part in range(out_ref.shape[0]):
        out_ref[part] = rows[:, part * units : (part + 1) * units]


def polar_update(grams, block):
    size, columns = block.shape
    vmem = pl.BlockSpec(memory_space=pltpu.VMEM)
    return pl.pallas_call(
        polar_kernel,
        out_shape=jax.ShapeDtypeStruct((NY, size, columns // NY), jnp.bfloat16),
        in_specs=[vmem, vmem],
        out_specs=vmem,
        compiler_params=pltpu.CompilerParams(vmem_limit_bytes=16 * 1024 * 1024),
        cost_estimate=pl.CostEstimate(flops=100_000_000, bytes_accessed=600_000, transcendentals=0),
        name="polar_update",
    )(grams, block)


def per_device(features, gate_pre, up_pre, hidden_grad, lengths, momentum):
    y, z, t = (lax.axis_index(name) for name in AXES)
    swap = [(a * NT + b, b * NT + a) for a in range(NY) for b in range(NT)]
    swapped = lax.ppermute(features, ("y", "t"), swap)
    turned = turn_first(features)
    lengths, swapped = lax.optimization_barrier((lengths, swapped))
    copies = gate_cotangent(y * NZ + z, lengths, gate_pre, up_pre, hidden_grad)

    by_blocks = lax.all_to_all(
        turned.reshape(NZ, BLK, turned.shape[1]), "z", split_axis=0, concat_axis=0, tiled=True
    ).reshape(turned.shape)
    copies, by_blocks = lax.optimization_barrier((copies, by_blocks))
    grads = lax.all_to_all(
        copies, AXES, split_axis=0, concat_axis=0, axis_index_groups=line_groups("y"), tiled=True
    ).reshape(-1, copies.shape[2])
    by_tokens = turn(swapped)
    even = lax.rem(t, 2) == 0
    kept = jnp.where(even, by_tokens, by_blocks)
    given = jnp.where(even, by_blocks, by_tokens)
    orders, halves = ([0], [0]), None
    for masks in [m for m in ((1, 1), (2, 6), (6, 2)) if max(m) < NT]:
        arrived = lax.ppermute(given if halves is None else kept, AXES, tensor_pairs(masks))
        orders = tuple(order + [o ^ mask for o in order] for order, mask in zip(orders, masks))
        halves = (kept, arrived)
        kept = jnp.concatenate(halves, axis=0)

    partial_value = partial_product(t, orders, halves, grads)
    pieces = partial_value.reshape(NZ, BLK, partial_value.shape[1])
    received = lax.all_to_all(
        pieces, AXES, split_axis=0, concat_axis=0, axis_index_groups=line_groups("z"), tiled=True
    )
    new_moment, nesterov, grams = momentum_step(received, momentum)
    grams = lax.all_to_all(grams, "t", split_axis=0, concat_axis=0, tiled=True)
    by_y = polar_update(grams, nesterov)
    by_y = lax.all_to_all(by_y, "y", split_axis=0, concat_axis=0, tiled=True)
    unit_count = by_y.shape[2] // NZ
    by_z = by_y.reshape(NY, BLK, NZ, unit_count).transpose(2, 3, 0, 1)
    by_z = lax.all_to_all(by_z, "z", split_axis=0, concat_axis=0, tiled=True)
    result = by_z.transpose(1, 2, 0, 3).reshape(1, unit_count, NY * NZ * BLK)
    return result, new_moment


def solution(mesh):
    fine = Mesh(mesh.devices.reshape(NY, NZ, NT), AXES)
    split = P(("y", "z"), "t")
    return jax.shard_map(
        per_device,
        mesh=fine,
        in_specs=(split, split, split, split, P(), split),
        out_specs=(P("t", ("y", "z"), None), split),
        check_vma=False,
    )
```

```python
import functools
import math

import jax
import jax.numpy as jnp
from jax import lax
from jax.experimental import pallas as pl
from jax.experimental.pallas import tpu as pltpu
from jax.sharding import Mesh
from jax.sharding import PartitionSpec as P

HID = 7168
SEQ_LEN = 128
BLK = 64
ITERS = 5
NY = 8
NZ = 8
NT = 8

momentum_decay = 0.95
linear_coeff = 3.4445
cubic_coeff = -4.775
quintic_coeff = 2.0315
norm_epsilon = 1e-07
update_gain = 0.2

HIGHEST = lax.Precision.HIGHEST
AXES = ("y", "z", "t")


def gate_kernel(place_ref, lengths_ref, gate_in, up_in, cotangent_in, copies_ref, *scratch):
    buffers, arrived = scratch[:3], scratch[3]
    sources = (gate_in, up_in, cotangent_in)
    copies = [
        pltpu.make_async_copy(source, buffer, arrived.at[i])
        for i, (source, buffer) in enumerate(zip(sources, buffers))
    ]
    for copy in copies:
        copy.start()
    for copy in copies:
        copy.wait()
    gate_value, up_value, cotangent = (buffer[...].astype(jnp.float32) for buffer in buffers)
    sigmoid_gate = jax.nn.sigmoid(gate_value)
    gate_grad = cotangent * up_value * sigmoid_gate * (1.0 + gate_value * (1.0 - sigmoid_gate))
    position = lax.broadcasted_iota(jnp.int32, gate_value.shape, 0)
    trained = position < lengths_ref[place_ref[0]]
    gate_grad = jnp.where(trained, gate_grad, 0.0).astype(copies_ref.dtype)
    for part in range(copies_ref.shape[0]):
        copies_ref[part] = gate_grad


def gate_cotangent(place, lengths, gate_pre, up_pre, hidden_grad):
    tokens, columns = gate_pre.shape
    hbm = pl.BlockSpec(memory_space=pltpu.HBM)
    vmem = pl.BlockSpec(memory_space=pltpu.VMEM)
    smem = pl.BlockSpec(memory_space=pltpu.SMEM)
    arrays = (gate_pre, up_pre, hidden_grad)
    return pl.pallas_call(
        gate_kernel,
        out_shape=jax.ShapeDtypeStruct((NZ, tokens, columns), jnp.bfloat16),
        in_specs=[smem, smem] + [hbm] * 3,
        out_specs=vmem,
        scratch_shapes=[pltpu.VMEM(array.shape, array.dtype) for array in arrays]
        + [pltpu.SemaphoreType.DMA((3,))],
        compiler_params=pltpu.CompilerParams(vmem_limit_bytes=60 * 1024 * 1024),
        cost_estimate=pl.CostEstimate(
            flops=64 * tokens * columns, bytes_accessed=400 * tokens * columns, transcendentals=tokens * columns
        ),
        name="gate_cotangent",
    )(jnp.reshape(place, (1,)), lengths, *arrays)


def turn_kernel(value_ref, turned_ref):
    turned_ref[...] = value_ref[...].T


def turn(value):
    rows, columns = value.shape
    vmem = pl.BlockSpec(memory_space=pltpu.VMEM)
    return pl.pallas_call(
        turn_kernel,
        out_shape=jax.ShapeDtypeStruct((columns, rows), value.dtype),
        in_specs=[vmem],
        out_specs=vmem,
        compiler_params=pltpu.CompilerParams(vmem_limit_bytes=8 * 1024 * 1024),
        cost_estimate=pl.CostEstimate(flops=rows * columns, bytes_accessed=4 * rows * columns, transcendentals=0),
        name="turn",
    )(value)


def device_number(y, z, t):
    return (y * NZ + z) * NT + t


def line_groups(even_axis):
    groups = []
    for t in range(NT):
        along_y = (t % 2 == 0) == (even_axis == "y")
        for fixed in range(NZ if along_y else NY):
            line = [(i, fixed) if along_y else (fixed, i) for i in range(NY if along_y else NZ)]
            groups.append([device_number(y, z, t) for y, z in line])
    return groups


def tensor_pairs(masks):
    return [
        (device_number(y, z, t), device_number(y, z, t ^ masks[t % 2]))
        for y in range(NY)
        for z in range(NZ)
        for t in range(NT)
    ]


def partial_kernel(orders, t_ref, first_ref, second_ref, grads_ref, out_ref, features):
    rows = out_ref.shape[0]
    tokens = first_ref.shape[1]
    t = t_ref[0]
    blocks = [(ref, start) for ref in (first_ref, second_ref) for start in range(0, ref.shape[0], rows)]

    @pl.when(lax.rem(t, 2) == 0)
    def _():
        for offset, (ref, start) in zip(orders[0], blocks):
            group = lax.bitwise_xor(t, offset)
            features[:, pl.ds(pl.multiple_of(group * tokens, tokens), tokens)] = ref[start : start + rows, :]

    @pl.when(lax.rem(t, 2) == 1)
    def _():
        for offset, (ref, start) in zip(orders[1], blocks):
            block_rows = pl.ds(pl.multiple_of(lax.bitwise_xor(t, offset) * BLK, BLK), BLK)
            for z in range(NZ):
                features[block_rows, z * tokens : (z + 1) * tokens] = ref[
                    start + z * BLK : start + (z + 1) * BLK, :
                ]

    step = 128
    for start in range(0, rows, step):
        product = jnp.dot(
            features[start : start + step, :], grads_ref[...], preferred_element_type=jnp.float32
        )
        out_ref[start : start + step, :] = product.astype(out_ref.dtype)


def partial_product(t, orders, feature_halves, grads):
    tokens, columns = grads.shape
    rows = NZ * BLK
    vmem = pl.BlockSpec(memory_space=pltpu.VMEM)
    return pl.pallas_call(
        functools.partial(partial_kernel, orders),
        out_shape=jax.ShapeDtypeStruct((rows, columns), jnp.bfloat16),
        in_specs=[pl.BlockSpec(memory_space=pltpu.SMEM), vmem, vmem, vmem],
        out_specs=vmem,
        scratch_shapes=[pltpu.VMEM((rows, tokens), jnp.bfloat16)],
        compiler_params=pltpu.CompilerParams(vmem_limit_bytes=32 * 1024 * 1024),
        cost_estimate=pl.CostEstimate(
            flops=2 * tokens * rows * columns, bytes_accessed=6_000_000, transcendentals=0
        ),
        name="partial_product",
    )(jnp.reshape(t, (1,)), *feature_halves, grads)


def momentum_kernel(parts_ref, momentum_ref, moment_ref, nesterov_ref, grams_ref):
    grad = parts_ref[0].astype(jnp.float32)
    for part in range(1, parts_ref.shape[0]):
        grad = grad + parts_ref[part].astype(jnp.float32)
    new_moment = momentum_decay * momentum_ref[...] + grad
    moment_ref[...] = new_moment
    nesterov = grad + momentum_decay * new_moment
    nesterov_ref[...] = nesterov
    gram = lax.dot_general(
        nesterov, nesterov, (((1,), (1,)), ((), ())), precision=HIGHEST, preferred_element_type=jnp.float32
    )
    half = gram.shape[0] // 2
    packed = jnp.concatenate([gram[:half], gram[half:]], axis=1)
    for part in range(grams_ref.shape[0]):
        grams_ref[part] = packed


def momentum_step(parts, momentum):
    size, columns = momentum.shape
    vmem = pl.BlockSpec(memory_space=pltpu.VMEM)
    return pl.pallas_call(
        momentum_kernel,
        out_shape=(
            jax.ShapeDtypeStruct((size, columns), jnp.float32),
            jax.ShapeDtypeStruct((size, columns), jnp.float32),
            jax.ShapeDtypeStruct((NT, size // 2, 2 * size), jnp.float32),
        ),
        in_specs=[vmem, vmem],
        out_specs=(vmem, vmem, vmem),
        compiler_params=pltpu.CompilerParams(vmem_limit_bytes=16 * 1024 * 1024),
        cost_estimate=pl.CostEstimate(flops=60_000_000, bytes_accessed=1_700_000, transcendentals=0),
        name="momentum_step",
    )(parts, momentum)


def polar_kernel(grams_ref, block_ref, out_ref):
    mul = functools.partial(jnp.dot, precision=HIGHEST, preferred_element_type=jnp.float32)
    packed = grams_ref[0]
    for part in range(1, grams_ref.shape[0]):
        packed = packed + grams_ref[part]
    size = packed.shape[1] // 2
    total = jnp.concatenate([packed[:, :size], packed[:, size:]], axis=0)
    shape = (size, size)
    diagonal = lax.broadcasted_iota(jnp.int32, shape, 0) == lax.broadcasted_iota(jnp.int32, shape, 1)
    eye = jnp.where(diagonal, 1.0, 0.0).astype(jnp.float32)
    squares = jnp.sum(jnp.sum(total * eye, axis=1, keepdims=True), axis=0, keepdims=True)
    inverse = 1.0 / (jnp.sqrt(squares) + norm_epsilon)
    gram = total * inverse * inverse
    mapping = None
    for iteration in range(ITERS):
        square = mul(gram, gram)
        poly = linear_coeff * eye + cubic_coeff * gram + quintic_coeff * square
        if iteration < ITERS - 1:
            mapping = poly if iteration == 0 else mul(poly, mapping)
            gram = mul(mul(poly, gram), poly)
    scaled = mul(mapping * (inverse * (update_gain * math.sqrt(HID))), block_ref[...])
    units = out_ref.shape[2]
    rows = mul(poly, scaled).astype(out_ref.dtype)
    for part in range(out_ref.shape[0]):
        out_ref[part] = rows[:, part * units : (part + 1) * units]


def polar_update(grams, block):
    size, columns = block.shape
    vmem = pl.BlockSpec(memory_space=pltpu.VMEM)
    return pl.pallas_call(
        polar_kernel,
        out_shape=jax.ShapeDtypeStruct((NY, size, columns // NY), jnp.bfloat16),
        in_specs=[vmem, vmem],
        out_specs=vmem,
        compiler_params=pltpu.CompilerParams(vmem_limit_bytes=16 * 1024 * 1024),
        cost_estimate=pl.CostEstimate(flops=100_000_000, bytes_accessed=600_000, transcendentals=0),
        name="polar_update",
    )(grams, block)


def per_device(features, gate_pre, up_pre, hidden_grad, lengths, momentum):
    y, z, t = (lax.axis_index(name) for name in AXES)
    swap = [(a * NT + b, b * NT + a) for a in range(NY) for b in range(NT)]
    swapped = lax.ppermute(features, ("y", "t"), swap)
    turned = turn(features)
    copies = gate_cotangent(y * NZ + z, lengths, gate_pre, up_pre, hidden_grad)

    by_blocks = lax.all_to_all(
        turned.reshape(NZ, BLK, turned.shape[1]), "z", split_axis=0, concat_axis=0, tiled=True
    ).reshape(turned.shape)
    copies, swapped, by_blocks = lax.optimization_barrier((copies, swapped, by_blocks))
    grads = lax.all_to_all(
        copies, AXES, split_axis=0, concat_axis=0, axis_index_groups=line_groups("y"), tiled=True
    ).reshape(-1, copies.shape[2])
    by_tokens = turn(swapped)
    even = lax.rem(t, 2) == 0
    kept = jnp.where(even, by_tokens, by_blocks)
    given = jnp.where(even, by_blocks, by_tokens)
    orders, halves = ([0], [0]), None
    for masks in [m for m in ((1, 1), (2, 6), (6, 2)) if max(m) < NT]:
        arrived = lax.ppermute(given if halves is None else kept, AXES, tensor_pairs(masks))
        orders = tuple(order + [o ^ mask for o in order] for order, mask in zip(orders, masks))
        halves = (kept, arrived)
        kept = jnp.concatenate(halves, axis=0)

    partial_value = partial_product(t, orders, halves, grads)
    pieces = partial_value.reshape(NZ, BLK, partial_value.shape[1])
    received = lax.all_to_all(
        pieces, AXES, split_axis=0, concat_axis=0, axis_index_groups=line_groups("z"), tiled=True
    )
    new_moment, nesterov, grams = momentum_step(received, momentum)
    grams = lax.all_to_all(grams, "t", split_axis=0, concat_axis=0, tiled=True)
    by_y = polar_update(grams, nesterov)
    by_y = lax.all_to_all(by_y, "y", split_axis=0, concat_axis=0, tiled=True)
    unit_count = by_y.shape[2] // NZ
    by_z = by_y.reshape(NY, BLK, NZ, unit_count).transpose(2, 3, 0, 1)
    by_z = lax.all_to_all(by_z, "z", split_axis=0, concat_axis=0, tiled=True)
    result = by_z.transpose(1, 2, 0, 3).reshape(1, unit_count, NY * NZ * BLK)
    return result, new_moment


def solution(mesh):
    fine = Mesh(mesh.devices.reshape(NY, NZ, NT), AXES)
    split = P(("y", "z"), "t")
    return jax.shard_map(
        per_device,
        mesh=fine,
        in_specs=(split, split, split, split, P(), split),
        out_specs=(P("t", ("y", "z"), None), split),
        check_vma=False,
    )
```

```python
import functools
import math

import jax
import jax.numpy as jnp
from jax import lax
from jax.experimental import pallas as pl
from jax.experimental.pallas import tpu as pltpu
from jax.sharding import Mesh
from jax.sharding import PartitionSpec as P

HID = 7168
SEQ_LEN = 128
BLK = 64
ITERS = 5
NY = 8
NZ = 8
NT = 8

momentum_decay = 0.95
linear_coeff = 3.4445
cubic_coeff = -4.775
quintic_coeff = 2.0315
norm_epsilon = 1e-07
update_gain = 0.2

HIGHEST = lax.Precision.HIGHEST
AXES = ("y", "z", "t")


def gate_kernel(place_ref, lengths_ref, gate_in, up_in, cotangent_in, copies_ref, *scratch):
    buffers, arrived = scratch[:3], scratch[3]
    sources = (gate_in, up_in, cotangent_in)
    copies = [
        pltpu.make_async_copy(source, buffer, arrived.at[i])
        for i, (source, buffer) in enumerate(zip(sources, buffers))
    ]
    for copy in copies:
        copy.start()
    for copy in copies:
        copy.wait()
    gate_value, up_value, cotangent = (buffer[...].astype(jnp.float32) for buffer in buffers)
    sigmoid_gate = jax.nn.sigmoid(gate_value)
    gate_grad = cotangent * up_value * sigmoid_gate * (1.0 + gate_value * (1.0 - sigmoid_gate))
    position = lax.broadcasted_iota(jnp.int32, gate_value.shape, 0)
    trained = position < lengths_ref[place_ref[0]]
    gate_grad = jnp.where(trained, gate_grad, 0.0).astype(copies_ref.dtype)
    for part in range(copies_ref.shape[0]):
        copies_ref[part] = gate_grad


def gate_cotangent(place, lengths, gate_pre, up_pre, hidden_grad):
    tokens, columns = gate_pre.shape
    hbm = pl.BlockSpec(memory_space=pltpu.HBM)
    vmem = pl.BlockSpec(memory_space=pltpu.VMEM)
    smem = pl.BlockSpec(memory_space=pltpu.SMEM)
    arrays = (gate_pre, up_pre, hidden_grad)
    return pl.pallas_call(
        gate_kernel,
        out_shape=jax.ShapeDtypeStruct((NZ, tokens, columns), jnp.bfloat16),
        in_specs=[smem, smem] + [hbm] * 3,
        out_specs=vmem,
        scratch_shapes=[pltpu.VMEM(array.shape, array.dtype) for array in arrays]
        + [pltpu.SemaphoreType.DMA((3,))],
        compiler_params=pltpu.CompilerParams(vmem_limit_bytes=60 * 1024 * 1024),
        cost_estimate=pl.CostEstimate(
            flops=64 * tokens * columns, bytes_accessed=400 * tokens * columns, transcendentals=tokens * columns
        ),
        name="gate_cotangent",
    )(jnp.reshape(place, (1,)), lengths, *arrays)


def turn_kernel(value_ref, turned_ref):
    turned_ref[...] = value_ref[...].T


def turn(value):
    rows, columns = value.shape
    vmem = pl.BlockSpec(memory_space=pltpu.VMEM)
    return pl.pallas_call(
        turn_kernel,
        out_shape=jax.ShapeDtypeStruct((columns, rows), value.dtype),
        in_specs=[vmem],
        out_specs=vmem,
        compiler_params=pltpu.CompilerParams(vmem_limit_bytes=8 * 1024 * 1024),
        cost_estimate=pl.CostEstimate(flops=rows * columns, bytes_accessed=4 * rows * columns, transcendentals=0),
        name="turn",
    )(value)


def device_number(y, z, t):
    return (y * NZ + z) * NT + t


def line_groups(even_axis):
    groups = []
    for t in range(NT):
        along_y = (t % 2 == 0) == (even_axis == "y")
        for fixed in range(NZ if along_y else NY):
            line = [(i, fixed) if along_y else (fixed, i) for i in range(NY if along_y else NZ)]
            groups.append([device_number(y, z, t) for y, z in line])
    return groups


def tensor_pairs(masks):
    return [
        (device_number(y, z, t), device_number(y, z, t ^ masks[t % 2]))
        for y in range(NY)
        for z in range(NZ)
        for t in range(NT)
    ]


def partial_kernel(orders, t_ref, first_ref, second_ref, grads_ref, out_ref, features):
    rows = out_ref.shape[0]
    tokens = first_ref.shape[1]
    t = t_ref[0]
    blocks = [(ref, start) for ref in (first_ref, second_ref) for start in range(0, ref.shape[0], rows)]

    @pl.when(lax.rem(t, 2) == 0)
    def _():
        for offset, (ref, start) in zip(orders[0], blocks):
            group = lax.bitwise_xor(t, offset)
            features[:, pl.ds(pl.multiple_of(group * tokens, tokens), tokens)] = ref[start : start + rows, :]

    @pl.when(lax.rem(t, 2) == 1)
    def _():
        for offset, (ref, start) in zip(orders[1], blocks):
            block_rows = pl.ds(pl.multiple_of(lax.bitwise_xor(t, offset) * BLK, BLK), BLK)
            for z in range(NZ):
                features[block_rows, z * tokens : (z + 1) * tokens] = ref[
                    start + z * BLK : start + (z + 1) * BLK, :
                ]

    step = 128
    for start in range(0, rows, step):
        product = jnp.dot(
            features[start : start + step, :], grads_ref[...], preferred_element_type=jnp.float32
        )
        out_ref[start : start + step, :] = product.astype(out_ref.dtype)


def partial_product(t, orders, feature_halves, grads):
    tokens, columns = grads.shape
    rows = NZ * BLK
    vmem = pl.BlockSpec(memory_space=pltpu.VMEM)
    return pl.pallas_call(
        functools.partial(partial_kernel, orders),
        out_shape=jax.ShapeDtypeStruct((rows, columns), jnp.bfloat16),
        in_specs=[pl.BlockSpec(memory_space=pltpu.SMEM), vmem, vmem, vmem],
        out_specs=vmem,
        scratch_shapes=[pltpu.VMEM((rows, tokens), jnp.bfloat16)],
        compiler_params=pltpu.CompilerParams(vmem_limit_bytes=32 * 1024 * 1024),
        cost_estimate=pl.CostEstimate(
            flops=2 * tokens * rows * columns, bytes_accessed=6_000_000, transcendentals=0
        ),
        name="partial_product",
    )(jnp.reshape(t, (1,)), *feature_halves, grads)


def momentum_kernel(parts_ref, momentum_ref, moment_ref, nesterov_ref, grams_ref):
    grad = parts_ref[0].astype(jnp.float32)
    for part in range(1, parts_ref.shape[0]):
        grad = grad + parts_ref[part].astype(jnp.float32)
    new_moment = momentum_decay * momentum_ref[...] + grad
    moment_ref[...] = new_moment
    nesterov = grad + momentum_decay * new_moment
    nesterov_ref[...] = nesterov
    gram = lax.dot_general(
        nesterov, nesterov, (((1,), (1,)), ((), ())), precision=HIGHEST, preferred_element_type=jnp.float32
    )
    half = gram.shape[0] // 2
    packed = jnp.concatenate([gram[:half], gram[half:]], axis=1)
    for part in range(grams_ref.shape[0]):
        grams_ref[part] = packed


def momentum_step(parts, momentum):
    size, columns = momentum.shape
    vmem = pl.BlockSpec(memory_space=pltpu.VMEM)
    return pl.pallas_call(
        momentum_kernel,
        out_shape=(
            jax.ShapeDtypeStruct((size, columns), jnp.float32),
            jax.ShapeDtypeStruct((size, columns), jnp.float32),
            jax.ShapeDtypeStruct((NT, size // 2, 2 * size), jnp.float32),
        ),
        in_specs=[vmem, vmem],
        out_specs=(vmem, vmem, vmem),
        compiler_params=pltpu.CompilerParams(vmem_limit_bytes=16 * 1024 * 1024),
        cost_estimate=pl.CostEstimate(flops=60_000_000, bytes_accessed=1_700_000, transcendentals=0),
        name="momentum_step",
    )(parts, momentum)


def polar_kernel(grams_ref, block_ref, out_ref):
    mul = functools.partial(jnp.dot, precision=HIGHEST, preferred_element_type=jnp.float32)
    packed = grams_ref[0]
    for part in range(1, grams_ref.shape[0]):
        packed = packed + grams_ref[part]
    size = packed.shape[1] // 2
    total = jnp.concatenate([packed[:, :size], packed[:, size:]], axis=0)
    shape = (size, size)
    diagonal = lax.broadcasted_iota(jnp.int32, shape, 0) == lax.broadcasted_iota(jnp.int32, shape, 1)
    eye = jnp.where(diagonal, 1.0, 0.0).astype(jnp.float32)
    squares = jnp.sum(jnp.sum(total * eye, axis=1, keepdims=True), axis=0, keepdims=True)
    inverse = 1.0 / (jnp.sqrt(squares) + norm_epsilon)
    gram = total * inverse * inverse
    mapping = None
    for iteration in range(ITERS):
        square = mul(gram, gram)
        poly = linear_coeff * eye + cubic_coeff * gram + quintic_coeff * square
        if iteration < ITERS - 1:
            mapping = poly if iteration == 0 else mul(poly, mapping)
            gram = mul(mul(poly, gram), poly)
    scaled = mul(mapping * (inverse * (update_gain * math.sqrt(HID))), block_ref[...])
    units = out_ref.shape[2]
    rows = mul(poly, scaled).astype(out_ref.dtype)
    for part in range(out_ref.shape[0]):
        out_ref[part] = rows[:, part * units : (part + 1) * units]


def polar_update(grams, block):
    size, columns = block.shape
    vmem = pl.BlockSpec(memory_space=pltpu.VMEM)
    return pl.pallas_call(
        polar_kernel,
        out_shape=jax.ShapeDtypeStruct((NY, size, columns // NY), jnp.bfloat16),
        in_specs=[vmem, vmem],
        out_specs=vmem,
        compiler_params=pltpu.CompilerParams(vmem_limit_bytes=16 * 1024 * 1024),
        cost_estimate=pl.CostEstimate(flops=100_000_000, bytes_accessed=600_000, transcendentals=0),
        name="polar_update",
    )(grams, block)


def exchange_whole(pieces):
    return lax.all_to_all(pieces, "z", split_axis=0, concat_axis=0, tiled=True)


def exchange_halves(pieces):
    half = pieces.shape[1] // 2
    return jnp.concatenate([exchange_whole(pieces[:, :half]), exchange_whole(pieces[:, half:])], axis=1)


def per_device(features, gate_pre, up_pre, hidden_grad, lengths, momentum):
    y, z, t = (lax.axis_index(name) for name in AXES)
    swap = [(a * NT + b, b * NT + a) for a in range(NY) for b in range(NT)]
    swapped = lax.ppermute(features, ("y", "t"), swap)
    turned = turn(features)
    copies = gate_cotangent(y * NZ + z, lengths, gate_pre, up_pre, hidden_grad)

    by_blocks = lax.cond(
        z < 2 * NZ, exchange_whole, exchange_halves, turned.reshape(NZ, BLK, turned.shape[1])
    ).reshape(turned.shape)
    copies, swapped, by_blocks = lax.optimization_barrier((copies, swapped, by_blocks))
    grads = lax.all_to_all(
        copies, AXES, split_axis=0, concat_axis=0, axis_index_groups=line_groups("y"), tiled=True
    ).reshape(-1, copies.shape[2])
    by_tokens = turn(swapped)
    even = lax.rem(t, 2) == 0
    kept = jnp.where(even, by_tokens, by_blocks)
    given = jnp.where(even, by_blocks, by_tokens)
    orders, halves = ([0], [0]), None
    for masks in [m for m in ((1, 1), (2, 6), (6, 2)) if max(m) < NT]:
        arrived = lax.ppermute(given if halves is None else kept, AXES, tensor_pairs(masks))
        orders = tuple(order + [o ^ mask for o in order] for order, mask in zip(orders, masks))
        halves = (kept, arrived)
        kept = jnp.concatenate(halves, axis=0)

    partial_value = partial_product(t, orders, halves, grads)
    pieces = partial_value.reshape(NZ, BLK, partial_value.shape[1])
    received = lax.all_to_all(
        pieces, AXES, split_axis=0, concat_axis=0, axis_index_groups=line_groups("z"), tiled=True
    )
    new_moment, nesterov, grams = momentum_step(received, momentum)
    grams = lax.all_to_all(grams, "t", split_axis=0, concat_axis=0, tiled=True)
    by_y = polar_update(grams, nesterov)
    by_y = lax.all_to_all(by_y, "y", split_axis=0, concat_axis=0, tiled=True)
    unit_count = by_y.shape[2] // NZ
    by_z = by_y.reshape(NY, BLK, NZ, unit_count).transpose(2, 3, 0, 1)
    by_z = lax.all_to_all(by_z, "z", split_axis=0, concat_axis=0, tiled=True)
    result = by_z.transpose(1, 2, 0, 3).reshape(1, unit_count, NY * NZ * BLK)
    return result, new_moment


def solution(mesh):
    fine = Mesh(mesh.devices.reshape(NY, NZ, NT), AXES)
    split = P(("y", "z"), "t")
    return jax.shard_map(
        per_device,
        mesh=fine,
        in_specs=(split, split, split, split, P(), split),
        out_specs=(P("t", ("y", "z"), None), split),
        check_vma=False,
    )
```

```python
import functools
import math

import jax
import jax.numpy as jnp
from jax import lax
from jax.experimental import pallas as pl
from jax.experimental.pallas import tpu as pltpu
from jax.sharding import Mesh
from jax.sharding import PartitionSpec as P

HID = 7168
SEQ_LEN = 128
BLK = 64
ITERS = 5
NY = 8
NZ = 8
NT = 8

momentum_decay = 0.95
linear_coeff = 3.4445
cubic_coeff = -4.775
quintic_coeff = 2.0315
norm_epsilon = 1e-07
update_gain = 0.2

HIGHEST = lax.Precision.HIGHEST
AXES = ("y", "z", "t")


def gate_kernel(place_ref, lengths_ref, gate_in, up_in, cotangent_in, copies_ref, *scratch):
    buffers, arrived = scratch[:3], scratch[3]
    sources = (gate_in, up_in, cotangent_in)
    copies = [
        pltpu.make_async_copy(source, buffer, arrived.at[i])
        for i, (source, buffer) in enumerate(zip(sources, buffers))
    ]
    for copy in copies:
        copy.start()
    for copy in copies:
        copy.wait()
    gate_value, up_value, cotangent = (buffer[...].astype(jnp.float32) for buffer in buffers)
    sigmoid_gate = jax.nn.sigmoid(gate_value)
    gate_grad = cotangent * up_value * sigmoid_gate * (1.0 + gate_value * (1.0 - sigmoid_gate))
    position = lax.broadcasted_iota(jnp.int32, gate_value.shape, 0)
    trained = position < lengths_ref[place_ref[0]]
    gate_grad = jnp.where(trained, gate_grad, 0.0).astype(copies_ref.dtype)
    for part in range(copies_ref.shape[0]):
        copies_ref[part] = gate_grad


def gate_cotangent(place, lengths, gate_pre, up_pre, hidden_grad):
    tokens, columns = gate_pre.shape
    hbm = pl.BlockSpec(memory_space=pltpu.HBM)
    vmem = pl.BlockSpec(memory_space=pltpu.VMEM)
    smem = pl.BlockSpec(memory_space=pltpu.SMEM)
    arrays = (gate_pre, up_pre, hidden_grad)
    return pl.pallas_call(
        gate_kernel,
        out_shape=jax.ShapeDtypeStruct((NZ, tokens, columns), jnp.bfloat16),
        in_specs=[smem, smem] + [hbm] * 3,
        out_specs=vmem,
        scratch_shapes=[pltpu.VMEM(array.shape, array.dtype) for array in arrays]
        + [pltpu.SemaphoreType.DMA((3,))],
        compiler_params=pltpu.CompilerParams(vmem_limit_bytes=60 * 1024 * 1024),
        cost_estimate=pl.CostEstimate(
            flops=64 * tokens * columns, bytes_accessed=400 * tokens * columns, transcendentals=tokens * columns
        ),
        name="gate_cotangent",
    )(jnp.reshape(place, (1,)), lengths, *arrays)


def turn_kernel(value_ref, turned_ref):
    turned_ref[...] = value_ref[...].T


def turn(value):
    rows, columns = value.shape
    vmem = pl.BlockSpec(memory_space=pltpu.VMEM)
    return pl.pallas_call(
        turn_kernel,
        out_shape=jax.ShapeDtypeStruct((columns, rows), value.dtype),
        in_specs=[vmem],
        out_specs=vmem,
        compiler_params=pltpu.CompilerParams(vmem_limit_bytes=8 * 1024 * 1024),
        cost_estimate=pl.CostEstimate(flops=rows * columns, bytes_accessed=4 * rows * columns, transcendentals=0),
        name="turn",
    )(value)


def device_number(y, z, t):
    return (y * NZ + z) * NT + t


def line_groups(even_axis):
    groups = []
    for t in range(NT):
        along_y = (t % 2 == 0) == (even_axis == "y")
        for fixed in range(NZ if along_y else NY):
            line = [(i, fixed) if along_y else (fixed, i) for i in range(NY if along_y else NZ)]
            groups.append([device_number(y, z, t) for y, z in line])
    return groups


def tensor_pairs(masks):
    return [
        (device_number(y, z, t), device_number(y, z, t ^ masks[t % 2]))
        for y in range(NY)
        for z in range(NZ)
        for t in range(NT)
    ]


def partial_kernel(orders, t_ref, first_ref, second_ref, grads_ref, out_ref, features):
    rows = out_ref.shape[0]
    tokens = first_ref.shape[1]
    t = t_ref[0]
    blocks = [(ref, start) for ref in (first_ref, second_ref) for start in range(0, ref.shape[0], rows)]

    @pl.when(lax.rem(t, 2) == 0)
    def _():
        for offset, (ref, start) in zip(orders[0], blocks):
            group = lax.bitwise_xor(t, offset)
            features[:, pl.ds(pl.multiple_of(group * tokens, tokens), tokens)] = ref[start : start + rows, :]

    @pl.when(lax.rem(t, 2) == 1)
    def _():
        for offset, (ref, start) in zip(orders[1], blocks):
            block_rows = pl.ds(pl.multiple_of(lax.bitwise_xor(t, offset) * BLK, BLK), BLK)
            for z in range(NZ):
                features[block_rows, z * tokens : (z + 1) * tokens] = ref[
                    start + z * BLK : start + (z + 1) * BLK, :
                ]

    step = 128
    for start in range(0, rows, step):
        product = jnp.dot(
            features[start : start + step, :], grads_ref[...], preferred_element_type=jnp.float32
        )
        out_ref[start : start + step, :] = product.astype(out_ref.dtype)


def partial_product(t, orders, feature_halves, grads):
    tokens, columns = grads.shape
    rows = NZ * BLK
    vmem = pl.BlockSpec(memory_space=pltpu.VMEM)
    return pl.pallas_call(
        functools.partial(partial_kernel, orders),
        out_shape=jax.ShapeDtypeStruct((rows, columns), jnp.bfloat16),
        in_specs=[pl.BlockSpec(memory_space=pltpu.SMEM), vmem, vmem, vmem],
        out_specs=vmem,
        scratch_shapes=[pltpu.VMEM((rows, tokens), jnp.bfloat16)],
        compiler_params=pltpu.CompilerParams(vmem_limit_bytes=32 * 1024 * 1024),
        cost_estimate=pl.CostEstimate(
            flops=2 * tokens * rows * columns, bytes_accessed=6_000_000, transcendentals=0
        ),
        name="partial_product",
    )(jnp.reshape(t, (1,)), *feature_halves, grads)


def momentum_kernel(parts_ref, momentum_ref, moment_ref, nesterov_ref, grams_ref):
    grad = parts_ref[0].astype(jnp.float32)
    for part in range(1, parts_ref.shape[0]):
        grad = grad + parts_ref[part].astype(jnp.float32)
    new_moment = momentum_decay * momentum_ref[...] + grad
    moment_ref[...] = new_moment
    nesterov = grad + momentum_decay * new_moment
    nesterov_ref[...] = nesterov
    gram = lax.dot_general(
        nesterov, nesterov, (((1,), (1,)), ((), ())), precision=HIGHEST, preferred_element_type=jnp.float32
    )
    half = gram.shape[0] // 2
    packed = jnp.concatenate([gram[:half], gram[half:]], axis=1)
    for part in range(grams_ref.shape[0]):
        grams_ref[part] = packed


def momentum_step(parts, momentum):
    size, columns = momentum.shape
    vmem = pl.BlockSpec(memory_space=pltpu.VMEM)
    return pl.pallas_call(
        momentum_kernel,
        out_shape=(
            jax.ShapeDtypeStruct((size, columns), jnp.float32),
            jax.ShapeDtypeStruct((size, columns), jnp.float32),
            jax.ShapeDtypeStruct((NT, size // 2, 2 * size), jnp.float32),
        ),
        in_specs=[vmem, vmem],
        out_specs=(vmem, vmem, vmem),
        compiler_params=pltpu.CompilerParams(vmem_limit_bytes=16 * 1024 * 1024),
        cost_estimate=pl.CostEstimate(flops=60_000_000, bytes_accessed=1_700_000, transcendentals=0),
        name="momentum_step",
    )(parts, momentum)


def polar_kernel(grams_ref, block_ref, out_ref):
    mul = functools.partial(jnp.dot, precision=HIGHEST, preferred_element_type=jnp.float32)
    packed = grams_ref[0]
    for part in range(1, grams_ref.shape[0]):
        packed = packed + grams_ref[part]
    size = packed.shape[1] // 2
    total = jnp.concatenate([packed[:, :size], packed[:, size:]], axis=0)
    shape = (size, size)
    diagonal = lax.broadcasted_iota(jnp.int32, shape, 0) == lax.broadcasted_iota(jnp.int32, shape, 1)
    eye = jnp.where(diagonal, 1.0, 0.0).astype(jnp.float32)
    squares = jnp.sum(jnp.sum(total * eye, axis=1, keepdims=True), axis=0, keepdims=True)
    inverse = 1.0 / (jnp.sqrt(squares) + norm_epsilon)
    gram = total * inverse * inverse
    mapping = None
    for iteration in range(ITERS):
        square = mul(gram, gram)
        poly = linear_coeff * eye + cubic_coeff * gram + quintic_coeff * square
        if iteration < ITERS - 1:
            mapping = poly if iteration == 0 else mul(poly, mapping)
            gram = mul(mul(poly, gram), poly)
    scaled = mul(mapping * (inverse * (update_gain * math.sqrt(HID))), block_ref[...])
    units = out_ref.shape[2]
    rows = mul(poly, scaled).astype(out_ref.dtype)
    for part in range(out_ref.shape[0]):
        out_ref[part] = rows[:, part * units : (part + 1) * units]


def polar_update(grams, block):
    size, columns = block.shape
    vmem = pl.BlockSpec(memory_space=pltpu.VMEM)
    return pl.pallas_call(
        polar_kernel,
        out_shape=jax.ShapeDtypeStruct((NY, size, columns // NY), jnp.bfloat16),
        in_specs=[vmem, vmem],
        out_specs=vmem,
        compiler_params=pltpu.CompilerParams(vmem_limit_bytes=16 * 1024 * 1024),
        cost_estimate=pl.CostEstimate(flops=100_000_000, bytes_accessed=600_000, transcendentals=0),
        name="polar_update",
    )(grams, block)


def exchange_whole(pieces):
    return lax.all_to_all(pieces, "z", split_axis=0, concat_axis=0, tiled=True)


def exchange_halves(pieces):
    half = pieces.shape[1] // 2
    return jnp.concatenate([exchange_whole(pieces[:, :half]), exchange_whole(pieces[:, half:])], axis=1)


def per_device(features, gate_pre, up_pre, hidden_grad, lengths, momentum):
    y, z, t = (lax.axis_index(name) for name in AXES)
    swap = [(a * NT + b, b * NT + a) for a in range(NY) for b in range(NT)]
    swapped = lax.ppermute(features, ("y", "t"), swap)
    copies = gate_cotangent(y * NZ + z, lengths, gate_pre, up_pre, hidden_grad)
    turned, copies = lax.optimization_barrier((turn(features), copies))

    by_blocks = lax.cond(
        z < 2 * NZ, exchange_whole, exchange_halves, turned.reshape(NZ, BLK, turned.shape[1])
    ).reshape(turned.shape)
    copies, swapped, by_blocks = lax.optimization_barrier((copies, swapped, by_blocks))
    grads = lax.all_to_all(
        copies, AXES, split_axis=0, concat_axis=0, axis_index_groups=line_groups("y"), tiled=True
    ).reshape(-1, copies.shape[2])
    by_tokens = turn(swapped)
    even = lax.rem(t, 2) == 0
    kept = jnp.where(even, by_tokens, by_blocks)
    given = jnp.where(even, by_blocks, by_tokens)
    orders, halves = ([0], [0]), None
    for masks in [m for m in ((1, 1), (2, 6), (6, 2)) if max(m) < NT]:
        arrived = lax.ppermute(given if halves is None else kept, AXES, tensor_pairs(masks))
        orders = tuple(order + [o ^ mask for o in order] for order, mask in zip(orders, masks))
        halves = (kept, arrived)
        kept = jnp.concatenate(halves, axis=0)

    partial_value = partial_product(t, orders, halves, grads)
    pieces = partial_value.reshape(NZ, BLK, partial_value.shape[1])
    received = lax.all_to_all(
        pieces, AXES, split_axis=0, concat_axis=0, axis_index_groups=line_groups("z"), tiled=True
    )
    new_moment, nesterov, grams = momentum_step(received, momentum)
    grams = lax.all_to_all(grams, "t", split_axis=0, concat_axis=0, tiled=True)
    by_y = polar_update(grams, nesterov)
    by_y = lax.all_to_all(by_y, "y", split_axis=0, concat_axis=0, tiled=True)
    unit_count = by_y.shape[2] // NZ
    by_z = by_y.reshape(NY, BLK, NZ, unit_count).transpose(2, 3, 0, 1)
    by_z = lax.all_to_all(by_z, "z", split_axis=0, concat_axis=0, tiled=True)
    result = by_z.transpose(1, 2, 0, 3).reshape(1, unit_count, NY * NZ * BLK)
    return result, new_moment


def solution(mesh):
    fine = Mesh(mesh.devices.reshape(NY, NZ, NT), AXES)
    split = P(("y", "z"), "t")
    return jax.shard_map(
        per_device,
        mesh=fine,
        in_specs=(split, split, split, split, P(), split),
        out_specs=(P("t", ("y", "z"), None), split),
        check_vma=False,
    )
```

```python
import functools
import math

import jax
import jax.numpy as jnp
from jax import lax
from jax.experimental import pallas as pl
from jax.experimental.pallas import tpu as pltpu
from jax.sharding import Mesh
from jax.sharding import PartitionSpec as P

HID = 7168
SEQ_LEN = 128
BLK = 64
ITERS = 5
NY = 8
NZ = 8
NT = 8

momentum_decay = 0.95
linear_coeff = 3.4445
cubic_coeff = -4.775
quintic_coeff = 2.0315
norm_epsilon = 1e-07
update_gain = 0.2

HIGHEST = lax.Precision.HIGHEST
AXES = ("y", "z", "t")


def gate_kernel(place_ref, lengths_ref, gate_in, up_in, cotangent_in, copies_out, *scratch):
    buffers, result, arrived, written = scratch[:3], scratch[3], scratch[4], scratch[5]
    sources = (gate_in, up_in, cotangent_in)
    half = result.shape[0] // 2
    rows = [pl.ds(part * half, half) for part in range(2)]
    loads = [
        [
            pltpu.make_async_copy(source.at[rows[part]], buffer.at[rows[part]], arrived.at[part, i])
            for i, (source, buffer) in enumerate(zip(sources, buffers))
        ]
        for part in range(2)
    ]
    for load in loads[0] + loads[1]:
        load.start()
    limit = lengths_ref[place_ref[0]]
    stores = []
    for part in range(2):
        for load in loads[part]:
            load.wait()
        gate_value, up_value, cotangent = (buffer[rows[part], :].astype(jnp.float32) for buffer in buffers)
        sigmoid_gate = jax.nn.sigmoid(gate_value)
        gate_grad = cotangent * up_value * sigmoid_gate * (1.0 + gate_value * (1.0 - sigmoid_gate))
        position = lax.broadcasted_iota(jnp.int32, gate_value.shape, 0) + part * half
        result[rows[part], :] = jnp.where(position < limit, gate_grad, 0.0).astype(result.dtype)
        for peer in range(copies_out.shape[0]):
            store = pltpu.make_async_copy(
                result.at[rows[part]], copies_out.at[peer, rows[part]], written.at[part, peer]
            )
            store.start()
            stores.append(store)
    for store in stores:
        store.wait()


def gate_cotangent(place, lengths, gate_pre, up_pre, hidden_grad):
    tokens, columns = gate_pre.shape
    hbm = pl.BlockSpec(memory_space=pltpu.HBM)
    smem = pl.BlockSpec(memory_space=pltpu.SMEM)
    arrays = (gate_pre, up_pre, hidden_grad)
    return pl.pallas_call(
        gate_kernel,
        out_shape=jax.ShapeDtypeStruct((NZ, tokens, columns), jnp.bfloat16),
        in_specs=[smem, smem] + [hbm] * 3,
        out_specs=hbm,
        scratch_shapes=[pltpu.VMEM(array.shape, array.dtype) for array in arrays]
        + [
            pltpu.VMEM((tokens, columns), jnp.bfloat16),
            pltpu.SemaphoreType.DMA((2, 3)),
            pltpu.SemaphoreType.DMA((2, NZ)),
        ],
        compiler_params=pltpu.CompilerParams(vmem_limit_bytes=60 * 1024 * 1024),
        cost_estimate=pl.CostEstimate(
            flops=64 * tokens * columns, bytes_accessed=400 * tokens * columns, transcendentals=tokens * columns
        ),
        name="gate_cotangent",
    )(jnp.reshape(place, (1,)), lengths, *arrays)


def turn_kernel(value_ref, turned_ref):
    turned_ref[...] = value_ref[...].T


def turn(value):
    rows, columns = value.shape
    vmem = pl.BlockSpec(memory_space=pltpu.VMEM)
    return pl.pallas_call(
        turn_kernel,
        out_shape=jax.ShapeDtypeStruct((columns, rows), value.dtype),
        in_specs=[vmem],
        out_specs=vmem,
        compiler_params=pltpu.CompilerParams(vmem_limit_bytes=8 * 1024 * 1024),
        cost_estimate=pl.CostEstimate(flops=rows * columns, bytes_accessed=4 * rows * columns, transcendentals=0),
        name="turn",
    )(value)


def device_number(y, z, t):
    return (y * NZ + z) * NT + t


def line_groups(even_axis):
    groups = []
    for t in range(NT):
        along_y = (t % 2 == 0) == (even_axis == "y")
        for fixed in range(NZ if along_y else NY):
            line = [(i, fixed) if along_y else (fixed, i) for i in range(NY if along_y else NZ)]
            groups.append([device_number(y, z, t) for y, z in line])
    return groups


def tensor_pairs(masks):
    return [
        (device_number(y, z, t), device_number(y, z, t ^ masks[t % 2]))
        for y in range(NY)
        for z in range(NZ)
        for t in range(NT)
    ]


def partial_kernel(orders, t_ref, first_ref, second_ref, grads_ref, out_ref, features):
    rows = out_ref.shape[0]
    tokens = first_ref.shape[1]
    t = t_ref[0]
    blocks = [(ref, start) for ref in (first_ref, second_ref) for start in range(0, ref.shape[0], rows)]

    @pl.when(lax.rem(t, 2) == 0)
    def _():
        for offset, (ref, start) in zip(orders[0], blocks):
            group = lax.bitwise_xor(t, offset)
            features[:, pl.ds(pl.multiple_of(group * tokens, tokens), tokens)] = ref[start : start + rows, :]

    @pl.when(lax.rem(t, 2) == 1)
    def _():
        for offset, (ref, start) in zip(orders[1], blocks):
            block_rows = pl.ds(pl.multiple_of(lax.bitwise_xor(t, offset) * BLK, BLK), BLK)
            for z in range(NZ):
                features[block_rows, z * tokens : (z + 1) * tokens] = ref[
                    start + z * BLK : start + (z + 1) * BLK, :
                ]

    step = 128
    for start in range(0, rows, step):
        product = jnp.dot(
            features[start : start + step, :], grads_ref[...], preferred_element_type=jnp.float32
        )
        out_ref[start : start + step, :] = product.astype(out_ref.dtype)


def partial_product(t, orders, feature_halves, grads):
    tokens, columns = grads.shape
    rows = NZ * BLK
    vmem = pl.BlockSpec(memory_space=pltpu.VMEM)
    return pl.pallas_call(
        functools.partial(partial_kernel, orders),
        out_shape=jax.ShapeDtypeStruct((rows, columns), jnp.bfloat16),
        in_specs=[pl.BlockSpec(memory_space=pltpu.SMEM), vmem, vmem, vmem],
        out_specs=vmem,
        scratch_shapes=[pltpu.VMEM((rows, tokens), jnp.bfloat16)],
        compiler_params=pltpu.CompilerParams(vmem_limit_bytes=32 * 1024 * 1024),
        cost_estimate=pl.CostEstimate(
            flops=2 * tokens * rows * columns, bytes_accessed=6_000_000, transcendentals=0
        ),
        name="partial_product",
    )(jnp.reshape(t, (1,)), *feature_halves, grads)


def momentum_kernel(parts_ref, momentum_ref, moment_ref, nesterov_ref, grams_ref):
    grad = parts_ref[0].astype(jnp.float32)
    for part in range(1, parts_ref.shape[0]):
        grad = grad + parts_ref[part].astype(jnp.float32)
    new_moment = momentum_decay * momentum_ref[...] + grad
    moment_ref[...] = new_moment
    nesterov = grad + momentum_decay * new_moment
    nesterov_ref[...] = nesterov
    gram = lax.dot_general(
        nesterov, nesterov, (((1,), (1,)), ((), ())), precision=HIGHEST, preferred_element_type=jnp.float32
    )
    half = gram.shape[0] // 2
    packed = jnp.concatenate([gram[:half], gram[half:]], axis=1)
    for part in range(grams_ref.shape[0]):
        grams_ref[part] = packed


def momentum_step(parts, momentum):
    size, columns = momentum.shape
    vmem = pl.BlockSpec(memory_space=pltpu.VMEM)
    return pl.pallas_call(
        momentum_kernel,
        out_shape=(
            jax.ShapeDtypeStruct((size, columns), jnp.float32),
            jax.ShapeDtypeStruct((size, columns), jnp.float32),
            jax.ShapeDtypeStruct((NT, size // 2, 2 * size), jnp.float32),
        ),
        in_specs=[vmem, vmem],
        out_specs=(vmem, vmem, vmem),
        compiler_params=pltpu.CompilerParams(vmem_limit_bytes=16 * 1024 * 1024),
        cost_estimate=pl.CostEstimate(flops=60_000_000, bytes_accessed=1_700_000, transcendentals=0),
        name="momentum_step",
    )(parts, momentum)


def polar_kernel(grams_ref, block_ref, out_ref):
    mul = functools.partial(jnp.dot, precision=HIGHEST, preferred_element_type=jnp.float32)
    packed = grams_ref[0]
    for part in range(1, grams_ref.shape[0]):
        packed = packed + grams_ref[part]
    size = packed.shape[1] // 2
    total = jnp.concatenate([packed[:, :size], packed[:, size:]], axis=0)
    shape = (size, size)
    diagonal = lax.broadcasted_iota(jnp.int32, shape, 0) == lax.broadcasted_iota(jnp.int32, shape, 1)
    eye = jnp.where(diagonal, 1.0, 0.0).astype(jnp.float32)
    squares = jnp.sum(jnp.sum(total * eye, axis=1, keepdims=True), axis=0, keepdims=True)
    inverse = 1.0 / (jnp.sqrt(squares) + norm_epsilon)
    gram = total * inverse * inverse
    mapping = None
    for iteration in range(ITERS):
        square = mul(gram, gram)
        poly = linear_coeff * eye + cubic_coeff * gram + quintic_coeff * square
        if iteration < ITERS - 1:
            mapping = poly if iteration == 0 else mul(poly, mapping)
            gram = mul(mul(poly, gram), poly)
    scaled = mul(mapping * (inverse * (update_gain * math.sqrt(HID))), block_ref[...])
    units = out_ref.shape[2]
    rows = mul(poly, scaled).astype(out_ref.dtype)
    for part in range(out_ref.shape[0]):
        out_ref[part] = rows[:, part * units : (part + 1) * units]


def polar_update(grams, block):
    size, columns = block.shape
    vmem = pl.BlockSpec(memory_space=pltpu.VMEM)
    return pl.pallas_call(
        polar_kernel,
        out_shape=jax.ShapeDtypeStruct((NY, size, columns // NY), jnp.bfloat16),
        in_specs=[vmem, vmem],
        out_specs=vmem,
        compiler_params=pltpu.CompilerParams(vmem_limit_bytes=16 * 1024 * 1024),
        cost_estimate=pl.CostEstimate(flops=100_000_000, bytes_accessed=600_000, transcendentals=0),
        name="polar_update",
    )(grams, block)


def exchange_whole(pieces):
    return lax.all_to_all(pieces, "z", split_axis=0, concat_axis=0, tiled=True)


def exchange_halves(pieces):
    half = pieces.shape[1] // 2
    return jnp.concatenate([exchange_whole(pieces[:, :half]), exchange_whole(pieces[:, half:])], axis=1)


def per_device(features, gate_pre, up_pre, hidden_grad, lengths, momentum):
    y, z, t = (lax.axis_index(name) for name in AXES)
    swap = [(a * NT + b, b * NT + a) for a in range(NY) for b in range(NT)]
    swapped = lax.ppermute(features, ("y", "t"), swap)
    turned = turn(features)
    copies = gate_cotangent(y * NZ + z, lengths, gate_pre, up_pre, hidden_grad)

    by_blocks = lax.cond(
        z < 2 * NZ, exchange_whole, exchange_halves, turned.reshape(NZ, BLK, turned.shape[1])
    ).reshape(turned.shape)
    copies, swapped, by_blocks = lax.optimization_barrier((copies, swapped, by_blocks))
    grads = lax.all_to_all(
        copies, AXES, split_axis=0, concat_axis=0, axis_index_groups=line_groups("y"), tiled=True
    ).reshape(-1, copies.shape[2])
    by_tokens = turn(swapped)
    even = lax.rem(t, 2) == 0
    kept = jnp.where(even, by_tokens, by_blocks)
    given = jnp.where(even, by_blocks, by_tokens)
    orders, halves = ([0], [0]), None
    for masks in [m for m in ((1, 1), (2, 6), (6, 2)) if max(m) < NT]:
        arrived = lax.ppermute(given if halves is None else kept, AXES, tensor_pairs(masks))
        orders = tuple(order + [o ^ mask for o in order] for order, mask in zip(orders, masks))
        halves = (kept, arrived)
        kept = jnp.concatenate(halves, axis=0)

    partial_value = partial_product(t, orders, halves, grads)
    pieces = partial_value.reshape(NZ, BLK, partial_value.shape[1])
    received = lax.all_to_all(
        pieces, AXES, split_axis=0, concat_axis=0, axis_index_groups=line_groups("z"), tiled=True
    )
    new_moment, nesterov, grams = momentum_step(received, momentum)
    grams = lax.all_to_all(grams, "t", split_axis=0, concat_axis=0, tiled=True)
    by_y = polar_update(grams, nesterov)
    by_y = lax.all_to_all(by_y, "y", split_axis=0, concat_axis=0, tiled=True)
    unit_count = by_y.shape[2] // NZ
    by_z = by_y.reshape(NY, BLK, NZ, unit_count).transpose(2, 3, 0, 1)
    by_z = lax.all_to_all(by_z, "z", split_axis=0, concat_axis=0, tiled=True)
    result = by_z.transpose(1, 2, 0, 3).reshape(1, unit_count, NY * NZ * BLK)
    return result, new_moment


def solution(mesh):
    fine = Mesh(mesh.devices.reshape(NY, NZ, NT), AXES)
    split = P(("y", "z"), "t")
    return jax.shard_map(
        per_device,
        mesh=fine,
        in_specs=(split, split, split, split, P(), split),
        out_specs=(P("t", ("y", "z"), None), split),
        check_vma=False,
    )
```
